32 devices in a mesh: dp: 8 (over z, y), head: 4 (over x, core).
Axes of the slice: x: 2, y: 2, z: 4, core: 2. Of those that a mesh axis runs over, the one named last changes fastest.
Arguments:
- tokens: bfloat16 [12288, 768], P('dp'), may hold values from -6 to 6
- teacher: bfloat16 [12288, 768], P('dp')
- segments: int32 [24, 512], P('dp'), may hold values from 0 to 3, never falling along the last dimension, each value on 1 to 256 neighbouring positions
- present: int32 [24, 512], P('dp'), may hold values from 0 to 1, as said below
- query_weight: bfloat16 [768, 768], P(None, 'head'), may hold values from -0.3125 to 0.3125
- query_bias: bfloat16 [768], P('head'), may hold values from -3 to 3
- key_weight: bfloat16 [768, 768], P(None, 'head'), may hold values from -0.3125 to 0.3125
- value_weight: bfloat16 [768, 768], P(None, 'head'), may hold values from -0.21875 to 0.21875
- value_bias: bfloat16 [768], P('head'), may hold values from -3 to 3
- output_weight: bfloat16 [768, 768], P('head'), may hold values from -3 to 3
- output_bias: bfloat16 [768], replicated, may hold values from -2 to 2
- first_gain: bfloat16 [768], replicated, may hold values from 0.5 to 1.5
- first_shift: bfloat16 [768], replicated, may hold values from -2 to 2
- inner_weight: bfloat16 [768, 3072], P(None, 'head'), may hold values from -0.21875 to 0.21875
- inner_bias: bfloat16 [3072], P('head'), may hold values from -3 to 3
- outer_weight: bfloat16 [3072, 768], P('head'), may hold values from -0.4375 to 0.4375
- outer_bias: bfloat16 [768], replicated, may hold values from -2 to 2
- second_gain: bfloat16 [768], replicated, may hold values from 0.5 to 1.5
- second_shift: bfloat16 [768], replicated, may hold values from -2 to 2
- head_alpha: float32 [12], P('head'), may hold values from -1.5 to 1.5
- head_noise: float32 [12], P('head'), may hold values from -2 to 2
- unit_alpha: float32 [3072], P('head'), may hold values from -1.5 to 1.5
- unit_noise: float32 [3072], P('head'), may hold values from -2 to 2
- hidden_alpha: float32 [768], replicated, may hold values from -1.5 to 1.5
- hidden_noise: float32 [768], replicated, may hold values from -2 to 2
- head_keep: int32 [12], P('head'), may hold values 0 or 1
- unit_keep: int32 [3072], P('head'), may hold values 0 or 1
- hidden_keep: int32 [768], replicated, may hold values 0 or 1
Outputs:
- student: bfloat16 [12288, 768], P('dp')
- pruned: bfloat16 [12288, 768], P('dp')
- tokens_grad: bfloat16 [12288, 768], P('dp')
- query_weight_grad: float32 [768, 768], P(None, 'head')
- query_bias_grad: float32 [768], P('head')
- key_weight_grad: float32 [768, 768], P(None, 'head')
- value_weight_grad: float32 [768, 768], P(None, 'head')
- value_bias_grad: float32 [768], P('head')
- output_weight_grad: float32 [768, 768], P('head')
- output_bias_grad: float32 [768], replicated
- first_gain_grad: float32 [768], replicated
- first_shift_grad: float32 [768], replicated
- inner_weight_grad: float32 [768, 3072], P(None, 'head')
- inner_bias_grad: float32 [3072], P('head')
- outer_weight_grad: float32 [3072, 768], P('head')
- outer_bias_grad: float32 [768], replicated
- second_gain_grad: float32 [768], replicated
- second_shift_grad: float32 [768], replicated
- head_alpha_grad: float32 [12], P('head')
- unit_alpha_grad: float32 [3072], P('head')
- hidden_alpha_grad: float32 [768], replicated
- mean_error: float32 [], replicated
- pruned_error: float32 [], replicated
The draws below stay inside these ranges and needn't reach their ends.
Inputs may be any that keep to these rules, and one draw needn't show every extreme that they name: `segments`: within each row of 512 positions the segment numbers never fall; equal numbers in a row mark one document. `present`: in each block of 512 positions the real tokens come first, at least 128 of them, and at least one padding position follows.
All inputs are finite; a program needn't handle non-finite values. No bound on the sum of `head_keep` or of `unit_keep` on one device may be relied on, other than what follows from the above.
Results may differ from the reference program's by a relative error of at most 0.022.
Values may be sent and summed in bfloat16 or wider, within the bound.
No kernel may reach another device: no remote copies, remote signals or barrier semaphores. Data moves between devices by JAX's collectives and lax.ppermute only.
A program may use at most 192 MiB of HBM per device.

```python
import math
import jax
import jax.numpy as jnp
import numpy as np
from jax import lax

D = 768
H = 12
HD = 64
FF = 3072
BLOCK = 512
BLK_DEV = 3
TOK_DEV = 1536
BLOCKS = 24
TOKENS = 12288
N_DP = 8
N_HEAD = 4


def draw_teacher(key, part):
    key = jax.random.fold_in(key, 5)
    place = lax.broadcasted_iota(jnp.int32, (TOKENS, 1), 0).astype(jnp.float32) / TOKENS
    base = jnp.clip(jax.random.normal(key, (TOKENS, D), jnp.float32), -4.0, 4.0)
    scale = 0.25 * jnp.exp(place * 3.178054)
    return (base * scale).astype(jnp.bfloat16)


def draw_present(key, part):
    key = jax.random.fold_in(key, 11)
    fill = jax.random.randint(key, (BLOCKS, 1), BLOCK // 4, BLOCK)
    position = lax.broadcasted_iota(jnp.int32, (BLOCKS, BLOCK), 1)
    return (position < fill).astype(jnp.int32)


def place_ends(drawn, stream_key, least, high):
    longest = drawn.shape.index(max(drawn.shape))
    spots = []
    for shift in (0, 1):
        where = [jax.random.randint(jax.random.fold_in(stream_key, axis), (), 0, length) for axis, length in enumerate(drawn.shape)]
        where[longest] = (where[longest] + shift) % drawn.shape[longest]
        spots.append(tuple(where))
    return drawn.at[spots[0]].set(least).at[spots[1]].set(high)


def levels(key, extent, cuts, smallest, high):
    loudness = 1.0
    for axis_at, shards_of in cuts:
        heights = jax.random.uniform(jax.random.fold_in(jax.random.fold_in(key, 6), axis_at), (shards_of,), jnp.float32, smallest / len(cuts), high / len(cuts))
        loudness = loudness * jnp.repeat(jnp.exp(heights), extent[axis_at] // shards_of).reshape((-1,) + (1,) * (len(extent) - 1 - axis_at))
    return loudness


def split_up(amount, total, limit, skew):
    portions = [(1 << 20) // math.isqrt(standing ** skew) + 1 for standing in range(2, amount + 1)]
    spare, holding = total - limit - (amount - 1), [1] * (amount - 1)
    while spare > 0:
        candidates = [i for i in range(amount - 1) if holding[i] < limit]
        mass, budget = sum([portions[i] for i in candidates]), spare
        for i in candidates:
            extra = min(limit - holding[i], max(1, budget * portions[i] // mass), spare)
            holding[i] = holding[i] + extra
            spare = spare - extra
    return np.array([limit] + holding)


def ragged(own_key, number_of, total, reach, lean):
    if number_of == 2:
        one = jax.random.randint(own_key, (), max(1, total - reach), min(reach, total - 1) + 1)
        return jnp.stack([one, total - one])
    sizes = jnp.asarray(split_up(number_of, total, reach, lean), jnp.int32)
    couples = (number_of - 1) // 2
    giver, taker = sizes[1:1 + 2 * couples:2], sizes[2:2 + 2 * couples:2]
    slack = jnp.minimum(giver - 1, reach - taker)
    shifted = jax.random.randint(jax.random.fold_in(own_key, 1), (couples,), 0, 1 << 20) % (slack + 1)
    sizes = sizes.at[1:1 + 2 * couples:2].set(giver - shifted).at[2:2 + 2 * couples:2].set(taker + shifted)
    return sizes[jax.random.permutation(jax.random.fold_in(own_key, 2), number_of)]


def normal_values(key, dims, spread, most, cuts=(), held_as=jnp.bfloat16):
    entries = spread * jax.random.normal(key, dims, jnp.float32)
    if cuts:
        entries = entries * levels(key, dims, cuts, -0.22, 0.18)
    return jnp.clip(entries, -most, most).astype(held_as)


def setup_inputs(seed: int = 0) -> dict:
    key_list = jax.random.split(jax.random.key(seed), 29)
    return {
        "tokens": normal_values(key_list[0], (TOKENS, D), 1.0, 6.0, ((0, 8),)),
        "teacher": draw_teacher(jax.random.fold_in(key_list[28], 71), 0),
        "segments": jax.vmap(lambda own: jnp.searchsorted(jnp.cumsum(ragged(own, 4, BLOCK, BLOCK // 2, 1)), jnp.arange(BLOCK), side="right"))(jax.random.split(key_list[2], BLOCKS)).reshape((BLOCKS, BLOCK)).astype(jnp.int32),
        "present": draw_present(jax.random.fold_in(key_list[28], 71), 0),
        "query_weight": normal_values(key_list[4], (D, H * HD), (D // 2) ** -0.5, 0.3125, ((1, 4),)),
        "query_bias": normal_values(key_list[5], (H * HD,), 0.5, 3.0, ((0, 4),)),
        "key_weight": normal_values(key_list[6], (D, H * HD), (D // 2) ** -0.5, 0.3125, ((1, 4),)),
        "value_weight": normal_values(key_list[7], (D, H * HD), D ** -0.5, 0.21875, ((1, 4),)),
        "value_bias": normal_values(key_list[8], (H * HD,), 0.5, 3.0, ((0, 4),)),
        "output_weight": normal_values(key_list[9], (H * HD, D), (HD // 16) ** -0.5, 3.0, ((0, 4),)),
        "output_bias": normal_values(key_list[10], (D,), 0.3, 2.0),
        "first_gain": jnp.clip(1.0 + 0.1 * jax.random.normal(key_list[11], (D,), jnp.float32), 0.5, 1.5).astype(jnp.bfloat16),
        "first_shift": normal_values(key_list[12], (D,), 0.3, 2.0),
        "inner_weight": normal_values(key_list[13], (D, FF), D ** -0.5, 0.21875, ((1, 4),)),
        "inner_bias": normal_values(key_list[14], (FF,), 0.5, 3.0, ((0, 4),)),
        "outer_weight": normal_values(key_list[15], (FF, D), (FF // 16) ** -0.5, 0.4375, ((0, 4),)),
        "outer_bias": normal_values(key_list[16], (D,), 0.3, 2.0),
        "second_gain": jnp.clip(1.0 + 0.1 * jax.random.normal(key_list[17], (D,), jnp.float32), 0.5, 1.5).astype(jnp.bfloat16),
        "second_shift": normal_values(key_list[18], (D,), 0.3, 2.0),
        "head_alpha": jnp.clip(jax.random.uniform(key_list[19], (H,), jnp.float32, -1.5, 1.5) * levels(key_list[19], (H,), ((0, 4),), -0.4, 0.0), -1.5, 1.5),
        "head_noise": jnp.clip(jax.random.uniform(key_list[20], (H,), jnp.float32, -2.0, 2.0) * levels(key_list[20], (H,), ((0, 4),), -0.4, 0.0), -2.0, 2.0),
        "unit_alpha": jnp.clip(jax.random.uniform(key_list[21], (FF,), jnp.float32, -1.5, 1.5) * levels(key_list[21], (FF,), ((0, 4),), -0.4, 0.0), -1.5, 1.5),
        "unit_noise": jnp.clip(jax.random.uniform(key_list[22], (FF,), jnp.float32, -2.0, 2.0) * levels(key_list[22], (FF,), ((0, 4),), -0.4, 0.0), -2.0, 2.0),
        "hidden_alpha": jnp.clip(jax.random.uniform(key_list[23], (D,), jnp.float32, -1.5, 1.5), -1.5, 1.5),
        "hidden_noise": jnp.clip(jax.random.uniform(key_list[24], (D,), jnp.float32, -2.0, 2.0), -2.0, 2.0),
        "head_keep": place_ends((jax.random.randint(key_list[25], (H,), 0, 4) < 3).astype(jnp.int32), jax.random.fold_in(key_list[25], 1), 0, 1),
        "unit_keep": place_ends((jax.random.randint(key_list[26], (FF,), 0, 3) < 2).astype(jnp.int32), jax.random.fold_in(key_list[26], 1), 0, 1),
        "hidden_keep": place_ends((jax.random.randint(key_list[27], (D,), 0, 8) < 7).astype(jnp.int32), jax.random.fold_in(key_list[27], 1), 0, 1),
    }


HIGH = lax.Precision.HIGHEST
epsilon = 1e-05

@jax.custom_vjp
def low(v):
    return lax.optimization_barrier(v.astype(jnp.bfloat16)).astype(jnp.float32)

@jax.custom_vjp
def low_back(v):
    return v

def low_keep(v):
    return (low(v), None)

def low_pass(kept, grad):
    return (grad,)

def back_keep(v):
    return (v, None)

def back_low(kept, grad):
    return (low(grad),)
low.defvjp(low_keep, low_pass)
low_back.defvjp(back_keep, back_low)

def gate_value(alpha, noise):
    return jax.nn.sigmoid((alpha + noise) * 1.5)

def normalize(inputs, gain, shift):
    average = lax.optimization_barrier(jnp.mean(inputs, axis=-1, keepdims=True))
    centered = inputs - average
    variance = lax.optimization_barrier(jnp.mean(centered * centered, axis=-1, keepdims=True))
    return centered * lax.rsqrt(variance + epsilon) * gain + shift

def attend_block(pieces):
    queries, keys_in, values_in, seg_row, live_row = pieces
    length = seg_row.shape[0]
    scores = jnp.einsum('qhd,khd->hqk', queries, keys_in, precision=HIGH) * HD ** (-0.5)
    diagonal = lax.broadcasted_iota(jnp.int32, (length, length), 0) == lax.broadcasted_iota(jnp.int32, (length, length), 1)
    allowed = (seg_row[:, None] == seg_row[None, :]) & ((live_row[None, :] == 1) | diagonal)
    scores = low_back(jnp.where(allowed[None], scores, -1e+30))
    probs = low(jax.nn.softmax(scores, axis=-1))
    return jnp.einsum('hqk,khd->qhd', probs, values_in, precision=HIGH)

def grouped(acts, weight):
    row_count = acts.shape[0]
    partial_sums = jnp.einsum('tgc,gcd->gtd', acts.reshape(row_count, N_HEAD, -1), weight.reshape(N_HEAD, -1, weight.shape[1]), precision=HIGH)
    return lax.optimization_barrier(jnp.sum(low(partial_sums), axis=0))

def layer(weights, gates, inputs, seg_rows, live_rows):
    query_weight, query_bias, key_weight, value_weight, value_bias, output_weight, output_bias, first_gain, first_shift, inner_weight, inner_bias, outer_weight, outer_bias, second_gain, second_shift = weights
    head_gate, unit_gate, hidden_gate = gates
    row_count = inputs.shape[0]
    queries = low_back(low(jnp.dot(inputs, query_weight, precision=HIGH) + query_bias))
    keys_in = low_back(low(jnp.dot(inputs, key_weight, precision=HIGH)))
    values_in = low_back(low(jnp.dot(inputs, value_weight, precision=HIGH) + value_bias))
    split = (row_count // BLOCK, BLOCK, H, HD)
    context = lax.map(jax.checkpoint(attend_block), (queries.reshape(split), keys_in.reshape(split), values_in.reshape(split), seg_rows, live_rows))
    context = low_back(context.reshape(row_count, H, HD))
    gated = low(head_gate[:, None] * context).reshape(row_count, H * HD)
    attn = low_back(grouped(gated, output_weight)) + output_bias
    first = normalize(inputs + hidden_gate * attn, first_gain, first_shift)
    inner = low_back(jnp.dot(low_back(low(first)), inner_weight, precision=HIGH) + inner_bias)
    hidden = low(unit_gate * jax.nn.gelu(inner, approximate=False))
    ffn = low_back(grouped(hidden, outer_weight)) + outer_bias
    return normalize(first + hidden_gate * ffn, second_gain, second_shift)

def reference(tokens, teacher, segments, present, query_weight, query_bias, key_weight, value_weight, value_bias, output_weight, output_bias, first_gain, first_shift, inner_weight, inner_bias, outer_weight, outer_bias, second_gain, second_shift, head_alpha, head_noise, unit_alpha, unit_noise, hidden_alpha, hidden_noise, head_keep, unit_keep, hidden_keep):
    weights = tuple((item.astype(jnp.float32) for item in (query_weight, query_bias, key_weight, value_weight, value_bias, output_weight, output_bias, first_gain, first_shift, inner_weight, inner_bias, outer_weight, outer_bias, second_gain, second_shift)))
    alphas = tuple((item.astype(jnp.float32) for item in (head_alpha, unit_alpha, hidden_alpha)))
    noises = tuple((item.astype(jnp.float32) for item in (head_noise, unit_noise, hidden_noise)))
    keeps = tuple((item.astype(jnp.float32) for item in (head_keep, unit_keep, hidden_keep)))

    def relaxed(params, inputs, seg_rows, live_rows):
        weights_in, alphas_in = params
        gates = tuple((gate_value(alpha, noise) for alpha, noise in zip(alphas_in, noises)))
        return layer(weights_in, gates, inputs, seg_rows, live_rows)
    inputs_all = tokens.astype(jnp.float32).reshape(N_DP, TOK_DEV, D)
    targets_all = teacher.astype(jnp.float32).reshape(N_DP, TOK_DEV, D)
    segs_all = segments.reshape(N_DP, BLK_DEV, BLOCK)
    lives_all = present.reshape(N_DP, BLK_DEV, BLOCK)
    zeros = jax.tree.map(jnp.zeros_like, (weights, alphas))

    def step(carry, pieces):
        grads, soft_sum, hard_sum, live_sum = carry
        inputs, target, seg_rows, live_rows = pieces
        student_f, pull = jax.vjp(lambda params, values: relaxed(params, values, seg_rows, live_rows), (weights, alphas), inputs)
        mask = live_rows.reshape(-1, 1).astype(jnp.float32)
        error = (student_f - target) * mask
        grad_params, grad_inputs = pull(error)
        pruned_f = layer(weights, keeps, inputs, seg_rows, live_rows)
        hard_error = (pruned_f - target) * mask
        grads = jax.tree.map(jnp.add, grads, grad_params)
        carry = (grads, soft_sum + 0.5 * jnp.sum(error * error), hard_sum + 0.5 * jnp.sum(hard_error * hard_error), live_sum + jnp.sum(mask))
        return (carry, (student_f.astype(jnp.bfloat16), pruned_f.astype(jnp.bfloat16), grad_inputs.astype(jnp.bfloat16)))
    start = (zeros, jnp.zeros((), jnp.float32), jnp.zeros((), jnp.float32), jnp.zeros((), jnp.float32))
    (grads, soft_sum, hard_sum, live_sum), (student, pruned, grad_inputs) = lax.scan(step, start, (inputs_all, targets_all, segs_all, lives_all))
    live_count = jnp.maximum(live_sum, 1.0)
    weight_grads, alpha_grads = grads
    g_qw, g_qb, g_kw, g_vw, g_vb, g_ow, g_ob, g_fg, g_fs, g_iw, g_ib, g_uw, g_ub, g_sg, g_ss = weight_grads
    g_ha, g_ua, g_da = alpha_grads
    return (student.reshape(TOKENS, D), pruned.reshape(TOKENS, D), grad_inputs.reshape(TOKENS, D), g_qw, g_qb, g_kw, g_vw, g_vb, g_ow, g_ob, g_fg, g_fs, g_iw, g_ib, g_uw, g_ub, g_sg, g_ss, g_ha, g_ua, g_da, soft_sum / live_count, hard_sum / live_count)
```

```python
from functools import partial

import jax
import jax.numpy as jnp
from jax import lax
from jax.experimental import pallas as pl
from jax.experimental.pallas import tpu as pltpu
from jax.sharding import PartitionSpec as P

F32 = jnp.float32
BF = jnp.bfloat16
HD = 64
EPS = 1e-05
VEC = 32
CH = 32
MB = 1024 * 1024

HGATE, HKEEP, OUTB, FG, FS, OUTERB, SG, SS, UGATE, INB, HEADG, QB, VB = range(13)


def dot(a, b):
    return jnp.dot(a, b, preferred_element_type=F32)


def dot_nt(a, b):
    return lax.dot_general(a, b, (((1,), (1,)), ((), ())), preferred_element_type=F32)


def dot_tn(a, b):
    return lax.dot_general(a, b, (((0,), (0,)), ((), ())), preferred_element_type=F32)


def gelu_parts(v):
    z = jnp.abs(v) * 0.7071067811865476
    e = jnp.exp(-(z * z))
    t = 1.0 / (1.0 + 0.3275911 * z)
    p = 0.5 * 1.061405429
    p = p * t - 0.5 * 1.453152027
    p = p * t + 0.5 * 1.421413741
    p = p * t - 0.5 * 0.284496736
    p = p * t + 0.5 * 0.254829592
    q = p * t * e
    return jnp.where(v >= 0.0, 1.0 - q, q), e


def fold(x):
    return jnp.sum(x.reshape(x.shape[0] // 8, 8, x.shape[1]), axis=0)


def mean(x):
    return jnp.mean(x, axis=1, keepdims=True)


def call(kernel, outs, args, specs=None, scratch=(), grid=(), prefetch=0, out_specs=None, flops=0, nbytes=0, limit=40, name=None):
    vmem = pl.BlockSpec(memory_space=pltpu.VMEM)
    specs = specs or [vmem] * (len(args) - prefetch)
    out_specs = out_specs or [vmem] * len(outs)
    return pl.pallas_call(
        kernel,
        out_shape=[jax.ShapeDtypeStruct(s, d) for s, d in outs],
        grid_spec=pltpu.PrefetchScalarGridSpec(
            num_scalar_prefetch=prefetch, grid=grid, in_specs=specs, out_specs=out_specs, scratch_shapes=list(scratch)
        ),
        compiler_params=pltpu.CompilerParams(vmem_limit_bytes=limit * MB),
        cost_estimate=pl.CostEstimate(flops=int(flops), bytes_accessed=int(nbytes), transcendentals=0),
        name=name,
    )(*args)


VM = pl.BlockSpec(memory_space=pltpu.VMEM)
SM = pl.BlockSpec(memory_space=pltpu.SMEM)
ANY = pl.BlockSpec(memory_space=pl.ANY)


def prep_kernel(ha, hn, hk, ua, un, uk, ib, da, dn, dk, ob, fg, fs, ub, sg, ss, qb, vb, win, wo, consts, pack):
    d = win.shape[0]
    w = win.shape[1]
    c = wo.shape[0]
    heads = ha.shape[0]

    def line(ref):
        return ref[...].astype(F32).reshape(1, ref.shape[0])

    def gate(a, n):
        return jax.nn.sigmoid((a + n) * 1.5)

    consts[...] = jnp.zeros_like(consts)
    consts[HGATE : HGATE + 1, :] = gate(line(da), line(dn))
    for row, ref in ((HKEEP, dk), (OUTB, ob), (FG, fg), (FS, fs), (OUTERB, ub), (SG, sg), (SS, ss), (INB, ib)):
        consts[row : row + 1, :] = line(ref)
    ugate = gate(line(ua), line(un))
    consts[UGATE : UGATE + 1, :] = ugate
    consts[QB : QB + 1, :c] = line(qb)
    consts[VB : VB + 1, :c] = line(vb)
    lane = lax.broadcasted_iota(jnp.int32, (1, w), 1)
    logit = jnp.zeros((1, w), F32)
    keep = jnp.zeros((1, w), F32)
    for i in range(heads):
        here = (lane >= i * HD) & (lane < (i + 1) * HD)
        logit = jnp.where(here, ha[i] + hn[i], logit)
        keep = jnp.where(here, hk[i].astype(F32), keep)
    hgate = jax.nn.sigmoid(logit * 1.5)
    consts[HEADG : HEADG + 1, :] = hgate

    def halves(x):
        high = x.astype(BF).astype(F32)
        return high, x - high

    uh, ul = halves(ugate)
    hh, hl = halves(hgate)
    pack[:d, :] = win[...]
    pack[d : d + c, :] = wo[...]
    rows = [uh, ul, line(uk), line(ib), hh, hl, keep] + [jnp.zeros((1, w), F32)] * (VEC - 7)
    pack[d + c :, :] = jnp.concatenate(rows, axis=0).astype(BF)


def attend_kernel(h_ref, tok, wq, wk, wv, consts, seg, live, c0, c1, cfar, e_ref, inv_ref, k_ref, v_ref, qst_ref, kt_ref, bias):
    c = wq.shape[0]
    length = tok.shape[0]
    quarter = length // 4
    x = tok[...]
    q = ((dot_nt(x, wq[...]) + consts[QB : QB + 1, :c]).astype(BF).astype(F32) * HD ** (-0.5)).astype(BF)
    k = dot_nt(x, wk[...]).astype(BF)
    v = (dot_nt(x, wv[...]) + consts[VB : VB + 1, :c]).astype(BF)
    k_ref[...] = k
    v_ref[...] = v
    qst = q.astype(F32).T.astype(BF)
    qst_ref[0] = qst
    kt_ref[0] = k.astype(F32).T.astype(BF)
    vt = v.astype(F32).T.astype(BF)
    seg_row = seg[0].astype(F32)
    code = jnp.where(live[0] == 1, seg_row, -1.0)
    code_col = jnp.broadcast_to(code, (128, length)).T[:, :1]
    row = lax.broadcasted_iota(jnp.int32, (length, length), 0)
    col = lax.broadcasted_iota(jnp.int32, (length, length), 1)
    bias[...] = jnp.where((code_col == seg_row) | (row == col), 0.0, -1e30)
    h = h_ref[0]
    inv_ref[...] = jnp.zeros_like(inv_ref)
    for i in range(c // HD):
        part = slice(i * HD, (i + 1) * HD)
        s = dot(k[:, part], qst[part, :]) + bias[...]
        top = jnp.max(s, axis=0, keepdims=True)
        e = jnp.exp(s - top)
        inv = 1.0 / jnp.sum(e, axis=0, keepdims=True)
        low = e.astype(BF)
        e_ref[0, i] = low
        inv_ref[0, i : i + 1, :] = inv
        ct = (dot(vt[part, :], low) * inv).astype(BF)
        bias_out = ((c0, 0), (c1, 1), (cfar, 2), (cfar, 3))
        for ref, r in bias_out:
            for j in range(4):

                @pl.when((h ^ r) == j)
                def _():
                    piece = ct[:, j * quarter : (j + 1) * quarter]
                    if r < 2:
                        ref[0, part, :] = piece
                    else:
                        ref[r - 2, 0, part, :] = piece


def load_rows(src, dst, h, sem, blocks, quarter):
    return [
        pltpu.make_async_copy(src.at[pl.ds(b * 4 * quarter + pl.multiple_of(h * quarter, quarter), quarter)], dst.at[pl.ds(b * quarter, quarter)], sem.at[b])
        for b in range(blocks)
    ]


def head_rows(vec, soft, c):
    if soft:
        return (vec[4:5, :] + vec[5:6, :])[:, :c]
    return vec[6:7, :][:, :c]


def project(pieces, wos, vecs, gated, attn, consts, soft):
    c = wos[0].shape[0]
    blocks, _, quarter = pieces[0].shape
    for r in range(4):
        g = head_rows(vecs[r][...].astype(F32), soft, c)
        for b in range(blocks):
            gated[r, b * quarter : (b + 1) * quarter, :] = (pieces[r][b].astype(F32).T * g).astype(BF)
    total = dot(gated[0], wos[0][...])
    for r in range(1, 4):
        total = total + dot(gated[r], wos[r][...])
    attn[...] = total + consts[OUTB : OUTB + 1, :]


def first_kernel(h_ref, c0, c1, xr, cr, a0, a1, a2, a3, tok_any, consts, first_low, normed, inv, attn, gated, wo, vec, tok, sem, tsem):
    blocks, c, quarter = c0.shape
    d = tok.shape[1]
    loads = load_rows(tok_any, tok, h_ref[0], tsem, blocks, quarter)
    for r, a in enumerate((a0, a1, a2, a3)):
        loads.append(pltpu.make_async_copy(a.at[pl.ds(d, c)], wo.at[r], sem.at[r]))
        loads.append(pltpu.make_async_copy(a.at[pl.ds(d + c, VEC)], vec.at[r], sem.at[4 + r]))
    for copy in loads:
        copy.start()
    for copy in loads:
        copy.wait()
    project([c0, c1, xr.at[0], cr.at[1]], [wo.at[r] for r in range(4)], [vec.at[r] for r in range(4)], gated, attn, consts, True)

    @pl.loop(0, tok.shape[0] // CH)
    def _(i):
        rows = pl.ds(pl.multiple_of(i * CH, CH), CH)
        x = tok[rows, :].astype(F32) + consts[HGATE : HGATE + 1, :] * attn[rows, :]
        x = x - mean(x)
        iv = lax.rsqrt(mean(x * x) + EPS)
        n = x * iv
        normed[rows, :] = n
        inv[rows, :] = jnp.broadcast_to(iv, (CH, 128))
        first_low[rows, :] = (n * consts[FG : FG + 1, :] + consts[FS : FS + 1, :]).astype(BF)


def ffn_forward(first, wins, outers, vecs, hidden, ffn, consts, soft, udact=None, waits=None):
    w = wins[0].shape[1]
    step = 256
    for r in range(4):
        if waits:
            for copy in waits[r]:
                copy.wait()
        vec = vecs[r][...].astype(F32)
        for s in range(0, w, step):
            at = slice(s, s + step)
            z = dot(first[...], wins[r][:, at]) + vec[3:4, at]
            phi, e = gelu_parts(z)
            if soft:
                g = vec[0:1, at] + vec[1:2, at]
                udact[r, :, at] = (g * (phi + z * e * 0.3989422804014327)).astype(BF)
            else:
                g = vec[2:3, at]
            hidden[r, :, at] = (g * (z * phi)).astype(BF)
    total = dot(hidden[0], outers[0][...])
    for r in range(1, 4):
        total = total + dot(hidden[r], outers[r][...])
    ffn[...] = total + consts[OUTERB : OUTERB + 1, :]


def row_mask(live, h, b, quarter, at):
    count = jnp.sum(live[b : b + 1, :].astype(F32))
    place = (h * quarter + at).astype(F32) + lax.broadcasted_iota(jnp.int32, (CH, 1), 0).astype(F32)
    return jnp.where(place < count, 1.0, 0.0)


def second_kernel(h_ref, first_low, normed, a0, a1, a2, a3, b0, b1, b2, b3, teach_any, live, consts, student, grad_two, gffn, udact, vecs_out, win, outer, vec, teach, hidden, ffn, acc, sem, tsem):
    blocks, length = live.shape
    quarter = length // 4
    d = normed.shape[1]
    c = a0.shape[0] - d - VEC
    h = h_ref[0]
    rowload = load_rows(teach_any, teach, h, tsem, blocks, quarter)
    waits = []
    for r, (a, b) in enumerate(zip((a0, a1, a2, a3), (b0, b1, b2, b3))):
        waits.append(
            [
                pltpu.make_async_copy(a.at[pl.ds(0, d)], win.at[r], sem.at[r]),
                pltpu.make_async_copy(a.at[pl.ds(d + c, VEC)], vec.at[r], sem.at[4 + r]),
                pltpu.make_async_copy(b, outer.at[r], sem.at[8 + r]),
            ]
        )
    for copies in waits:
        for copy in copies:
            copy.start()
    for copy in rowload:
        copy.start()
    wins = [win.at[r] for r in range(4)]
    ffn_forward(first_low, wins, [outer.at[r] for r in range(4)], [vec.at[r] for r in range(4)], hidden, ffn, consts, True, udact, waits)
    for copy in rowload:
        copy.wait()
    acc[...] = jnp.zeros_like(acc)
    for b in range(blocks):

        @pl.loop(0, quarter // CH)
        def _(i):
            rows = pl.ds(pl.multiple_of(b * quarter + i * CH, CH), CH)
            f = ffn[rows, :]
            hg = consts[HGATE : HGATE + 1, :]
            x = normed[rows, :] * consts[FG : FG + 1, :] + consts[FS : FS + 1, :] + hg * f
            x = x - mean(x)
            iv = lax.rsqrt(mean(x * x) + EPS)
            n = x * iv
            out = n * consts[SG : SG + 1, :] + consts[SS : SS + 1, :]
            student[rows, :] = out.astype(BF)
            err = (out - teach[rows, :].astype(F32)) * row_mask(live, h, b, quarter, i * CH)
            acc[0] += fold(err * n)
            acc[1] += fold(err)
            acc[4] += fold(err * err)
            e = err * consts[SG : SG + 1, :]
            g = iv * (e - mean(e) - n * mean(e * n))
            grad_two[rows, :] = g
            gf = hg * g
            acc[2] += fold(gf)
            acc[3] += fold(g * f)
            gffn[rows, :] = gf.astype(BF)

    vecs_out[...] = jnp.zeros_like(vecs_out)
    for j in range(5):
        vecs_out[j : j + 1, :] = jnp.sum(acc[j], axis=0, keepdims=True)


def hard_kernel(h_ref, c0, c1, xr, cr, a0, a1, a2, a3, b0, b1, b2, b3, tok_any, teach_any, live, consts, pruned, vecs_out, win, wo, outer, vec, tok, teach, gated, attn, first, low, hidden, acc, sem, tsem):
    blocks, length = live.shape
    quarter = length // 4
    d = tok.shape[1]
    c = a0.shape[0] - d - VEC
    h = h_ref[0]
    rowload = load_rows(tok_any, tok, h, tsem.at[0], blocks, quarter) + load_rows(teach_any, teach, h, tsem.at[1], blocks, quarter)
    early, late = [], []
    for r, (a, b) in enumerate(zip((a0, a1, a2, a3), (b0, b1, b2, b3))):
        early.append(pltpu.make_async_copy(a.at[pl.ds(d, c)], wo.at[r], sem.at[r]))
        early.append(pltpu.make_async_copy(a.at[pl.ds(d + c, VEC)], vec.at[r], sem.at[4 + r]))
        late.append([pltpu.make_async_copy(a.at[pl.ds(0, d)], win.at[r], sem.at[8 + r]), pltpu.make_async_copy(b, outer.at[r], sem.at[12 + r])])
    for copy in early + rowload:
        copy.start()
    for copies in late:
        for copy in copies:
            copy.start()
    for copy in early + rowload:
        copy.wait()
    vecs = [vec.at[r] for r in range(4)]
    project([c0, c1, xr.at[0], cr.at[1]], [wo.at[r] for r in range(4)], vecs, gated, attn, consts, False)

    @pl.loop(0, tok.shape[0] // CH)
    def _(i):
        rows = pl.ds(pl.multiple_of(i * CH, CH), CH)
        x = tok[rows, :].astype(F32) + consts[HKEEP : HKEEP + 1, :] * attn[rows, :]
        x = x - mean(x)
        n = x * lax.rsqrt(mean(x * x) + EPS)
        y = n * consts[FG : FG + 1, :] + consts[FS : FS + 1, :]
        first[rows, :] = y
        low[rows, :] = y.astype(BF)

    ffn_forward(low, [win.at[r] for r in range(4)], [outer.at[r] for r in range(4)], vecs, hidden, attn, consts, False, None, late)
    acc[...] = jnp.zeros_like(acc)
    for b in range(blocks):

        @pl.loop(0, quarter // CH)
        def _(i):
            rows = pl.ds(pl.multiple_of(b * quarter + i * CH, CH), CH)
            x = first[rows, :] + consts[HKEEP : HKEEP + 1, :] * attn[rows, :]
            x = x - mean(x)
            n = x * lax.rsqrt(mean(x * x) + EPS)
            out = n * consts[SG : SG + 1, :] + consts[SS : SS + 1, :]
            pruned[rows, :] = out.astype(BF)
            err = (out - teach[rows, :].astype(F32)) * row_mask(live, h, b, quarter, i * CH)
            acc[...] += fold(err * err)

    vecs_out[...] = jnp.broadcast_to(jnp.sum(acc[...], axis=0, keepdims=True), vecs_out.shape)


def back_kernel(gffn, udact, a0, a1, a2, a3, b0, b1, b2, b3, grad_two, normed, inv, attn, gated, consts, g0, g1, gfar, dout, grad_one, vecs_out, win, wo, outer, vec, gi, back, ga, acc, sem):
    d = normed.shape[1]
    c = a0.shape[0] - d - VEC
    w = win.shape[2]
    blocks, _, quarter = g0.shape
    late, waits = [], []
    for r, (a, b) in enumerate(zip((a0, a1, a2, a3), (b0, b1, b2, b3))):
        waits.append([pltpu.make_async_copy(b, outer.at[r], sem.at[r]), pltpu.make_async_copy(a.at[pl.ds(0, d)], win.at[r], sem.at[4 + r])])
        late.append(pltpu.make_async_copy(a.at[pl.ds(d, c)], wo.at[r], sem.at[8 + r]))
        late.append(pltpu.make_async_copy(a.at[pl.ds(d + c, VEC)], vec.at[r], sem.at[12 + r]))
    for copies in waits:
        for copy in copies:
            copy.start()
    for copy in late:
        copy.start()
    for r in range(4):
        for copy in waits[r]:
            copy.wait()
        for s in range(0, w, 256):
            at = slice(s, s + 256)
            gi[r, :, at] = (dot_nt(gffn[...], outer[r, at, :]) * udact[r, :, at].astype(F32)).astype(BF)
    total = dot_nt(gi[0], win[0])
    for r in range(1, 4):
        total = total + dot_nt(gi[r], win[r])
    back[...] = total
    acc[...] = jnp.zeros_like(acc)

    @pl.loop(0, back.shape[0] // CH)
    def _(i):
        rows = pl.ds(pl.multiple_of(i * CH, CH), CH)
        n = normed[rows, :]
        gf = grad_two[rows, :] + back[rows, :]
        acc[0] += fold(gf * n)
        acc[1] += fold(gf)
        e = gf * consts[FG : FG + 1, :]
        g = inv[rows, :1] * (e - mean(e) - n * mean(e * n))
        grad_one[rows, :] = g
        gat = consts[HGATE : HGATE + 1, :] * g
        acc[2] += fold(gat)
        acc[3] += fold(g * attn[rows, :])
        ga[rows, :] = gat.astype(BF)

    vecs_out[...] = jnp.zeros_like(vecs_out)
    for j in range(4):
        vecs_out[j : j + 1, :] = jnp.sum(acc[j], axis=0, keepdims=True)
    for copy in late:
        copy.wait()
    for r in range(4):
        gg = dot_nt(ga[...], wo[r]) * head_rows(vec[r].astype(F32), True, c)
        for b in range(blocks):
            piece = gg[b * quarter : (b + 1) * quarter, :].T.astype(BF)
            if r == 0:
                g0[b] = piece
            elif r == 1:
                g1[b] = piece
            else:
                gfar[r - 2, b] = piece
        dout[r] = dot_tn(gated[r], ga[...]).astype(BF)


def units_kernel(f0, f1, fx, fd, consts, win, hidden, udact):
    for r, f in enumerate((f0, f1, fx, fd)):
        rows = slice(r * f0.shape[0], (r + 1) * f0.shape[0])
        for s in range(0, win.shape[1], 256):
            at = slice(s, s + 256)
            z = dot(f[...], win[:, at]) + consts[INB : INB + 1, at]
            phi, e = gelu_parts(z)
            g = consts[UGATE : UGATE + 1, at]
            udact[rows, at] = (g * (phi + z * e * 0.3989422804014327)).astype(BF)
            hidden[rows, at] = (g * (z * phi)).astype(BF)


def slots(src, keep, send, first_bit, second_bit):
    n = keep.shape[1]
    for a in range(2):
        for b in range(2):
            j = (first_bit ^ a) * 2 + (second_bit ^ b)
            rows = src[pl.ds(pl.multiple_of(j * n, 16), n), :].astype(BF)
            if a == 0:
                keep[b] = rows
            else:
                send[b] = rows


def grads_kernel(bits, f0, f1, fx, fd, g0, g1, gx, gd, outer, consts, hidden, udact, akeep, asend, bkeep, bsend, vecs_out, first, gffn, gi, big, acc, sem):
    n = f0.shape[0]
    loads = []
    for r, (f, g) in enumerate(zip((f0, f1, fx, fd), (g0, g1, gx, gd))):
        loads.append(pltpu.make_async_copy(g, gffn.at[pl.ds(r * n, n)], sem.at[r]))
        loads.append(pltpu.make_async_copy(f, first.at[pl.ds(r * n, n)], sem.at[4 + r]))
    for copy in loads:
        copy.start()
    for copy in loads:
        copy.wait()
    big[...] = dot_tn(hidden[...], gffn[...])
    slots(big, akeep, asend, bits[0], bits[1])
    acc[...] = jnp.zeros_like(acc)
    for r in range(4):
        rows = slice(r * n, (r + 1) * n)
        for s in range(0, outer.shape[0], 256):
            at = slice(s, s + 256)
            gh = dot_nt(gffn[rows, :], outer[at, :])
            g = (gh * udact[rows, at].astype(F32)).astype(BF)
            gi[rows, at] = g
            acc[0, :, at] += fold(gh * hidden[rows, at].astype(F32))
            acc[1, :, at] += fold(g.astype(F32))
    big[...] = dot_tn(first[...], gi[...])
    slots(big, bkeep, bsend, bits[1], bits[0])
    vecs_out[...] = jnp.zeros_like(vecs_out)
    for j in range(2):
        vecs_out[j : j + 1, :] = jnp.sum(acc[j], axis=0, keepdims=True)


def attend_back_kernel(ids, g0, g1, gxr, gcr, e_ref, inv_ref, k_ref, v_ref, qst, kt, tok, wq, wk, wv, dout, v2, v3, vh, live, keep, send, dqkv, own, dct, dt, low, wacc, cacc):
    b = pl.program_id(0)
    h = ids[0]
    c, d = wq.shape
    length = tok.shape[0]
    quarter = length // 4
    blocks = live.shape[0]
    heads = c // HD

    @pl.when(b == 0)
    def _():
        wacc[...] = jnp.zeros_like(wacc)
        cacc[...] = jnp.zeros_like(cacc)

    for r, piece in enumerate((g0[0], g1[0], gxr[0, 0], gcr[1, 0])):
        dct[:, pl.ds(pl.multiple_of((h ^ r) * quarter, 128), quarter)] = piece
    for i in range(heads):
        part = slice(i * HD, (i + 1) * HD)
        inv = inv_ref[0, i : i + 1, :]
        dcp = (dct[part, :].astype(F32) * inv).astype(BF)
        dp = dot(v_ref[:, part], dcp)
        e = e_ref[0, i].astype(F32)
        w = e * dp
        delta = jnp.sum(w, axis=0, keepdims=True)
        ds = (w - e * (inv * delta)).astype(BF)
        dt[i * HD : (i + 1) * HD, :] = (dot(kt[0, part, :], ds) * HD ** (-0.5)).astype(BF)
        dt[c + i * HD : c + (i + 1) * HD, :] = dot_nt(qst[0, part, :], ds).astype(BF)
        dt[2 * c + i * HD : 2 * c + (i + 1) * HD, :] = dot_nt(dcp, e_ref[0, i]).astype(BF)
        cacc[8:9, i * 128 : (i + 1) * 128] += jnp.broadcast_to(jnp.sum(delta, axis=1, keepdims=True), (1, 128))
    wacc[...] += dot(dt[...], tok[...])
    nat = dt[...].astype(F32).T
    cacc[0:8, : 3 * c] += fold(nat)
    nat = nat.astype(BF)
    part = dot(nat[:, :c], wq[...]) + dot(nat[:, c : 2 * c], wk[...]) + dot(nat[:, 2 * c :], wv[...])
    low[...] = part.astype(BF)
    for r in range(4):
        rows = low[pl.ds(pl.multiple_of((h ^ r) * quarter, quarter), quarter), :]
        at = pl.ds(pl.multiple_of(b * quarter, quarter), quarter)
        if r % 2 == 0:
            keep[r // 2, at, :] = rows
        else:
            send[r // 2, at, :] = rows

    @pl.when(b == blocks - 1)
    def _():
        dqkv[...] = wacc[...].astype(BF)
        lane = lax.broadcasted_iota(jnp.int32, (1, d), 1)
        col = jnp.sum(cacc[0:8, :], axis=0, keepdims=True)
        line = jnp.where(lane < c, col[:, :d], 0.0)
        vals = col[:, 2 * c : 3 * c]
        own[...] = jnp.zeros_like(own)
        own[0:1, :] = line
        own[1:2, :c] = vals
        for i in range(heads):
            own[2:3, i * 128 : (i + 1) * 128] = cacc[8:9, i * 128 : (i + 1) * 128]
        n = ids[4]
        me = ids[3]
        soft = jnp.sum(v2[4:5, :])
        hard = jnp.sum(vh[0:1, :])
        count = jnp.zeros((), F32)
        for j in range(blocks):
            real = jnp.sum(live[j : j + 1, :].astype(F32))
            count += jnp.clip(real - (h * quarter).astype(F32), 0.0, float(quarter))
        marks = jnp.zeros((1, d), F32)
        for j, value in enumerate((soft, hard, count)):
            full = jnp.broadcast_to(value, (1, d))
            high = full.astype(BF).astype(F32)
            marks = jnp.where(lane == me + 2 * j * n, high, marks)
            marks = jnp.where(lane == me + (2 * j + 1) * n, full - high, marks)
        vec = jnp.concatenate(
            [v2[0:3, :], v3[0:3, :], v2[3:4, :] + v3[3:4, :], marks, jnp.zeros((8, d), F32)], axis=0
        ).astype(BF)
        at = blocks * quarter
        for r in range(4):
            ref = send if r % 2 else keep
            ref[r // 2, at : at + c, :] = dout[r]
            ref[r // 2, at + c : at + c + 16, :] = vec


def tail_kernel(bits, part, recv, grad_one, dqkv, own, vg, rows_out, ckeep, csend, big):
    t, d = grad_one.shape
    c = dqkv.shape[0] // 3
    both = part[...].astype(F32) + recv[...].astype(F32)
    rows_out[...] = (grad_one[...] + both[:t, :]).astype(BF)
    n = 3 * c
    big[...] = jnp.zeros_like(big)
    big[:n, :] = dqkv[...].astype(F32)
    big[n : n + c + 16, :] = both[t:, :]
    big[n + c + 16 : n + c + 24, :] = own[...]
    big[n + c + 24 : n + c + 32, :] = vg[...]
    slots(big, ckeep, csend, bits[0], bits[1])


def final_kernel(bits, n_dev, consts, ak, ao, aq, bk, bo, bq, ck, co, cq, uw, iw, qw, kw, vw, ow, qb, vb, ob, fg, fs, ib, ub, sg, ss, ha, ua, da, me, pe, big):
    d = consts.shape[1]
    c = qw.shape[0]

    def place(dst, refs, first_bit, second_bit):
        k, o, q = refs
        n = k.shape[0]
        for a in range(2):
            for b in range(2):
                j = (first_bit ^ a) * 2 + (second_bit ^ b)
                src = (k if b == 0 else o)[...] if a == 0 else q[b]
                dst[pl.ds(pl.multiple_of(j * n, 16), n), :] = src.astype(F32)

    place(uw, (ak, ao, aq), bits[0], bits[1])
    place(iw, (bk, bo, bq), bits[1], bits[0])
    place(big, (ck, co, cq), bits[0], bits[1])
    qw[...] = big[:c, :]
    kw[...] = big[c : 2 * c, :]
    vw[...] = big[2 * c : 3 * c, :]
    n = 3 * c
    ow[...] = big[n : n + c, :]
    n = n + c
    vec = big[n : n + 16, :]
    own = big[n + 16 : n + 32, :]
    for ref, row in ((sg, 0), (ss, 1), (ub, 2), (fg, 3), (fs, 4), (ob, 5)):
        ref[...] = vec[row : row + 1, :].reshape(d)
    hg = consts[HGATE : HGATE + 1, :]
    da[...] = (1.5 * vec[6:7, :] * hg * (1.0 - hg)).reshape(d)
    ug = consts[UGATE : UGATE + 1, :]
    ua[...] = (1.5 * own[8:9, :] * (1.0 - ug)).reshape(d)
    ib[...] = own[9:10, :].reshape(d)
    qb[...] = own[0:1, :c].reshape(c)
    vb[...] = own[1:2, :c].reshape(c)
    gate = consts[HEADG : HEADG + 1, :]
    for i in range(c // HD):
        g = gate[0, i * HD]
        ha[i] = 1.5 * own[2, i * 128] * (1.0 - g)
    lane = lax.broadcasted_iota(jnp.int32, (1, d), 1)
    nd = n_dev[0]
    marks = vec[7:8, :]

    def between(lo, hi):
        return jnp.sum(jnp.where((lane >= lo * nd) & (lane < hi * nd), marks, 0.0))

    live = jnp.maximum(between(4, 6), 1.0)
    me[0] = 0.5 * between(0, 2) / live
    pe[0] = 0.5 * between(2, 4) / live


def spread_kernel(h_ref, *refs):
    count = (len(refs) - 1) // 5
    sem = refs[-1]
    copies = []
    for a in range(count):
        out = refs[4 * count + a]
        for r in range(4):
            src = refs[4 * a + r]
            blocks = out.shape[0]
            quarter = out.shape[1] // 4
            for b in range(blocks):
                at = pl.ds(pl.multiple_of((h_ref[0] ^ r) * quarter, quarter), quarter)
                copies.append(pltpu.make_async_copy(src.at[pl.ds(b * quarter, quarter)], out.at[b, at], sem.at[len(copies)]))
    for copy in copies:
        copy.start()
    for copy in copies:
        copy.wait()


def shards(
    tokens, teacher, segments, present, query_weight, query_bias, key_weight, value_weight, value_bias, output_weight, output_bias,
    first_gain, first_shift, inner_weight, inner_bias, outer_weight, outer_bias, second_gain, second_shift, head_alpha, head_noise,
    unit_alpha, unit_noise, hidden_alpha, hidden_noise, head_keep, unit_keep, hidden_keep, n_dp,
):
    rows, d = tokens.shape
    blocks, length = segments.shape
    heads = head_alpha.shape[0]
    c = heads * HD
    w = unit_alpha.shape[0]
    quarter = length // 4
    t = blocks * quarter
    n_head = 4
    h = lax.axis_index("head").astype(jnp.int32)
    i_dp = lax.axis_index("dp").astype(jnp.int32)
    bit0, bit1 = i_dp & 1, (i_dp >> 1) & 1
    ids = jnp.stack([h, bit0, bit1, i_dp * n_head + h, jnp.int32(n_dp * n_head)])
    bits = ids[1:3]
    hs = ids[:1]

    def hop(x, mask, axis="head"):
        size = n_head if axis == "head" else n_dp
        return lax.ppermute(x, axis, [(i, i ^ mask) for i in range(size)])

    consts, pack = call(
        prep_kernel,
        [((16, d), F32), ((d + c + VEC, w), BF)],
        (head_alpha, head_noise, head_keep, unit_alpha, unit_noise, unit_keep, inner_bias, hidden_alpha, hidden_noise, hidden_keep, output_bias,
         first_gain, first_shift, outer_bias, second_gain, second_shift, query_bias, value_bias, inner_weight, output_weight),
        specs=[SM] * 3 + [VM] * 17, nbytes=4e6, name="prep",
    )

    a2 = hop(pack, 2)
    b2 = hop(outer_weight, 2)
    a1 = hop(pack, 1)
    b1 = hop(outer_weight, 1)
    a3 = hop(a2, 1)
    b3 = hop(b2, 1)
    packs = (pack, a1, a2, a3)
    outers = (outer_weight, b1, b2, b3)

    seg3 = segments.reshape(blocks, 1, length)
    live3 = present.reshape(blocks, 1, length)
    full = lambda *s: pl.BlockSpec(s, lambda b, *_: (0,) * len(s))
    c0, c1, cfar, e, inv_l, k, v, qst, kt = call(
        attend_kernel,
        [((blocks, c, quarter), BF), ((blocks, c, quarter), BF), ((2, blocks, c, quarter), BF), ((blocks, heads, length, length), BF),
         ((blocks, 8, length), F32), ((rows, c), BF), ((rows, c), BF), ((blocks, c, length), BF), ((blocks, c, length), BF)],
        (hs, tokens, query_weight.T, key_weight.T, value_weight.T, consts, seg3, live3),
        prefetch=1, grid=(blocks,),
        specs=[pl.BlockSpec((length, d), lambda b, *_: (b, 0)), full(c, d), full(c, d), full(c, d), full(16, d),
               pl.BlockSpec((1, 1, length), lambda b, *_: (b, 0, 0)), pl.BlockSpec((1, 1, length), lambda b, *_: (b, 0, 0))],
        out_specs=[pl.BlockSpec((1, c, quarter), lambda b, *_: (b, 0, 0)), pl.BlockSpec((1, c, quarter), lambda b, *_: (b, 0, 0)),
                   pl.BlockSpec((2, 1, c, quarter), lambda b, *_: (0, b, 0, 0)), pl.BlockSpec((1, heads, length, length), lambda b, *_: (b, 0, 0, 0)),
                   pl.BlockSpec((1, 8, length), lambda b, *_: (b, 0, 0)), pl.BlockSpec((length, c), lambda b, *_: (b, 0)),
                   pl.BlockSpec((length, c), lambda b, *_: (b, 0)), pl.BlockSpec((1, c, length), lambda b, *_: (b, 0, 0)),
                   pl.BlockSpec((1, c, length), lambda b, *_: (b, 0, 0))],
        scratch=[pltpu.VMEM((length, length), F32)],
        flops=8e9, nbytes=1e7, name="attend",
    )

    def exchange(near1, far):
        there = hop(far, 2)
        return hop(near1, 1), there, hop(there, 1)

    c1r, cxr, ccr = exchange(c1, cfar)

    first_low, normed, inv1, attn, gated = call(
        first_kernel,
        [((t, d), BF), ((t, d), F32), ((t, 128), F32), ((t, d), F32), ((4, t, c), BF)],
        (hs, c0, c1r, cxr, ccr, *packs, tokens, consts),
        prefetch=1, specs=[VM] * 4 + [ANY] * 5 + [VM],
        scratch=[pltpu.VMEM((4, c, w), BF), pltpu.VMEM((4, VEC, w), BF), pltpu.VMEM((t, d), BF), pltpu.SemaphoreType.DMA((8,)), pltpu.SemaphoreType.DMA((blocks,))],
        flops=2 * t * d * d, nbytes=8e6, name="first",
    )

    def gather(x):
        there = hop(x, 2)
        return x, hop(x, 1), there, hop(there, 1)

    firsts = gather(first_low)

    student_rows, grad_two, gffn, udact, v2 = call(
        second_kernel,
        [((t, d), BF), ((t, d), F32), ((t, d), BF), ((4, t, w), BF), ((8, d), F32)],
        (hs, first_low, normed, *packs, *outers, teacher, present, consts),
        prefetch=1, specs=[VM] * 2 + [ANY] * 9 + [VM] * 2,
        scratch=[pltpu.VMEM((4, d, w), BF), pltpu.VMEM((4, w, d), BF), pltpu.VMEM((4, VEC, w), BF), pltpu.VMEM((t, d), BF), pltpu.VMEM((4, t, w), BF),
                 pltpu.VMEM((t, d), F32), pltpu.VMEM((5, 8, d), F32), pltpu.SemaphoreType.DMA((12,)), pltpu.SemaphoreType.DMA((blocks,))],
        flops=16 * t * d * w, nbytes=2e7, name="second",
    )

    gffns = gather(gffn)

    g0, g1, gfar, dout, grad_one, v3 = call(
        back_kernel,
        [((blocks, c, quarter), BF), ((blocks, c, quarter), BF), ((2, blocks, c, quarter), BF), ((4, c, d), BF), ((t, d), F32), ((8, d), F32)],
        (gffn, udact, *packs, *outers, grad_two, normed, inv1, attn, gated, consts),
        specs=[VM] * 2 + [ANY] * 8 + [VM] * 6,
        scratch=[pltpu.VMEM((4, d, w), BF), pltpu.VMEM((4, c, w), BF), pltpu.VMEM((4, w, d), BF), pltpu.VMEM((4, VEC, w), BF), pltpu.VMEM((4, t, w), BF),
                 pltpu.VMEM((t, d), F32), pltpu.VMEM((t, d), BF), pltpu.VMEM((4, 8, d), F32), pltpu.SemaphoreType.DMA((16,))],
        flops=20 * t * d * w, nbytes=2e7, name="back",
    )

    g1r, gxr, gcr = exchange(g1, gfar)

    hidden_own, udact_own = call(
        units_kernel, [((rows, w), BF), ((rows, w), BF)], (*firsts, consts, inner_weight), flops=2 * rows * d * w * 2, nbytes=1e7, name="units"
    )

    pruned_rows, vh = call(
        hard_kernel,
        [((t, d), BF), ((8, d), F32)],
        (hs, c0, c1r, cxr, ccr, *packs, *outers, tokens, teacher, present, consts),
        prefetch=1, specs=[VM] * 4 + [ANY] * 10 + [VM] * 2,
        scratch=[pltpu.VMEM((4, d, w), BF), pltpu.VMEM((4, c, w), BF), pltpu.VMEM((4, w, d), BF), pltpu.VMEM((4, VEC, w), BF), pltpu.VMEM((t, d), BF),
                 pltpu.VMEM((t, d), BF), pltpu.VMEM((4, t, c), BF), pltpu.VMEM((t, d), F32), pltpu.VMEM((t, d), F32), pltpu.VMEM((t, d), BF),
                 pltpu.VMEM((4, t, w), BF), pltpu.VMEM((8, d), F32), pltpu.SemaphoreType.DMA((16,)), pltpu.SemaphoreType.DMA((2, blocks))],
        flops=20 * t * d * w, nbytes=2e7, name="hard",
    )

    akeep, asend, bkeep, bsend, vg = call(
        grads_kernel,
        [((2, w // 4, d), BF)] * 2 + [((2, d // 4, w), BF)] * 2 + [((8, w), F32)],
        (bits, *firsts, *gffns, outer_weight, consts, hidden_own, udact_own),
        prefetch=1, specs=[ANY] * 8 + [VM] * 4,
        scratch=[pltpu.VMEM((rows, d), BF), pltpu.VMEM((rows, d), BF), pltpu.VMEM((rows, w), BF), pltpu.VMEM((w, d), F32), pltpu.VMEM((2, 8, w), F32), pltpu.SemaphoreType.DMA((8,))],
        flops=6 * rows * d * w, nbytes=2e7, name="grads",
    )

    def add(x, y):
        return (x.astype(F32) + y.astype(F32)).astype(BF)

    def chain(keep, send, one, two):
        got = hop(send, one, "dp")
        mine, give = add(keep[0], got[0]), add(keep[1], got[1])
        mine = add(mine, hop(give, two, "dp"))
        mask = 4
        while mask < n_dp:
            mine = add(mine, hop(mine, mask, "dp"))
            mask *= 2
        other = hop(mine, two, "dp")
        return mine, other, hop(jnp.stack([mine, other]), one, "dp")

    a_parts = chain(akeep, asend, 1, 2)
    b_parts = chain(bkeep, bsend, 2, 1)

    pick = lambda *s: pl.BlockSpec((1,) + s, lambda b, *_: (b,) + (0,) * len(s))
    extra = t + c + 16
    keep, send, dqkv, own = call(
        attend_back_kernel,
        [((2, extra, d), BF), ((2, extra, d), BF), ((3 * c, d), BF), ((8, d), F32)],
        (ids, g0, g1r, gxr, gcr, e, inv_l, k, v, qst, kt, tokens, query_weight.T, key_weight.T, value_weight.T, dout, v2, v3, vh, present),
        prefetch=1, grid=(blocks,),
        specs=[pick(c, quarter), pick(c, quarter), pl.BlockSpec((2, 1, c, quarter), lambda b, *_: (0, b, 0, 0)),
               pl.BlockSpec((2, 1, c, quarter), lambda b, *_: (0, b, 0, 0)), pick(heads, length, length), pick(8, length),
               pl.BlockSpec((length, c), lambda b, *_: (b, 0)), pl.BlockSpec((length, c), lambda b, *_: (b, 0)), pick(c, length), pick(c, length),
               pl.BlockSpec((length, d), lambda b, *_: (b, 0)), full(c, d), full(c, d), full(c, d), full(4, c, d), full(8, d), full(8, d), full(8, d),
               full(blocks, length)],
        out_specs=[full(2, extra, d), full(2, extra, d), full(3 * c, d), full(8, d)],
        scratch=[pltpu.VMEM((c, length), BF), pltpu.VMEM((3 * c, length), BF), pltpu.VMEM((length, d), BF), pltpu.VMEM((3 * c, d), F32), pltpu.VMEM((16, d), F32)],
        flops=12e9, nbytes=2e7, name="attend_back",
    )
    got = hop(send, 1)
    give = add(keep[1], got[1])
    mine = add(keep[0], got[0])
    recv = hop(give, 2)
    n_c = 4 * ((3 * c + c + 32 + 63) // 64) * 16
    grad_rows, ckeep, csend = call(
        tail_kernel,
        [((t, d), BF)] + [((2, n_c // 4, d), BF)] * 2,
        (bits, mine, recv, grad_one, dqkv, own, vg),
        prefetch=1, specs=[VM] * 6, scratch=[pltpu.VMEM((n_c, d), F32)], nbytes=1e7, name="tail",
    )
    c_parts = chain(ckeep, csend, 1, 2)

    outs = call(
        spread_kernel,
        [((blocks, length, d), BF)] * 3,
        (hs, *gather(student_rows), *gather(pruned_rows), *gather(grad_rows)),
        prefetch=1, specs=[ANY] * 12, out_specs=[ANY] * 3, scratch=[pltpu.SemaphoreType.DMA((12 * blocks,))], nbytes=2e7, name="spread",
    )
    student, pruned, tokens_grad = (o.reshape(rows, d) for o in outs)

    uw, iw, qw, kw, vw, ow, qb, vb, ob, fg, fs, ib, ub, sg, ss, ha, ua, da, me, pe = call(
        final_kernel,
        [((w, d), F32), ((d, w), F32), ((c, d), F32), ((c, d), F32), ((c, d), F32), ((c, d), F32), ((c,), F32), ((c,), F32), ((d,), F32), ((d,), F32), ((d,), F32),
         ((w,), F32), ((d,), F32), ((d,), F32), ((d,), F32), ((heads,), F32), ((w,), F32), ((d,), F32), ((1,), F32), ((1,), F32)],
        (bits, ids[4:5], consts, *a_parts, *b_parts, *c_parts),
        prefetch=2, specs=[VM] * 10, out_specs=[VM] * 15 + [SM] + [VM] * 2 + [SM] * 2,
        scratch=[pltpu.VMEM((n_c, d), F32)], nbytes=2e7, name="final",
    )
    return (
        student, pruned, tokens_grad, qw.T, qb, kw.T, vw.T, vb, ow, ob, fg, fs, iw, ib, uw, ub, sg, ss, ha, ua, da, me.reshape(()), pe.reshape(()),
    )


def solution(mesh):
    row, col, lead, unit, none = P("dp", None), P(None, "head"), P("head", None), P("head"), P()
    return jax.shard_map(
        partial(shards, n_dp=mesh.shape["dp"]),
        mesh=mesh,
        in_specs=(row, row, row, row, col, unit, col, col, unit, lead, none, none, none, col, unit, lead, none, none, none) + (unit,) * 4 + (none,) * 2 + (unit,) * 2 + (none,),
        out_specs=(row, row, row, col, unit, col, col, unit, lead, none, none, none, col, unit, lead, none, none, none, unit, unit, none, none, none),
        check_vma=False,
    )
```

```python
from functools import partial

import jax
import jax.numpy as jnp
from jax import lax
from jax.experimental import pallas as pl
from jax.experimental.pallas import tpu as pltpu
from jax.sharding import PartitionSpec as P

F32 = jnp.float32
BF = jnp.bfloat16
HD = 64
EPS = 1e-05
VEC = 32
CH = 32
MB = 1024 * 1024
COST = 5e8

HGATE, HKEEP, OUTB, FG, FS, OUTERB, SG, SS, UGATE, INB, HEADG, QB, VB = range(13)


def dot(a, b):
    return jnp.dot(a, b, preferred_element_type=F32)


def dot_nt(a, b):
    return lax.dot_general(a, b, (((1,), (1,)), ((), ())), preferred_element_type=F32)


def dot_tn(a, b):
    return lax.dot_general(a, b, (((0,), (0,)), ((), ())), preferred_element_type=F32)


def gelu_parts(v):
    z = jnp.abs(v) * 0.7071067811865476
    e = jnp.exp(-(z * z))
    t = 1.0 / (1.0 + 0.3275911 * z)
    p = 0.5 * 1.061405429
    p = p * t - 0.5 * 1.453152027
    p = p * t + 0.5 * 1.421413741
    p = p * t - 0.5 * 0.284496736
    p = p * t + 0.5 * 0.254829592
    q = p * t * e
    return jnp.where(v >= 0.0, 1.0 - q, q), e


def fold(x):
    return jnp.sum(x.reshape(x.shape[0] // 8, 8, x.shape[1]), axis=0)


def mean(x):
    return jnp.mean(x, axis=1, keepdims=True)


def call(kernel, outs, args, specs=None, scratch=(), grid=(), prefetch=0, out_specs=None, us=1.0, limit=40, name=None):
    vmem = pl.BlockSpec(memory_space=pltpu.VMEM)
    specs = specs or [vmem] * (len(args) - prefetch)
    out_specs = out_specs or [vmem] * len(outs)
    return pl.pallas_call(
        kernel,
        out_shape=[pltpu.HBM(*o[:2]) if len(o) > 2 else jax.ShapeDtypeStruct(*o) for o in outs],
        grid_spec=pltpu.PrefetchScalarGridSpec(
            num_scalar_prefetch=prefetch, grid=grid, in_specs=specs, out_specs=out_specs, scratch_shapes=list(scratch)
        ),
        compiler_params=pltpu.CompilerParams(vmem_limit_bytes=limit * MB),
        cost_estimate=pl.CostEstimate(flops=int(us * COST), bytes_accessed=0, transcendentals=0),
        name=name,
    )(*args)


VM = pl.BlockSpec(memory_space=pltpu.VMEM)
SM = pl.BlockSpec(memory_space=pltpu.SMEM)
ANY = pl.BlockSpec(memory_space=pl.ANY)
HBM = pl.BlockSpec(memory_space=pltpu.HBM)


def prep_kernel(*refs):
    count = (len(refs) - 3) // 2
    srcs, wo, consts, pack, held, sem = refs[:count], refs[count], refs[count + 1], refs[count + 2], refs[count + 3 : -1], refs[-1]
    w = consts.shape[1]
    c = wo.shape[0]
    copies = [pltpu.make_async_copy(a, b, sem.at[i]) for i, (a, b) in enumerate(zip(srcs, held))]
    copies.append(pltpu.make_async_copy(wo, pack.at[pl.ds(0, c)], sem.at[count]))
    for copy in copies:
        copy.start()
    for copy in copies:
        copy.wait()
    ua, un, uk, ib, da, dn, dk, ob, fg, fs, ub, sg, ss, qb, vb, ha, hn, hk = held

    def line(ref):
        return ref[...].astype(F32).reshape(1, ref.shape[0])

    def gate(a, n):
        return jax.nn.sigmoid((a + n) * 1.5)

    consts[...] = jnp.zeros_like(consts)
    consts[HGATE : HGATE + 1, :] = gate(line(da), line(dn))
    for row, ref in ((HKEEP, dk), (OUTB, ob), (FG, fg), (FS, fs), (OUTERB, ub), (SG, sg), (SS, ss), (INB, ib)):
        consts[row : row + 1, :] = line(ref)
    ugate = gate(line(ua), line(un))
    consts[UGATE : UGATE + 1, :] = ugate
    consts[QB : QB + 1, :c] = line(qb)
    consts[VB : VB + 1, :c] = line(vb)
    lane = lax.broadcasted_iota(jnp.int32, (1, w), 1)
    logit = jnp.zeros((1, w), F32)
    keep = jnp.zeros((1, w), F32)
    for i in range(c // HD):
        here = (lane >= i * HD) & (lane < (i + 1) * HD)
        logit = jnp.where(here, ha[i] + hn[i], logit)
        keep = jnp.where(here, hk[i].astype(F32), keep)
    hgate = jax.nn.sigmoid(logit * 1.5)
    consts[HEADG : HEADG + 1, :] = hgate

    def halves(x):
        high = x.astype(BF).astype(F32)
        return high, x - high

    uh, ul = halves(ugate)
    hh, hl = halves(hgate)
    rows = [uh, ul, line(uk), line(ib), hh, hl, keep] + [jnp.zeros((1, w), F32)] * (VEC - 7)
    pack[c:, :] = jnp.concatenate(rows, axis=0).astype(BF)


def attend_kernel(ids, tok, wq, wk, wv, consts, seg, live, c0, c1, cfar, e_ref, inv_ref, k_ref, v_ref, qst_ref, kt_ref, bias):
    c = wq.shape[0]
    length = tok.shape[0]
    quarter = length // 4
    x = tok[...]
    q = ((dot_nt(x, wq[...]) + consts[QB : QB + 1, :c]).astype(BF).astype(F32) * HD ** (-0.5)).astype(BF)
    k = dot_nt(x, wk[...]).astype(BF)
    v = (dot_nt(x, wv[...]) + consts[VB : VB + 1, :c]).astype(BF)
    k_ref[...] = k
    v_ref[...] = v
    qst = q.astype(F32).T.astype(BF)
    qst_ref[0] = qst
    kt_ref[0] = k.astype(F32).T.astype(BF)
    vt = v.astype(F32).T.astype(BF)
    seg_row = seg[0].astype(F32)
    code = jnp.where(live[0] == 1, seg_row, -1.0)
    code_col = jnp.broadcast_to(code, (128, length)).T[:, :1]
    row = lax.broadcasted_iota(jnp.int32, (length, length), 0)
    col = lax.broadcasted_iota(jnp.int32, (length, length), 1)
    bias[...] = jnp.where((code_col == seg_row) | (row == col), 0.0, -1e30)
    h = ids[0]
    inv_ref[...] = jnp.zeros_like(inv_ref)
    for i in range(c // HD):
        part = slice(i * HD, (i + 1) * HD)
        s = dot(k[:, part], qst[part, :]) + bias[...]
        top = jnp.max(s, axis=0, keepdims=True)
        e = jnp.exp(s - top)
        inv = 1.0 / jnp.sum(e, axis=0, keepdims=True)
        low = e.astype(BF)
        e_ref[0, i] = low
        inv_ref[0, i : i + 1, :] = inv
        ct = (dot(vt[part, :], low) * inv).astype(BF)
        bias_out = ((c0, 0), (c1, 1), (cfar, 2), (cfar, 3))
        for ref, r in bias_out:
            for j in range(4):

                @pl.when((h ^ r) == j)
                def _():
                    piece = ct[:, j * quarter : (j + 1) * quarter]
                    if r < 2:
                        ref[0, part, :] = piece
                    else:
                        ref[r - 2, 0, part, :] = piece


def mark(marks, value, first, second):
    lane = lax.broadcasted_iota(jnp.int32, marks.shape, 1)
    full = jnp.broadcast_to(value, marks.shape)
    high = full.astype(BF).astype(F32)
    return jnp.where(lane == first, high, jnp.where(lane == second, full - high, marks))


def pull(srcs, dst, p, sem):
    half = dst.shape[1] // 2
    w0, w1, w2x, w2y, w3x, w3y = srcs
    mine = pl.ds(pl.multiple_of(p * half, 16), half)
    other = pl.ds(pl.multiple_of((1 - p) * half, 16), half)
    return [
        [pltpu.make_async_copy(w0, dst.at[0], sem.at[0])],
        [pltpu.make_async_copy(w1, dst.at[1], sem.at[1])],
        [pltpu.make_async_copy(w2x, dst.at[2, mine], sem.at[2]), pltpu.make_async_copy(w2y, dst.at[2, other], sem.at[3])],
        [pltpu.make_async_copy(w3x, dst.at[3, mine], sem.at[4]), pltpu.make_async_copy(w3y, dst.at[3, other], sem.at[5])],
    ]


def pull_packs(packs, wo, vec, sem):
    c = wo.shape[1] if wo is not None else packs[0].shape[0] - VEC
    copies = []
    for r, a in enumerate(packs):
        if wo is not None:
            copies.append(pltpu.make_async_copy(a.at[pl.ds(0, c)], wo.at[r], sem.at[r]))
        copies.append(pltpu.make_async_copy(a.at[pl.ds(c, VEC)], vec.at[r], sem.at[4 + r]))
    return copies


def start(copies):
    for copy in copies:
        copy.start()


def wait(copies):
    for copy in copies:
        copy.wait()


def load_rows(src, dst, h, sem, blocks, quarter):
    return [
        pltpu.make_async_copy(src.at[pl.ds(b * 4 * quarter + pl.multiple_of(h * quarter, quarter), quarter)], dst.at[pl.ds(b * quarter, quarter)], sem.at[b])
        for b in range(blocks)
    ]


def head_rows(vec, soft, c):
    if soft:
        return (vec[4:5, :] + vec[5:6, :])[:, :c]
    return vec[6:7, :][:, :c]


def project(pieces, wos, vecs, gated, attn, consts, soft):
    c = wos[0].shape[0]
    blocks, _, quarter = pieces[0].shape
    for r in range(4):
        g = head_rows(vecs[r][...].astype(F32), soft, c)
        for b in range(blocks):
            gated[r, b * quarter : (b + 1) * quarter, :] = (pieces[r][b].astype(F32).T * g).astype(BF)
    total = dot(gated[0], wos[0][...])
    for r in range(1, 4):
        total = total + dot(gated[r], wos[r][...])
    attn[...] = total + consts[OUTB : OUTB + 1, :]


def first_kernel(ids, c0, c1, xr, cr, s0, s1, s2, s3, tok_any, consts, first_low, normed, inv, attn, gated, wo, vec, tok, sem, tsem):
    blocks, c, quarter = c0.shape
    loads = load_rows(tok_any, tok, ids[0], tsem, blocks, quarter) + pull_packs((s0, s1, s2, s3), wo, vec, sem)
    start(loads)
    wait(loads)
    project([c0, c1, xr.at[0], cr.at[1]], [wo.at[r] for r in range(4)], [vec.at[r] for r in range(4)], gated, attn, consts, True)

    @pl.loop(0, tok.shape[0] // CH)
    def _(i):
        rows = pl.ds(pl.multiple_of(i * CH, CH), CH)
        x = tok[rows, :].astype(F32) + consts[HGATE : HGATE + 1, :] * attn[rows, :]
        x = x - mean(x)
        iv = lax.rsqrt(mean(x * x) + EPS)
        n = x * iv
        normed[rows, :] = n
        inv[rows, :] = jnp.broadcast_to(iv, (CH, 128))
        first_low[rows, :] = (n * consts[FG : FG + 1, :] + consts[FS : FS + 1, :]).astype(BF)


def ffn_inner(first, wins, vecs, hidden, soft, udact=None, waits=None):
    w = wins[0].shape[1]
    step = 256
    for r in range(4):
        wait(waits[r])
        vec = vecs[r][...].astype(F32)
        for s in range(0, w, step):
            at = slice(s, s + step)
            z = dot(first[...], wins[r][:, at]) + vec[3:4, at]
            phi, e = gelu_parts(z)
            if soft:
                g = vec[0:1, at] + vec[1:2, at]
                udact[r, :, at] = (g * (phi + z * e * 0.3989422804014327)).astype(BF)
            else:
                g = vec[2:3, at]
            hidden[r, :, at] = (g * (z * phi)).astype(BF)


def ffn_outer(hidden, outers, ffn, consts, waits):
    wait(waits[0])
    total = dot(hidden[0], outers[0][...])
    for r in range(1, 4):
        wait(waits[r])
        total = total + dot(hidden[r], outers[r][...])
    ffn[...] = total + consts[OUTERB : OUTERB + 1, :]


def row_mask(live, h, b, quarter, at):
    count = jnp.sum(live[b : b + 1, :].astype(F32))
    place = (h * quarter + at).astype(F32) + lax.broadcasted_iota(jnp.int32, (CH, 1), 0).astype(F32)
    return jnp.where(place < count, 1.0, 0.0)


def inner_kernel(ids, first_low, *refs):
    wsrc, packs, hidden, udact, win, vec, sem, vsem = refs[:6], refs[6:10], *refs[10:]
    waits = pull(wsrc, win, ids[1], sem)
    small = pull_packs(packs, None, vec, vsem)
    start(small)
    for copies in waits:
        start(copies)
    wait(small)
    ffn_inner(first_low, [win.at[r] for r in range(4)], [vec.at[r] for r in range(4)], hidden, True, udact, waits)


def second_kernel(ids, hidden, normed, *refs):
    wsrc, teach_any, live, consts, student, grad_two, gffn, vecs_out, outer, teach, ffn, acc, sem, tsem = refs[:6], *refs[6:]
    blocks, length = live.shape
    quarter = length // 4
    h = ids[0]
    rowload = load_rows(teach_any, teach, h, tsem, blocks, quarter)
    waits = pull(wsrc, outer, ids[1], sem)
    for copies in waits:
        start(copies)
    start(rowload)
    ffn_outer(hidden, [outer.at[r] for r in range(4)], ffn, consts, waits)
    wait(rowload)
    acc[...] = jnp.zeros_like(acc)
    for b in range(blocks):

        @pl.loop(0, quarter // CH)
        def _(i):
            rows = pl.ds(pl.multiple_of(b * quarter + i * CH, CH), CH)
            f = ffn[rows, :]
            hg = consts[HGATE : HGATE + 1, :]
            x = normed[rows, :] * consts[FG : FG + 1, :] + consts[FS : FS + 1, :] + hg * f
            x = x - mean(x)
            iv = lax.rsqrt(mean(x * x) + EPS)
            n = x * iv
            out = n * consts[SG : SG + 1, :] + consts[SS : SS + 1, :]
            student[rows, :] = out.astype(BF)
            err = (out - teach[rows, :].astype(F32)) * row_mask(live, h, b, quarter, i * CH)
            acc[0] += fold(err * n)
            acc[1] += fold(err)
            acc[4] += fold(err * err)
            e = err * consts[SG : SG + 1, :]
            g = iv * (e - mean(e) - n * mean(e * n))
            grad_two[rows, :] = g
            gf = hg * g
            acc[2] += fold(gf)
            acc[3] += fold(g * f)
            gffn[rows, :] = gf.astype(BF)

    vecs_out[...] = jnp.zeros_like(vecs_out)
    for j in range(5):
        vecs_out[j : j + 1, :] = jnp.sum(acc[j], axis=0, keepdims=True)


def hard_kernel(ids, c0, c1, xr, cr, *refs):
    isrc, osrc, packs = refs[:6], refs[6:12], refs[12:16]
    tok_any, teach_any, live, consts, pruned, win, wo, outer, vec, tok, teach, gated, attn, first, low, hidden, acc, sem, tsem = refs[16:]
    blocks, length = live.shape
    quarter = length // 4
    h = ids[0]
    early = load_rows(tok_any, tok, h, tsem.at[0], blocks, quarter) + pull_packs(packs, wo, vec, sem.at[2])
    rowload = load_rows(teach_any, teach, h, tsem.at[1], blocks, quarter)
    iwaits, owaits = pull(isrc, win, ids[1], sem.at[0]), pull(osrc, outer, ids[1], sem.at[1])
    start(early)
    for copies in iwaits + owaits + [rowload]:
        start(copies)
    wait(early)
    vecs = [vec.at[r] for r in range(4)]
    project([c0, c1, xr.at[0], cr.at[1]], [wo.at[r] for r in range(4)], vecs, gated, attn, consts, False)

    @pl.loop(0, tok.shape[0] // CH)
    def _(i):
        rows = pl.ds(pl.multiple_of(i * CH, CH), CH)
        x = tok[rows, :].astype(F32) + consts[HKEEP : HKEEP + 1, :] * attn[rows, :]
        x = x - mean(x)
        n = x * lax.rsqrt(mean(x * x) + EPS)
        y = n * consts[FG : FG + 1, :] + consts[FS : FS + 1, :]
        first[rows, :] = y
        low[rows, :] = y.astype(BF)

    ffn_inner(low, [win.at[r] for r in range(4)], vecs, hidden, False, None, iwaits)
    ffn_outer(hidden, [outer.at[r] for r in range(4)], attn, consts, owaits)
    wait(rowload)
    acc[...] = jnp.zeros_like(acc)
    for b in range(blocks):

        @pl.loop(0, quarter // CH)
        def _(i):
            rows = pl.ds(pl.multiple_of(b * quarter + i * CH, CH), CH)
            x = first[rows, :] + consts[HKEEP : HKEEP + 1, :] * attn[rows, :]
            x = x - mean(x)
            n = x * lax.rsqrt(mean(x * x) + EPS)
            out = n * consts[SG : SG + 1, :] + consts[SS : SS + 1, :]
            pruned[rows, :] = out.astype(BF)
            err = (out - teach[rows, :].astype(F32)) * row_mask(live, h, b, quarter, i * CH)
            acc[...] += fold(err * err)

    error = mark(jnp.zeros((1, pruned.shape[1]), F32), jnp.sum(acc[...]), 0, 1)
    pruned[blocks * quarter :, :] = jnp.concatenate([error, jnp.zeros((15, pruned.shape[1]), F32)], axis=0).astype(BF)


def back_kernel(ids, gffn, udact, *refs):
    isrc, osrc, packs = refs[:6], refs[6:12], refs[12:16]
    grad_two, normed, inv, attn, gated, v2, live, consts, g0, g1, gfar, dkeep, dsend, grad_one, win, wo, outer, vec, gi, back, ga, acc, sem = refs[16:]
    c = wo.shape[1]
    w = win.shape[2]
    blocks, _, quarter = g0.shape
    owaits, iwaits = pull(osrc, outer, ids[1], sem.at[0]), pull(isrc, win, ids[1], sem.at[1])
    late = pull_packs(packs, wo, vec, sem.at[2])
    for copies in owaits + iwaits + [late]:
        start(copies)
    for r in range(4):
        wait(owaits[r])
        for s in range(0, w, 256):
            at = slice(s, s + 256)
            gi[r, :, at] = (dot_nt(gffn[...], outer[r, at, :]) * udact[r, :, at].astype(F32)).astype(BF)
    wait(iwaits[0])
    total = dot_nt(gi[0], win[0])
    for r in range(1, 4):
        wait(iwaits[r])
        total = total + dot_nt(gi[r], win[r])
    back[...] = total
    acc[...] = jnp.zeros_like(acc)

    @pl.loop(0, back.shape[0] // CH)
    def _(i):
        rows = pl.ds(pl.multiple_of(i * CH, CH), CH)
        n = normed[rows, :]
        gf = grad_two[rows, :] + back[rows, :]
        acc[0] += fold(gf * n)
        acc[1] += fold(gf)
        e = gf * consts[FG : FG + 1, :]
        g = inv[rows, :1] * (e - mean(e) - n * mean(e * n))
        grad_one[rows, :] = g
        gat = consts[HGATE : HGATE + 1, :] * g
        acc[2] += fold(gat)
        acc[3] += fold(g * attn[rows, :])
        ga[rows, :] = gat.astype(BF)

    d = back.shape[1]
    v3 = [jnp.sum(acc[j], axis=0, keepdims=True) for j in range(4)]
    count = jnp.zeros((), F32)
    for j in range(blocks):
        real = jnp.sum(live[j : j + 1, :].astype(F32))
        count += jnp.clip(real - (ids[0] * quarter).astype(F32), 0.0, float(quarter))
    marks = mark(jnp.zeros((1, d), F32), jnp.sum(v2[4:5, :]), ids[3], ids[3] + ids[4])
    marks = mark(marks, count, ids[3] + 2 * ids[4], ids[3] + 3 * ids[4])
    lines = jnp.concatenate([v2[0:3, :], *v3[:3], v2[3:4, :] + v3[3], marks, jnp.zeros((8, d), F32)], axis=0).astype(BF)
    wait(late)
    for r in range(4):
        gg = dot_nt(ga[...], wo[r]) * head_rows(vec[r].astype(F32), True, c)
        for b in range(blocks):
            piece = gg[b * quarter : (b + 1) * quarter, :].T.astype(BF)
            if r == 0:
                g0[b] = piece
            elif r == 1:
                g1[b] = piece
            else:
                gfar[r - 2, b] = piece
        part = dsend if r % 2 else dkeep
        part[r // 2, :c, :] = dot_tn(gated[r], ga[...]).astype(BF)
        part[r // 2, c:, :] = lines


def units_kernel(f0, f1, fx, fd, consts, win, hidden, udact):
    for r, f in enumerate((f0, f1, fx, fd)):
        rows = slice(r * f0.shape[0], (r + 1) * f0.shape[0])
        for s in range(0, win.shape[1], 256):
            at = slice(s, s + 256)
            z = dot(f[...], win[:, at]) + consts[INB : INB + 1, at]
            phi, e = gelu_parts(z)
            g = consts[UGATE : UGATE + 1, at]
            udact[rows, at] = (g * (phi + z * e * 0.3989422804014327)).astype(BF)
            hidden[rows, at] = (g * (z * phi)).astype(BF)


def slots(src, keep, send, first_bit, second_bit):
    n = keep.shape[1]
    for a in range(2):
        for b in range(2):
            j = (first_bit ^ a) * 2 + (second_bit ^ b)
            rows = src[pl.ds(pl.multiple_of(j * n, 16), n), :].astype(BF)
            if a == 0:
                keep[b] = rows
            else:
                send[b] = rows


def grads_kernel(ids, f0, f1, fx, fd, g0, g1, gx, gd, outer, consts, hidden, udact, akeep, asend, bkeep, bsend, vecs_out, first, gffn, gi, big, acc, sem):
    n = f0.shape[0]
    loads = []
    for r, (f, g) in enumerate(zip((f0, f1, fx, fd), (g0, g1, gx, gd))):
        loads.append(pltpu.make_async_copy(g, gffn.at[pl.ds(r * n, n)], sem.at[r]))
        loads.append(pltpu.make_async_copy(f, first.at[pl.ds(r * n, n)], sem.at[4 + r]))
    for copy in loads:
        copy.start()
    for copy in loads:
        copy.wait()
    big[...] = dot_tn(hidden[...], gffn[...])
    slots(big, akeep, asend, ids[1], ids[2])
    acc[...] = jnp.zeros_like(acc)
    for r in range(4):
        rows = slice(r * n, (r + 1) * n)
        for s in range(0, outer.shape[0], 256):
            at = slice(s, s + 256)
            gh = dot_nt(gffn[rows, :], outer[at, :])
            g = (gh * udact[rows, at].astype(F32)).astype(BF)
            gi[rows, at] = g
            acc[0, :, at] += fold(gh * hidden[rows, at].astype(F32))
            acc[1, :, at] += fold(g.astype(F32))
    big[...] = dot_tn(first[...], gi[...])
    slots(big, bkeep, bsend, ids[2], ids[1])
    vecs_out[...] = jnp.zeros_like(vecs_out)
    for j in range(2):
        vecs_out[j : j + 1, :] = jnp.sum(acc[j], axis=0, keepdims=True)


def attend_back_kernel(ids, g0, g1, gxr, gcr, e_ref, inv_ref, k_ref, v_ref, qst, kt, tok, wq, wk, wv, dmine, drecv, vg, keep, send, ckeep, csend, dct, dt, low, wacc, cacc, big):
    b = pl.program_id(0)
    h = ids[0]
    c, d = wq.shape
    length = tok.shape[0]
    quarter = length // 4
    heads = c // HD

    @pl.when(b == 0)
    def _():
        wacc[...] = jnp.zeros_like(wacc)
        cacc[...] = jnp.zeros_like(cacc)

    for r, piece in enumerate((g0[0], g1[0], gxr[0, 0], gcr[1, 0])):
        dct[:, pl.ds(pl.multiple_of((h ^ r) * quarter, 128), quarter)] = piece
    for i in range(heads):
        part = slice(i * HD, (i + 1) * HD)
        inv = inv_ref[0, i : i + 1, :]
        dcp = (dct[part, :].astype(F32) * inv).astype(BF)
        dp = dot(v_ref[:, part], dcp)
        e = e_ref[0, i].astype(F32)
        w = e * dp
        delta = jnp.sum(w, axis=0, keepdims=True)
        ds = (w - e * (inv * delta)).astype(BF)
        dt[i * HD : (i + 1) * HD, :] = (dot(kt[0, part, :], ds) * HD ** (-0.5)).astype(BF)
        dt[c + i * HD : c + (i + 1) * HD, :] = dot_nt(qst[0, part, :], ds).astype(BF)
        dt[2 * c + i * HD : 2 * c + (i + 1) * HD, :] = dot_nt(dcp, e_ref[0, i]).astype(BF)
        cacc[8:9, i * 128 : (i + 1) * 128] += jnp.broadcast_to(jnp.sum(delta, axis=1, keepdims=True), (1, 128))
    wacc[...] += dot(dt[...], tok[...])
    nat = dt[...].astype(F32).T
    cacc[0:8, : 3 * c] += fold(nat)
    nat = nat.astype(BF)
    part = dot(nat[:, :c], wq[...]) + dot(nat[:, c : 2 * c], wk[...]) + dot(nat[:, 2 * c :], wv[...])
    low[...] = part.astype(BF)
    for r in range(4):
        rows = low[pl.ds(pl.multiple_of((h ^ r) * quarter, quarter), quarter), :]
        at = pl.ds(pl.multiple_of(b * quarter, quarter), quarter)
        if r % 2 == 0:
            keep[r // 2, at, :] = rows
        else:
            send[r // 2, at, :] = rows

    @pl.when(b == pl.num_programs(0) - 1)
    def _():
        n = 3 * c
        big[...] = jnp.zeros_like(big)
        big[:n, :] = wacc[...]
        big[n : n + c + 16, :] = dmine[...].astype(F32) + drecv[...].astype(F32)
        n = n + c + 16
        col = jnp.sum(cacc[0:8, :], axis=0, keepdims=True)
        big[n : n + 1, :c] = col[:, :c]
        big[n + 1 : n + 2, :c] = col[:, 2 * c : 3 * c]
        big[n + 2 : n + 3, : heads * 128] = cacc[8:9, : heads * 128]
        big[n + 8 : n + 16, :] = vg[...]
        slots(big, ckeep, csend, ids[1], ids[2])


def final_kernel(ids, consts, ak, ao, aq, bk, bo, bq, ck, co, cq, hard, uw, iw, qw, kw, vw, ow, qb, vb, ob, fg, fs, ib, ub, sg, ss, ha, ua, da, me, pe, big):
    d = consts.shape[1]
    c = qw.shape[0]

    def place(dst, refs, first_bit, second_bit):
        k, o, q = refs
        n = k.shape[0]
        for a in range(2):
            for b in range(2):
                j = (first_bit ^ a) * 2 + (second_bit ^ b)
                src = (k if b == 0 else o)[...] if a == 0 else q[b]
                dst[pl.ds(pl.multiple_of(j * n, 16), n), :] = src.astype(F32)

    place(uw, (ak, ao, aq), ids[1], ids[2])
    place(iw, (bk, bo, bq), ids[2], ids[1])
    place(big, (ck, co, cq), ids[1], ids[2])
    qw[...] = big[:c, :]
    kw[...] = big[c : 2 * c, :]
    vw[...] = big[2 * c : 3 * c, :]
    n = 3 * c
    ow[...] = big[n : n + c, :]
    n = n + c
    vec = big[n : n + 16, :]
    own = big[n + 16 : n + 32, :]
    for ref, row in ((sg, 0), (ss, 1), (ub, 2), (fg, 3), (fs, 4), (ob, 5)):
        ref[...] = vec[row : row + 1, :].reshape(d)
    hg = consts[HGATE : HGATE + 1, :]
    da[...] = (1.5 * vec[6:7, :] * hg * (1.0 - hg)).reshape(d)
    ug = consts[UGATE : UGATE + 1, :]
    ua[...] = (1.5 * own[8:9, :] * (1.0 - ug)).reshape(d)
    ib[...] = own[9:10, :].reshape(d)
    qb[...] = own[0:1, :c].reshape(c)
    vb[...] = own[1:2, :c].reshape(c)
    gate = consts[HEADG : HEADG + 1, :]
    for i in range(c // HD):
        g = gate[0, i * HD]
        ha[i] = 1.5 * own[2, i * 128] * (1.0 - g)
    lane = lax.broadcasted_iota(jnp.int32, (1, d), 1)
    nd = ids[4]
    hard_sum = hard[0, 0]
    marks = vec[7:8, :]

    def between(lo, hi):
        return jnp.sum(jnp.where((lane >= lo * nd) & (lane < hi * nd), marks, 0.0))

    live = jnp.maximum(between(2, 4), 1.0)
    me[0] = 0.5 * between(0, 2) / live
    pe[0] = 0.5 * hard_sum / live


def spread_kernel(h_ref, *refs):
    count = (len(refs) - 1) // 5
    sem = refs[-1]
    copies = []
    for a in range(count):
        out = refs[4 * count + a]
        for r in range(4):
            src = refs[4 * a + r]
            blocks = out.shape[0]
            quarter = out.shape[1] // 4
            for b in range(blocks):
                at = pl.ds(pl.multiple_of((h_ref[0] ^ r) * quarter, quarter), quarter)
                copies.append(pltpu.make_async_copy(src.at[pl.ds(b * quarter, quarter)], out.at[b, at], sem.at[len(copies)]))
    for copy in copies:
        copy.start()
    for copy in copies:
        copy.wait()


def shards(
    tokens, teacher, segments, present, query_weight, query_bias, key_weight, value_weight, value_bias, output_weight, output_bias,
    first_gain, first_shift, inner_weight, inner_bias, outer_weight, outer_bias, second_gain, second_shift, head_alpha, head_noise,
    unit_alpha, unit_noise, hidden_alpha, hidden_noise, head_keep, unit_keep, hidden_keep, n_dp,
):
    rows, d = tokens.shape
    blocks, length = segments.shape
    heads = head_alpha.shape[0]
    c = heads * HD
    w = unit_alpha.shape[0]
    quarter = length // 4
    t = blocks * quarter
    n_head = 4
    h = lax.axis_index("head").astype(jnp.int32)
    i_dp = lax.axis_index("dp").astype(jnp.int32)
    bit0, bit1 = i_dp & 1, (i_dp >> 1) & 1
    ids = jnp.stack([h, bit0, bit1, i_dp * n_head + h, jnp.int32(n_dp * n_head)])

    def hop(x, mask, axis="head"):
        size = n_head if axis == "head" else n_dp
        return lax.ppermute(x, axis, [(i, i ^ mask) for i in range(size)])

    def in_hbm(x):
        return pltpu.with_memory_space_constraint(x, pltpu.HBM)

    def after(x, *done):
        return lax.optimization_barrier((x, *done))[0]

    def add(x, y):
        return (x.astype(F32) + y.astype(F32)).astype(BF)

    half = d // 2
    inner_x = hop(lax.dynamic_slice_in_dim(inner_weight, bit0 * half, half), 2)
    outer_x = hop(lax.dynamic_slice_in_dim(outer_weight, bit0 * half, half), 2)
    inner_1, outer_1 = hop(inner_weight, 1), hop(outer_weight, 1)

    small = (unit_alpha, unit_noise, unit_keep, inner_bias, hidden_alpha, hidden_noise, hidden_keep, output_bias, first_gain, first_shift,
             outer_bias, second_gain, second_shift, query_bias, value_bias, head_alpha, head_noise, head_keep)
    consts, pack = call(
        prep_kernel,
        [((16, d), F32), ((c + VEC, w), BF)],
        tuple(in_hbm(a) for a in (*small, output_weight)),
        specs=[ANY] * 19, scratch=[(pltpu.VMEM if a.shape[0] > heads else pltpu.SMEM)(a.shape, a.dtype) for a in small] + [pltpu.SemaphoreType.DMA((19,))], us=2, name="prep",
    )
    pack_2 = hop(pack, 2)
    pack_1 = hop(pack, 1)

    seg3 = segments.reshape(blocks, 1, length)
    live3 = present.reshape(blocks, 1, length)
    full = lambda *s: pl.BlockSpec(s, lambda b, *_: (0,) * len(s))
    c0, c1, cfar, e, inv_l, k, v, qst, kt = call(
        attend_kernel,
        [((blocks, c, quarter), BF), ((blocks, c, quarter), BF), ((2, blocks, c, quarter), BF), ((blocks, heads, length, length), BF, HBM),
         ((blocks, 8, length), F32), ((rows, c), BF, HBM), ((rows, c), BF, HBM), ((blocks, c, length), BF, HBM), ((blocks, c, length), BF, HBM)],
        (ids, in_hbm(tokens), *(in_hbm(a.T) for a in (query_weight, key_weight, value_weight)), consts, seg3, live3),
        prefetch=1, grid=(blocks,),
        specs=[pl.BlockSpec((length, d), lambda b, *_: (b, 0)), full(c, d), full(c, d), full(c, d), full(16, d),
               pl.BlockSpec((1, 1, length), lambda b, *_: (b, 0, 0)), pl.BlockSpec((1, 1, length), lambda b, *_: (b, 0, 0))],
        out_specs=[pl.BlockSpec((1, c, quarter), lambda b, *_: (b, 0, 0)), pl.BlockSpec((1, c, quarter), lambda b, *_: (b, 0, 0)),
                   pl.BlockSpec((2, 1, c, quarter), lambda b, *_: (0, b, 0, 0)), pl.BlockSpec((1, heads, length, length), lambda b, *_: (b, 0, 0, 0)),
                   pl.BlockSpec((1, 8, length), lambda b, *_: (b, 0, 0)), pl.BlockSpec((length, c), lambda b, *_: (b, 0)),
                   pl.BlockSpec((length, c), lambda b, *_: (b, 0)), pl.BlockSpec((1, c, length), lambda b, *_: (b, 0, 0)),
                   pl.BlockSpec((1, c, length), lambda b, *_: (b, 0, 0))],
        scratch=[pltpu.VMEM((length, length), F32)], us=9, name="attend",
    )
    cx = hop(cfar, 2)
    c1r = hop(c1, 1)
    inner_x, outer_x, pack_2 = after(inner_x, c0), after(outer_x, c0), after(pack_2, c0)
    inner_y, inner_3x = hop(inner_x, 1, "dp"), hop(inner_x, 1)
    outer_y, outer_3x = hop(outer_x, 1, "dp"), hop(outer_x, 1)
    packs = (pack, pack_1, pack_2, hop(pack_2, 1))
    pieces = (c0, c1r, cx, hop(cx, 1))

    first_low, normed, inv1, attn, gated = call(
        first_kernel,
        [((t, d), BF), ((t, d), F32), ((t, 128), F32), ((t, d), F32), ((4, t, c), BF)],
        (ids, *pieces, *packs, tokens, consts),
        prefetch=1, specs=[VM] * 4 + [ANY] * 5 + [VM],
        scratch=[pltpu.VMEM((4, c, w), BF), pltpu.VMEM((4, VEC, w), BF), pltpu.VMEM((t, d), BF), pltpu.SemaphoreType.DMA((8,)), pltpu.SemaphoreType.DMA((blocks,))],
        us=5, name="first",
    )
    first_2 = hop(first_low, 2)
    first_1 = hop(first_low, 1)
    inner_y, outer_y = after(inner_y, first_low), after(outer_y, first_low)
    inners = (inner_weight, inner_1, inner_x, inner_y, inner_3x, hop(inner_y, 1))

    hidden, udact = call(
        inner_kernel,
        [((4, t, w), BF), ((4, t, w), BF)],
        (ids, first_low, *inners, *packs),
        prefetch=1, specs=[VM] + [ANY] * 10,
        scratch=[pltpu.VMEM((4, d, w), BF), pltpu.VMEM((4, VEC, w), BF), pltpu.SemaphoreType.DMA((6,)), pltpu.SemaphoreType.DMA((8,))], us=9, name="inner",
    )
    outer_y = after(outer_y, hidden)
    outers = (outer_weight, outer_1, outer_x, outer_y, outer_3x, hop(outer_y, 1))

    student_rows, grad_two, gffn, v2 = call(
        second_kernel,
        [((t, d), BF), ((t, d), F32), ((t, d), BF), ((8, d), F32)],
        (ids, hidden, normed, *outers, teacher, present, consts),
        prefetch=1, specs=[VM] * 2 + [ANY] * 7 + [VM] * 2,
        scratch=[pltpu.VMEM((4, w, d), BF), pltpu.VMEM((t, d), BF), pltpu.VMEM((t, d), F32), pltpu.VMEM((5, 8, d), F32), pltpu.SemaphoreType.DMA((6,)),
                 pltpu.SemaphoreType.DMA((blocks,))], us=6, name="second",
    )
    gffn_2 = hop(gffn, 2)
    gffn_1 = hop(gffn, 1)
    first_2 = after(first_2, gffn)
    firsts = (first_low, first_1, first_2, hop(first_2, 1))

    g0, g1, gfar, dkeep, dsend, grad_one = call(
        back_kernel,
        [((blocks, c, quarter), BF), ((blocks, c, quarter), BF), ((2, blocks, c, quarter), BF), ((2, c + 16, d), BF), ((2, c + 16, d), BF), ((t, d), F32)],
        (ids, gffn, udact, *inners, *outers, *packs, grad_two, normed, inv1, attn, gated, v2, present, consts),
        prefetch=1, specs=[VM] * 2 + [ANY] * 16 + [VM] * 8,
        scratch=[pltpu.VMEM((4, d, w), BF), pltpu.VMEM((4, c, w), BF), pltpu.VMEM((4, w, d), BF), pltpu.VMEM((4, VEC, w), BF), pltpu.VMEM((4, t, w), BF),
                 pltpu.VMEM((t, d), F32), pltpu.VMEM((t, d), BF), pltpu.VMEM((4, 8, d), F32), pltpu.SemaphoreType.DMA((3, 8))], us=13, name="back",
    )
    gx = hop(gfar, 2)
    g1r = hop(g1, 1)
    d_got = hop(dsend, 1)
    gffn_2 = after(gffn_2, g0)
    gffns = (gffn, gffn_1, gffn_2, hop(gffn_2, 1))

    hidden_own, udact_own = call(
        units_kernel, [((rows, w), BF), ((rows, w), BF)], (after(firsts[0], g0), *firsts[1:], consts, inner_weight), us=6, name="units"
    )
    gx, d_got = after(gx, hidden_own), after(d_got, hidden_own)
    gpieces = (g0, g1r, gx, hop(gx, 1))
    d_mine, d_give = add(dkeep[0], d_got[0]), add(dkeep[1], d_got[1])
    d_recv = hop(d_give, 2)

    akeep, asend, bkeep, bsend, vg = call(
        grads_kernel,
        [((2, w // 4, d), BF)] * 2 + [((2, d // 4, w), BF)] * 2 + [((8, w), F32)],
        (ids, *firsts, *gffns, outer_weight, consts, hidden_own, udact_own),
        prefetch=1, specs=[ANY] * 8 + [VM] * 4,
        scratch=[pltpu.VMEM((rows, d), BF), pltpu.VMEM((rows, d), BF), pltpu.VMEM((rows, w), BF), pltpu.VMEM((w, d), F32), pltpu.VMEM((2, 8, w), F32), pltpu.SemaphoreType.DMA((8,))],
        us=8, name="grads",
    )
    gpieces = (after(g0, akeep), *gpieces[1:])
    a_got, b_got = hop(asend, 1, "dp"), hop(bsend, 2, "dp")
    student_rows = after(student_rows, akeep)
    student_2 = hop(student_rows, 2)
    student_1 = hop(student_rows, 1)

    pick = lambda *s: pl.BlockSpec((1,) + s, lambda b, *_: (b,) + (0,) * len(s))
    n_c = 4 * ((3 * c + c + 32 + 63) // 64) * 16
    keep, send, ckeep, csend = call(
        attend_back_kernel,
        [((2, t, d), BF), ((2, t, d), BF), ((2, n_c // 4, d), BF), ((2, n_c // 4, d), BF)],
        (ids, *gpieces, e, inv_l, k, v, qst, kt, tokens, query_weight.T, key_weight.T, value_weight.T, d_mine, d_recv, vg),
        prefetch=1, grid=(blocks,),
        specs=[pick(c, quarter), pick(c, quarter), pl.BlockSpec((2, 1, c, quarter), lambda b, *_: (0, b, 0, 0)),
               pl.BlockSpec((2, 1, c, quarter), lambda b, *_: (0, b, 0, 0)), pick(heads, length, length), pick(8, length),
               pl.BlockSpec((length, c), lambda b, *_: (b, 0)), pl.BlockSpec((length, c), lambda b, *_: (b, 0)), pick(c, length), pick(c, length),
               pl.BlockSpec((length, d), lambda b, *_: (b, 0)), full(c, d), full(c, d), full(c, d), full(c + 16, d), full(c + 16, d), full(8, d)],
        out_specs=[full(2, t, d), full(2, t, d), full(2, n_c // 4, d), full(2, n_c // 4, d)],
        scratch=[pltpu.VMEM((c, length), BF), pltpu.VMEM((3 * c, length), BF), pltpu.VMEM((length, d), BF), pltpu.VMEM((3 * c, d), F32), pltpu.VMEM((16, d), F32),
                 pltpu.VMEM((n_c, d), F32)],
        us=15, name="attend_back",
    )
    got = hop(send, 1)
    c_got = hop(csend, 1, "dp")
    a_got, b_got, student_2 = after(a_got, keep), after(b_got, keep), after(student_2, keep)
    students = (student_rows, student_1, student_2, hop(student_2, 1))
    a_mine, a_give = add(akeep[0], a_got[0]), add(akeep[1], a_got[1])
    b_mine, b_give = add(bkeep[0], b_got[0]), add(bkeep[1], b_got[1])
    a_got, b_got = hop(a_give, 2, "dp"), hop(b_give, 1, "dp")
    give = add(keep[1], got[1])
    mine = add(keep[0], got[0])
    recv = hop(give, 2)
    both = after(jnp.stack([add(a_mine, a_got), add(b_mine, b_got)]), give)

    def across(x):
        mask = 4
        while mask < n_dp:
            x = add(x, hop(x, mask, "dp"))
            mask *= 2
        return x

    summed = across(both)
    c_got = after(c_got, both)
    c_mine, c_give = add(ckeep[0], c_got[0]), add(ckeep[1], c_got[1])
    c_got = hop(c_give, 2, "dp")
    (pruned_rows,) = call(
        hard_kernel,
        [((t + 16, d), BF)],
        (ids, after(c0, both, c_give), *pieces[1:], *inners, *outers, *packs, tokens, teacher, present, consts),
        prefetch=1, specs=[VM] * 4 + [ANY] * 18 + [VM] * 2,
        scratch=[pltpu.VMEM((4, d, w), BF), pltpu.VMEM((4, c, w), BF), pltpu.VMEM((4, w, d), BF), pltpu.VMEM((4, VEC, w), BF), pltpu.VMEM((t, d), BF),
                 pltpu.VMEM((t, d), BF), pltpu.VMEM((4, t, c), BF), pltpu.VMEM((t, d), F32), pltpu.VMEM((t, d), F32), pltpu.VMEM((t, d), BF),
                 pltpu.VMEM((4, t, w), BF), pltpu.VMEM((8, d), F32), pltpu.SemaphoreType.DMA((3, 8)), pltpu.SemaphoreType.DMA((2, blocks))],
        us=15, name="hard",
    )
    recv, c_got = after(recv, pruned_rows), after(c_got, pruned_rows)
    grad_rows = (grad_one + (mine.astype(F32) + recv.astype(F32))).astype(BF)
    grad_2 = hop(grad_rows, 2)
    grad_1 = hop(grad_rows, 1)
    pruned_2 = hop(after(pruned_rows, grad_rows), 2)
    pruned_1 = hop(pruned_rows, 1)
    c_mine = across(add(c_mine, c_got))
    summed = after(summed, grad_rows)
    a_mine, b_mine = summed[0], summed[1]
    a_other, b_other = hop(a_mine, 2, "dp"), hop(b_mine, 1, "dp")
    a_parts = (a_mine, a_other, hop(jnp.stack([a_mine, a_other]), 1, "dp"))
    b_parts = (b_mine, b_other, hop(jnp.stack([b_mine, b_other]), 2, "dp"))
    c_other = hop(c_mine, 2, "dp")
    c_parts = (c_mine, c_other, hop(jnp.stack([c_mine, c_other]), 1, "dp"))
    grads = (grad_rows, grad_1, grad_2, hop(grad_2, 1))
    pruneds = (pruned_rows, pruned_1, pruned_2, hop(pruned_2, 1))
    hard_sum = jnp.broadcast_to(sum(jnp.sum(x[t : t + 8, :128].astype(F32)) for x in pruneds), (8, 128))
    mask = 1
    while mask < n_dp:
        hard_sum = hard_sum + hop(hard_sum, mask, "dp")
        mask *= 2

    outs = call(
        spread_kernel,
        [((blocks, length, d), BF)] * 3,
        (ids, *students, *pruneds, *grads),
        prefetch=1, specs=[VM] * 12, out_specs=[ANY] * 3, scratch=[pltpu.SemaphoreType.DMA((12 * blocks,))], us=3, name="spread",
    )
    student, pruned, tokens_grad = (o.reshape(rows, d) for o in outs)

    uw, iw, qw, kw, vw, ow, qb, vb, ob, fg, fs, ib, ub, sg, ss, ha, ua, da, me, pe = call(
        final_kernel,
        [((w, d), F32), ((d, w), F32), ((c, d), F32), ((c, d), F32), ((c, d), F32), ((c, d), F32), ((c,), F32), ((c,), F32), ((d,), F32), ((d,), F32), ((d,), F32),
         ((w,), F32), ((d,), F32), ((d,), F32), ((d,), F32), ((heads,), F32), ((w,), F32), ((d,), F32), ((1,), F32), ((1,), F32)],
        (ids, consts, *a_parts, *b_parts, *c_parts, hard_sum),
        prefetch=1, specs=[VM] * 11, out_specs=[VM] * 15 + [SM] + [VM] * 2 + [SM] * 2,
        scratch=[pltpu.VMEM((n_c, d), F32)], us=4, name="final",
    )
    return (
        student, pruned, tokens_grad, qw.T, qb, kw.T, vw.T, vb, ow, ob, fg, fs, iw, ib, uw, ub, sg, ss, ha, ua, da, me.reshape(()), pe.reshape(()),
    )


def solution(mesh):
    row, col, lead, unit, none = P("dp", None), P(None, "head"), P("head", None), P("head"), P()
    return jax.shard_map(
        partial(shards, n_dp=mesh.shape["dp"]),
        mesh=mesh,
        in_specs=(row, row, row, row, col, unit, col, col, unit, lead, none, none, none, col, unit, lead, none, none, none) + (unit,) * 4 + (none,) * 2 + (unit,) * 2 + (none,),
        out_specs=(row, row, row, col, unit, col, col, unit, lead, none, none, none, col, unit, lead, none, none, none, unit, unit, none, none, none),
        check_vma=False,
    )
```

```python
from functools import partial

import jax
import jax.numpy as jnp
from jax import lax
from jax.experimental import pallas as pl
from jax.experimental.pallas import tpu as pltpu
from jax.sharding import PartitionSpec as P

F32 = jnp.float32
BF = jnp.bfloat16
HD = 64
EPS = 1e-05
VEC = 32
CH = 128
MB = 1024 * 1024
COST = 5e8

HGATE, HKEEP, OUTB, FG, FS, OUTERB, SG, SS, UGATE, INB, HEADG, QB, VB = range(13)


def dot(a, b):
    return jnp.dot(a, b, preferred_element_type=F32)


def dot_nt(a, b):
    return lax.dot_general(a, b, (((1,), (1,)), ((), ())), preferred_element_type=F32)


def dot_tn(a, b):
    return lax.dot_general(a, b, (((0,), (0,)), ((), ())), preferred_element_type=F32)


def gelu_parts(v):
    z = jnp.abs(v) * 0.7071067811865476
    e = jnp.exp(-(z * z))
    t = 1.0 / (1.0 + 0.3275911 * z)
    p = 0.5 * 1.061405429
    p = p * t - 0.5 * 1.453152027
    p = p * t + 0.5 * 1.421413741
    p = p * t - 0.5 * 0.284496736
    p = p * t + 0.5 * 0.254829592
    q = p * t * e
    return jnp.where(v >= 0.0, 1.0 - q, q), e


def fold(x):
    return jnp.sum(x.reshape(x.shape[0] // 8, 8, x.shape[1]), axis=0)


def mean(x):
    return jnp.mean(x, axis=1, keepdims=True)


def call(kernel, outs, args, specs=None, scratch=(), grid=(), prefetch=0, out_specs=None, us=1.0, limit=40, name=None):
    vmem = pl.BlockSpec(memory_space=pltpu.VMEM)
    specs = specs or [vmem] * (len(args) - prefetch)
    out_specs = out_specs or [vmem] * len(outs)
    return pl.pallas_call(
        kernel,
        out_shape=[pltpu.HBM(*o[:2]) if len(o) > 2 else jax.ShapeDtypeStruct(*o) for o in outs],
        grid_spec=pltpu.PrefetchScalarGridSpec(
            num_scalar_prefetch=prefetch, grid=grid, in_specs=specs, out_specs=out_specs, scratch_shapes=list(scratch)
        ),
        compiler_params=pltpu.CompilerParams(vmem_limit_bytes=limit * MB),
        cost_estimate=pl.CostEstimate(flops=int(us * COST), bytes_accessed=0, transcendentals=0),
        name=name,
    )(*args)


VM = pl.BlockSpec(memory_space=pltpu.VMEM)
SM = pl.BlockSpec(memory_space=pltpu.SMEM)
ANY = pl.BlockSpec(memory_space=pl.ANY)
HBM = pl.BlockSpec(memory_space=pltpu.HBM)


def prep_kernel(*refs):
    count = (len(refs) - 3) // 2
    srcs, wo, consts, pack, held, sem = refs[:count], refs[count], refs[count + 1], refs[count + 2], refs[count + 3 : -1], refs[-1]
    w = consts.shape[1]
    c = wo.shape[0]
    copies = [pltpu.make_async_copy(a, b, sem.at[i]) for i, (a, b) in enumerate(zip(srcs, held))]
    copies.append(pltpu.make_async_copy(wo, pack.at[pl.ds(0, c)], sem.at[count]))
    for copy in copies:
        copy.start()
    for copy in copies:
        copy.wait()
    ua, un, uk, ib, da, dn, dk, ob, fg, fs, ub, sg, ss, qb, vb, ha, hn, hk = held

    def line(ref):
        return ref[...].astype(F32).reshape(1, ref.shape[0])

    def gate(a, n):
        return jax.nn.sigmoid((a + n) * 1.5)

    consts[...] = jnp.zeros_like(consts)
    consts[HGATE : HGATE + 1, :] = gate(line(da), line(dn))
    for row, ref in ((HKEEP, dk), (OUTB, ob), (FG, fg), (FS, fs), (OUTERB, ub), (SG, sg), (SS, ss), (INB, ib)):
        consts[row : row + 1, :] = line(ref)
    ugate = gate(line(ua), line(un))
    consts[UGATE : UGATE + 1, :] = ugate
    consts[QB : QB + 1, :c] = line(qb)
    consts[VB : VB + 1, :c] = line(vb)
    lane = lax.broadcasted_iota(jnp.int32, (1, w), 1)
    logit = jnp.zeros((1, w), F32)
    keep = jnp.zeros((1, w), F32)
    for i in range(c // HD):
        here = (lane >= i * HD) & (lane < (i + 1) * HD)
        logit = jnp.where(here, ha[i] + hn[i], logit)
        keep = jnp.where(here, hk[i].astype(F32), keep)
    hgate = jax.nn.sigmoid(logit * 1.5)
    consts[HEADG : HEADG + 1, :] = hgate

    def halves(x):
        high = x.astype(BF).astype(F32)
        return high, x - high

    uh, ul = halves(ugate)
    hh, hl = halves(hgate)
    rows = [uh, ul, line(uk), line(ib), hh, hl, keep] + [jnp.zeros((1, w), F32)] * (VEC - 7)
    pack[c:, :] = jnp.concatenate(rows, axis=0).astype(BF)


def attend_kernel(ids, tok, wq, wk, wv, consts, seg, live, c0, c1, cfar, e_ref, inv_ref, k_ref, v_ref, q_ref, qst_ref, kt_ref, bias, ct):
    c = wq.shape[0]
    length = tok.shape[0]
    quarter = length // 4
    x = tok[...]
    q = ((dot_nt(x, wq[...]) + consts[QB : QB + 1, :c]).astype(BF).astype(F32) * HD ** (-0.5)).astype(BF)
    k = dot_nt(x, wk[...]).astype(BF)
    v = (dot_nt(x, wv[...]) + consts[VB : VB + 1, :c]).astype(BF)
    k_ref[...] = k
    v_ref[...] = v
    q_ref[...] = q
    qst = q.astype(F32).T.astype(BF)
    qst_ref[0] = qst
    kt_ref[0] = k.astype(F32).T.astype(BF)
    vt = v.astype(F32).T.astype(BF)
    seg_row = seg[0].astype(F32)
    code = jnp.where(live[0] == 1, seg_row, -1.0)
    code_col = jnp.broadcast_to(code, (128, length)).T[:, :1]
    row = lax.broadcasted_iota(jnp.int32, (length, length), 0)
    col = lax.broadcasted_iota(jnp.int32, (length, length), 1)
    bias[...] = jnp.where((code_col == seg_row) | (row == col), 0.0, -1e30)
    h = ids[0]
    inv_ref[...] = jnp.zeros_like(inv_ref)
    for i in range(c // HD):
        part = slice(i * HD, (i + 1) * HD)
        s = dot(k[:, part], qst[part, :]) + bias[...]
        top = jnp.max(s, axis=0, keepdims=True)
        e = jnp.exp(s - top)
        inv = 1.0 / jnp.sum(e, axis=0, keepdims=True)
        low = e.astype(BF)
        e_ref[0, i] = low
        inv_ref[0, i : i + 1, :] = inv
        ct[part, :] = (dot(vt[part, :], low) * inv).astype(BF)
    for r in range(4):
        piece = ct[:, pl.ds(pl.multiple_of((h ^ r) * quarter, 128), quarter)]
        if r < 2:
            (c0, c1)[r][0] = piece
        else:
            cfar[r - 2, 0] = piece


def mark(marks, value, first, second):
    lane = lax.broadcasted_iota(jnp.int32, marks.shape, 1)
    full = jnp.broadcast_to(value, marks.shape)
    high = full.astype(BF).astype(F32)
    return jnp.where(lane == first, high, jnp.where(lane == second, full - high, marks))


def unit_chunks(weights, p):
    half = weights[2].shape[1]
    chunks = []
    for r in range(2):
        chunks += [(r, weights[r], s, 256, s) for s in range(0, weights[r].shape[1], 256)]
    for r, (mine, other) in ((2, weights[2:4]), (3, weights[4:6])):
        for ref, base in ((mine, p * half), (other, (1 - p) * half)):
            for s in range(0, half, 256):
                chunks.append((r, ref, s, min(256, half - s), pl.multiple_of(base + s, 128)))
    return chunks


def start(copies):
    for copy in copies:
        copy.start()


def wait(copies):
    for copy in copies:
        copy.wait()


def load_rows(src, dst, h, sem, blocks, quarter):
    return [
        pltpu.make_async_copy(src.at[pl.ds(b * 4 * quarter + pl.multiple_of(h * quarter, quarter), quarter)], dst.at[pl.ds(b * quarter, quarter)], sem.at[b])
        for b in range(blocks)
    ]


def head_rows(vec, soft, c):
    if soft:
        return (vec[4:5, :] + vec[5:6, :])[:, :c]
    return vec[6:7, :][:, :c]


def project(pieces, packs, gated, attn, consts, soft):
    blocks, c, quarter = pieces[0].shape
    for r in range(4):
        g = head_rows(packs[r][c:, :].astype(F32), soft, c)
        for b in range(blocks):
            gated[r, b * quarter : (b + 1) * quarter, :] = (pieces[r][b].astype(F32).T * g).astype(BF)
    total = dot(gated[0], packs[0][:c, :])
    for r in range(1, 4):
        total = total + dot(gated[r], packs[r][:c, :])
    attn[...] = total + consts[OUTB : OUTB + 1, :]


def first_kernel(soft, ids, c0, c1, xr, cr, s0, s1, s2, s3, tok_any, consts, first_low, normed, *refs):
    if soft:
        inv, attn, gated, tok, tsem = refs
    else:
        tok, tsem, attn, gated = refs
    blocks, c, quarter = c0.shape
    loads = load_rows(tok_any, tok, ids[0], tsem, blocks, quarter)
    start(loads)
    project([c0, c1, xr.at[0], cr.at[1]], [s0, s1, s2, s3], gated, attn, consts, soft)
    wait(loads)
    gate = HGATE if soft else HKEEP

    @pl.loop(0, tok.shape[0] // CH)
    def _(i):
        rows = pl.ds(pl.multiple_of(i * CH, CH), CH)
        x = tok[rows, :].astype(F32) + consts[gate : gate + 1, :] * attn[rows, :]
        x = x - mean(x)
        iv = lax.rsqrt(mean(x * x) + EPS)
        n = x * iv
        normed[rows, :] = n
        if soft:
            inv[rows, :] = jnp.broadcast_to(iv, (CH, 128))
        first_low[rows, :] = (n * consts[FG : FG + 1, :] + consts[FS : FS + 1, :]).astype(BF)


def ffn_inner(first, wins, packs, p, hidden, soft, udact=None):
    c = packs[0].shape[0] - VEC
    for r, ref, s, n, unit in unit_chunks(wins, p):
        at = pl.ds(unit, n)
        vec = packs[r][c : c + 16, at].astype(F32)
        z = dot(first[...], ref[:, s : s + n]) + vec[3:4, :]
        phi, e = gelu_parts(z)
        if soft:
            g = vec[0:1, :] + vec[1:2, :]
            udact[r, :, at] = (g * (phi + z * e * 0.3989422804014327)).astype(BF)
        else:
            g = vec[2:3, :]
        hidden[r, :, at] = (g * (z * phi)).astype(BF)


def ffn_outer(hidden, outers, ffn, consts):
    half = outers[2].shape[0]
    total = dot(hidden[0], outers[0][...]) + dot(hidden[1], outers[1][...])
    for r, (a, b) in ((2, outers[2:4]), (3, outers[4:6])):
        total = total + dot(hidden[r, :, :half], a[...]) + dot(hidden[r, :, half:], b[...])
    ffn[...] = total + consts[OUTERB : OUTERB + 1, :]


def row_mask(live, h, b, quarter, at):
    count = jnp.sum(live[b : b + 1, :].astype(F32))
    place = (h * quarter + at).astype(F32) + lax.broadcasted_iota(jnp.int32, (CH, 1), 0).astype(F32)
    return jnp.where(place < count, 1.0, 0.0)


def inner_kernel(soft, ids, first_low, *refs):
    ffn_inner(first_low, refs[:6], refs[6:10], ids[1], refs[10], soft, refs[11] if soft else None)


def second_kernel(ids, hidden, normed, *refs):
    wsrc, teach_any, live, consts, student, grad_two, gffn, vecs_out, teach, ffn, acc, tsem = refs[:6], *refs[6:]
    blocks, length = live.shape
    quarter = length // 4
    h = ids[0]
    rowload = load_rows(teach_any, teach, h, tsem, blocks, quarter)
    start(rowload)
    ffn_outer(hidden, wsrc, ffn, consts)
    wait(rowload)
    acc[...] = jnp.zeros_like(acc)
    for b in range(blocks):

        @pl.loop(0, quarter // CH)
        def _(i):
            rows = pl.ds(pl.multiple_of(b * quarter + i * CH, CH), CH)
            f = ffn[rows, :]
            hg = consts[HGATE : HGATE + 1, :]
            x = normed[rows, :] * consts[FG : FG + 1, :] + consts[FS : FS + 1, :] + hg * f
            x = x - mean(x)
            iv = lax.rsqrt(mean(x * x) + EPS)
            n = x * iv
            out = n * consts[SG : SG + 1, :] + consts[SS : SS + 1, :]
            student[rows, :] = out.astype(BF)
            err = (out - teach[rows, :].astype(F32)) * row_mask(live, h, b, quarter, i * CH)
            acc[0] += fold(err * n)
            acc[1] += fold(err)
            acc[4] += fold(err * err)
            e = err * consts[SG : SG + 1, :]
            g = iv * (e - mean(e) - n * mean(e * n))
            grad_two[rows, :] = g
            gf = hg * g
            acc[2] += fold(gf)
            acc[3] += fold(g * f)
            gffn[rows, :] = gf.astype(BF)

    vecs_out[...] = jnp.zeros_like(vecs_out)
    for j in range(5):
        vecs_out[j : j + 1, :] = jnp.sum(acc[j], axis=0, keepdims=True)


def hard_kernel(ids, hidden, normed, *refs):
    wsrc, teach_any, live, consts, pruned, error, teach, ffn, acc, tsem = refs[:6], *refs[6:]
    blocks, length = live.shape
    quarter = length // 4
    h = ids[0]
    rowload = load_rows(teach_any, teach, h, tsem, blocks, quarter)
    start(rowload)
    ffn_outer(hidden, wsrc, ffn, consts)
    wait(rowload)
    acc[...] = jnp.zeros_like(acc)
    for b in range(blocks):

        @pl.loop(0, quarter // CH)
        def _(i):
            rows = pl.ds(pl.multiple_of(b * quarter + i * CH, CH), CH)
            x = normed[rows, :] * consts[FG : FG + 1, :] + consts[FS : FS + 1, :] + consts[HKEEP : HKEEP + 1, :] * ffn[rows, :]
            x = x - mean(x)
            n = x * lax.rsqrt(mean(x * x) + EPS)
            out = n * consts[SG : SG + 1, :] + consts[SS : SS + 1, :]
            pruned[rows, :] = out.astype(BF)
            err = (out - teach[rows, :].astype(F32)) * row_mask(live, h, b, quarter, i * CH)
            acc[...] += fold(err * err)

    error[...] = jnp.broadcast_to(jnp.sum(acc[...]), error.shape)


def back_kernel(ids, gffn, udact, *refs):
    isrc, osrc, packs = refs[:6], refs[6:12], refs[12:16]
    grad_two, normed, inv, attn, gated, v2, live, consts, g0, g1, gfar, dkeep, dsend, grad_one, gi, back, ga, acc = refs[16:]
    c = packs[0].shape[0] - VEC
    w = gi.shape[2]
    half = w // 2
    blocks, _, quarter = g0.shape
    for r, (a, b) in ((0, osrc[:1] * 2), (1, osrc[1:2] * 2), (2, osrc[2:4]), (3, osrc[4:6])):
        for s in (0, 256, 512) if r < 2 else (0, 256, half, half + 256):
            n = 256 if r < 2 or s % half == 0 else half - 256
            ref, row = (a, s) if r < 2 or s < half else (b, s - half)
            at = slice(s, s + n)
            gi[r, :, at] = (dot_nt(gffn[...], ref[row : row + n, :]) * udact[r, :, at].astype(F32)).astype(BF)
    total = dot_nt(gi[0], isrc[0][...]) + dot_nt(gi[1], isrc[1][...])
    for r, (x, y) in ((2, isrc[2:4]), (3, isrc[4:6])):
        for ref, q in ((x, ids[1]), (y, 1 - ids[1])):
            total = total + dot_nt(gi[r, :, pl.ds(pl.multiple_of(q * half, 128), half)], ref[...])
    back[...] = total
    acc[...] = jnp.zeros_like(acc)

    @pl.loop(0, back.shape[0] // CH)
    def _(i):
        rows = pl.ds(pl.multiple_of(i * CH, CH), CH)
        n = normed[rows, :]
        gf = grad_two[rows, :] + back[rows, :]
        acc[0] += fold(gf * n)
        acc[1] += fold(gf)
        e = gf * consts[FG : FG + 1, :]
        g = inv[rows, :1] * (e - mean(e) - n * mean(e * n))
        grad_one[rows, :] = g
        gat = consts[HGATE : HGATE + 1, :] * g
        acc[2] += fold(gat)
        acc[3] += fold(g * attn[rows, :])
        ga[rows, :] = gat.astype(BF)

    d = back.shape[1]
    v3 = [jnp.sum(acc[j], axis=0, keepdims=True) for j in range(4)]
    count = jnp.zeros((), F32)
    for j in range(blocks):
        real = jnp.sum(live[j : j + 1, :].astype(F32))
        count += jnp.clip(real - (ids[0] * quarter).astype(F32), 0.0, float(quarter))
    marks = mark(jnp.zeros((1, d), F32), jnp.sum(v2[4:5, :]), ids[3], ids[3] + ids[4])
    marks = mark(marks, count, ids[3] + 2 * ids[4], ids[3] + 3 * ids[4])
    lines = jnp.concatenate([v2[0:3, :], *v3[:3], v2[3:4, :] + v3[3], marks, jnp.zeros((8, d), F32)], axis=0).astype(BF)
    for r in range(4):
        gg = dot_nt(ga[...], packs[r][:c, :]) * head_rows(packs[r][c:, :].astype(F32), True, c)
        for b in range(blocks):
            piece = gg[b * quarter : (b + 1) * quarter, :].T.astype(BF)
            if r == 0:
                g0[b] = piece
            elif r == 1:
                g1[b] = piece
            else:
                gfar[r - 2, b] = piece
        part = dsend if r % 2 else dkeep
        part[r // 2, :c, :] = dot_tn(gated[r], ga[...]).astype(BF)
        part[r // 2, c:, :] = lines


def units_kernel(f0, f1, fx, fd, consts, win, hidden, udact):
    for r, f in enumerate((f0, f1, fx, fd)):
        rows = slice(r * f0.shape[0], (r + 1) * f0.shape[0])
        for s in range(0, win.shape[1], 256):
            at = slice(s, s + 256)
            z = dot(f[...], win[:, at]) + consts[INB : INB + 1, at]
            phi, e = gelu_parts(z)
            g = consts[UGATE : UGATE + 1, at]
            udact[rows, at] = (g * (phi + z * e * 0.3989422804014327)).astype(BF)
            hidden[rows, at] = (g * (z * phi)).astype(BF)


def slots(src, keep, send, first_bit, second_bit):
    n = keep.shape[1]
    for a in range(2):
        for b in range(2):
            j = (first_bit ^ a) * 2 + (second_bit ^ b)
            rows = src[pl.ds(pl.multiple_of(j * n, 16), n), :].astype(BF)
            if a == 0:
                keep[b] = rows
            else:
                send[b] = rows


def rows_dot(lefts, rights):
    total = dot_tn(lefts[0], rights[0])
    for left, right in zip(lefts[1:], rights[1:]):
        total = total + dot_tn(left, right)
    return total


def outer_grad_kernel(ids, g0, g1, gx, gd, hidden, akeep, asend, big):
    n = g0.shape[0]
    big[...] = rows_dot([hidden[r * n : (r + 1) * n, :] for r in range(4)], [g0[...], g1[...], gx[...], gd[...]])
    slots(big, akeep, asend, ids[1], ids[2])


def inner_grad_kernel(ids, f0, f1, fx, fd, g0, g1, gx, gd, outer, hidden, udact, bkeep, bsend, vecs_out, gi, big, acc):
    n = f0.shape[0]
    gffns = (g0, g1, gx, gd)
    acc[...] = jnp.zeros_like(acc)
    for r in range(4):
        rows = slice(r * n, (r + 1) * n)
        for s in range(0, outer.shape[0], 256):
            at = slice(s, s + 256)
            gh = dot_nt(gffns[r][...], outer[at, :])
            g = (gh * udact[rows, at].astype(F32)).astype(BF)
            gi[rows, at] = g
            acc[0, :, at] += fold(gh * hidden[rows, at].astype(F32))
            acc[1, :, at] += fold(g.astype(F32))
    big[...] = rows_dot([f0[...], f1[...], fx[...], fd[...]], [gi[r * n : (r + 1) * n, :] for r in range(4)])
    slots(big, bkeep, bsend, ids[2], ids[1])
    vecs_out[...] = jnp.zeros_like(vecs_out)
    for j in range(2):
        vecs_out[j : j + 1, :] = jnp.sum(acc[j], axis=0, keepdims=True)


def attend_back_kernel(ids, g0, g1, gxr, gcr, e_ref, inv_ref, k_ref, v_ref, q_ref, kt, tok, wq, wk, wv, keep, send, wacc, cacc, dct, nat, low):
    b = pl.program_id(0)
    h = ids[0]
    c, d = wq.shape
    length = tok.shape[0]
    quarter = length // 4
    heads = c // HD

    @pl.when(b == 0)
    def _():
        wacc[...] = jnp.zeros_like(wacc)
        cacc[...] = jnp.zeros_like(cacc)

    for r, piece in enumerate((g0[0], g1[0], gxr[0, 0], gcr[1, 0])):
        dct[:, pl.ds(pl.multiple_of((h ^ r) * quarter, 128), quarter)] = piece
    dq, dk, dv = [], [], []
    for i in range(heads):
        part = slice(i * HD, (i + 1) * HD)
        inv = inv_ref[0, i : i + 1, :]
        dcp = dct[part, :].astype(F32) * inv
        dp = dot(v_ref[:, part], dcp.astype(BF))
        e = e_ref[0, i].astype(F32)
        w = e * dp
        delta = jnp.sum(w, axis=0, keepdims=True)
        ds = (w - e * (inv * delta)).astype(BF)
        dq.append(dot(kt[0, part, :], ds) * HD ** (-0.5))
        dk.append(dot(ds, q_ref[:, part]).astype(BF))
        dv.append(dot(e_ref[0, i], dcp.T.astype(BF)).astype(BF))
        cacc[8:9, i * 128 : (i + 1) * 128] += jnp.broadcast_to(jnp.sum(delta, axis=1, keepdims=True), (1, 128))
    dq = jnp.concatenate(dq, axis=0).T.astype(BF)
    nat[...] = jnp.concatenate([dq, *dk, *dv], axis=1)
    wacc[...] += dot_tn(nat[...], tok[...])
    cacc[0:8, : 3 * c] += fold(nat[...].astype(F32))
    part = dot(nat[:, :c], wq[...]) + dot(nat[:, c : 2 * c], wk[...]) + dot(nat[:, 2 * c :], wv[...])
    low[...] = part.astype(BF)
    for r in range(4):
        rows = low[pl.ds(pl.multiple_of((h ^ r) * quarter, quarter), quarter), :]
        at = pl.ds(pl.multiple_of(b * quarter, quarter), quarter)
        if r % 2 == 0:
            keep[r // 2, at, :] = rows
        else:
            send[r // 2, at, :] = rows


def turn_kernel(ids, wacc, cacc, dmine, drecv, vg, akeep, agot, bkeep, bgot, amine, agive, bmine, bgive, ckeep, csend, big):
    n = wacc.shape[0]
    c = n // 3
    big[n + c + 32 :, :] = jnp.zeros((big.shape[0] - n - c - 32, big.shape[1]), F32)
    big[:n, :] = wacc[...]
    big[n : n + c + 16, :] = dmine[...].astype(F32) + drecv[...].astype(F32)
    n = n + c + 16
    big[n : n + 16, :] = jnp.zeros((16, big.shape[1]), F32)
    col = jnp.sum(cacc[0:8, :], axis=0, keepdims=True)
    big[n : n + 1, :c] = col[:, :c]
    big[n + 1 : n + 2, :c] = col[:, 2 * c : 3 * c]
    big[n + 2 : n + 3, : c * 2] = cacc[8:9, : c * 2]
    big[n + 8 : n + 16, :] = vg[...]
    slots(big, ckeep, csend, ids[1], ids[2])
    for keep, got, mine, give in ((akeep, agot, amine, agive), (bkeep, bgot, bmine, bgive)):
        mine[...] = (keep[0].astype(F32) + got[0].astype(F32)).astype(BF)
        give[...] = (keep[1].astype(F32) + got[1].astype(F32)).astype(BF)


def third_kernel(ids, mine, got, error, error_1, out):
    n, d = mine.shape
    out[:n, :] = (mine[...].astype(F32) + got[...].astype(F32)).astype(BF)
    total = error[0:1, :1] + error_1[0:1, :1]
    place = ids[3] // 4
    zero = jnp.zeros((1, d), F32)
    rows = [mark(zero, total, place, -1), mark(zero, total, -1, place), jnp.zeros((14, d), F32)]
    out[n:, :] = jnp.concatenate(rows, axis=0).astype(BF)


def pair_kernel(amine, aother, bmine, bother, apair, bpair):
    apair[0], apair[1] = amine[...], aother[...]
    bpair[0], bpair[1] = bmine[...], bother[...]


def last_kernel(mine, other, out):
    n = mine.shape[0] - 16
    out[:n, :] = mine[:n, :]
    out[n : 2 * n, :] = other[:n, :]
    out[2 * n :, :] = (mine[n:, :].astype(F32) + other[n:, :].astype(F32)).astype(BF)


def weights_kernel(ids, ak, ao, aq, bk, bo, bq, uw, iw):
    for dst, k, o, q, first_bit, second_bit in ((uw, ak, ao, aq, ids[1], ids[2]), (iw, bk, bo, bq, ids[2], ids[1])):
        n = k.shape[0]
        for a in range(2):
            for b in range(2):
                j = (first_bit ^ a) * 2 + (second_bit ^ b)
                src = (k if b == 0 else o)[...] if a == 0 else q[b]
                dst[pl.ds(pl.multiple_of(j * n, 16), n), :] = src.astype(F32)


def final_kernel(ids, consts, cpair, cq, qw, kw, vw, ow, qb, vb, ob, fg, fs, ib, ub, sg, ss, ha, ua, da, me, pe, big):
    d = consts.shape[1]
    c = qw.shape[0]

    n = big.shape[0] // 4
    for a, src in enumerate((cpair, cq)):
        for b in range(2):
            j = (ids[1] ^ a) * 2 + (ids[2] ^ b)
            big[pl.ds(pl.multiple_of(j * n, 16), n), :] = src[b * n : (b + 1) * n, :].astype(F32)
    qw[...] = big[:c, :]
    kw[...] = big[c : 2 * c, :]
    vw[...] = big[2 * c : 3 * c, :]
    n = 3 * c
    ow[...] = big[n : n + c, :]
    n = n + c
    vec = big[n : n + 16, :]
    own = big[n + 16 : n + 32, :]
    for ref, row in ((sg, 0), (ss, 1), (ub, 2), (fg, 3), (fs, 4), (ob, 5)):
        ref[...] = vec[row : row + 1, :].reshape(d)
    hg = consts[HGATE : HGATE + 1, :]
    da[...] = (1.5 * vec[6:7, :] * hg * (1.0 - hg)).reshape(d)
    ug = consts[UGATE : UGATE + 1, :]
    ua[...] = (1.5 * own[8:9, :] * (1.0 - ug)).reshape(d)
    ib[...] = own[9:10, :].reshape(d)
    qb[...] = own[0:1, :c].reshape(c)
    vb[...] = own[1:2, :c].reshape(c)
    gate = consts[HEADG : HEADG + 1, :]
    for i in range(c // HD):
        g = gate[0, i * HD]
        ha[i] = 1.5 * own[2, i * 128] * (1.0 - g)
    lane = lax.broadcasted_iota(jnp.int32, (1, d), 1)
    nd = ids[4]
    m = cpair.shape[0] - 16
    hard_sum = jnp.sum(cpair[m:, :].astype(F32) + cq[m:, :].astype(F32))
    marks = vec[7:8, :]

    def between(lo, hi):
        return jnp.sum(jnp.where((lane >= lo * nd) & (lane < hi * nd), marks, 0.0))

    live = jnp.maximum(between(2, 4), 1.0)
    me[0] = 0.5 * between(0, 2) / live
    pe[0] = 0.5 * hard_sum / live


def spread_kernel(h_ref, *refs):
    count = (len(refs) - 1) // 5
    sem = refs[-1]
    copies = []
    for a in range(count):
        out = refs[4 * count + a]
        for r in range(4):
            src = refs[4 * a + r]
            blocks = out.shape[0]
            quarter = out.shape[1] // 4
            for b in range(blocks):
                at = pl.ds(pl.multiple_of((h_ref[0] ^ r) * quarter, quarter), quarter)
                copies.append(pltpu.make_async_copy(src.at[pl.ds(b * quarter, quarter)], out.at[b, at], sem.at[len(copies)]))
    for copy in copies:
        copy.start()
    for copy in copies:
        copy.wait()


def shards(
    tokens, teacher, segments, present, query_weight, query_bias, key_weight, value_weight, value_bias, output_weight, output_bias,
    first_gain, first_shift, inner_weight, inner_bias, outer_weight, outer_bias, second_gain, second_shift, head_alpha, head_noise,
    unit_alpha, unit_noise, hidden_alpha, hidden_noise, head_keep, unit_keep, hidden_keep, n_dp,
):
    rows, d = tokens.shape
    blocks, length = segments.shape
    heads = head_alpha.shape[0]
    c = heads * HD
    w = unit_alpha.shape[0]
    quarter = length // 4
    t = blocks * quarter
    n_head = 4
    h = lax.axis_index("head").astype(jnp.int32)
    i_dp = lax.axis_index("dp").astype(jnp.int32)
    bit0, bit1 = i_dp & 1, (i_dp >> 1) & 1
    ids = jnp.stack([h, bit0, bit1, i_dp * n_head + h, jnp.int32(n_dp * n_head)])

    def hop(x, mask, axis="head"):
        size = n_head if axis == "head" else n_dp
        return lax.ppermute(x, axis, [(i, i ^ mask) for i in range(size)])

    def in_hbm(x):
        return pltpu.with_memory_space_constraint(x, pltpu.HBM)

    def after(x, *done):
        return lax.optimization_barrier((x, *done))[0]

    def add(x, y):
        return (x.astype(F32) + y.astype(F32)).astype(BF)

    half = d // 2
    inner_half = lax.dynamic_slice_in_dim(inner_weight, bit0 * half, half, axis=1)
    inner_x = hop(inner_half, 2)

    small = (unit_alpha, unit_noise, unit_keep, inner_bias, hidden_alpha, hidden_noise, hidden_keep, output_bias, first_gain, first_shift,
             outer_bias, second_gain, second_shift, query_bias, value_bias, head_alpha, head_noise, head_keep)
    consts, pack = call(
        prep_kernel,
        [((16, d), F32), ((c + VEC, w), BF)],
        tuple(in_hbm(a) for a in (*small, after(output_weight, inner_half))),
        specs=[ANY] * 19, scratch=[(pltpu.VMEM if a.shape[0] > heads else pltpu.SMEM)(a.shape, a.dtype) for a in small] + [pltpu.SemaphoreType.DMA((19,))], us=2, limit=8, name="prep",
    )
    pack_2 = hop(pack, 2)
    pack_1 = hop(pack, 1)
    inner_1, outer_1 = hop(inner_weight, 1), hop(outer_weight, 1)

    seg3 = segments.reshape(blocks, 1, length)
    live3 = present.reshape(blocks, 1, length)
    full = lambda *s: pl.BlockSpec(s, lambda b, *_: (0,) * len(s))
    c0, c1, cfar, e, inv_l, k, v, q, qst, kt = call(
        attend_kernel,
        [((blocks, c, quarter), BF), ((blocks, c, quarter), BF), ((2, blocks, c, quarter), BF), ((blocks, heads, length, length), BF, HBM),
         ((blocks, 8, length), F32), ((rows, c), BF, HBM), ((rows, c), BF, HBM), ((rows, c), BF, HBM), ((blocks, c, length), BF, HBM), ((blocks, c, length), BF, HBM)],
        (ids, in_hbm(tokens), *(in_hbm(a.T) for a in (query_weight, key_weight, value_weight)), consts, seg3, live3),
        prefetch=1, grid=(blocks,),
        specs=[pl.BlockSpec((length, d), lambda b, *_: (b, 0)), full(c, d), full(c, d), full(c, d), full(16, d),
               pl.BlockSpec((1, 1, length), lambda b, *_: (b, 0, 0)), pl.BlockSpec((1, 1, length), lambda b, *_: (b, 0, 0))],
        out_specs=[pl.BlockSpec((1, c, quarter), lambda b, *_: (b, 0, 0)), pl.BlockSpec((1, c, quarter), lambda b, *_: (b, 0, 0)),
                   pl.BlockSpec((2, 1, c, quarter), lambda b, *_: (0, b, 0, 0)), pl.BlockSpec((1, heads, length, length), lambda b, *_: (b, 0, 0, 0)),
                   pl.BlockSpec((1, 8, length), lambda b, *_: (b, 0, 0)), pl.BlockSpec((length, c), lambda b, *_: (b, 0)),
                   pl.BlockSpec((length, c), lambda b, *_: (b, 0)), pl.BlockSpec((length, c), lambda b, *_: (b, 0)),
                   pl.BlockSpec((1, c, length), lambda b, *_: (b, 0, 0)), pl.BlockSpec((1, c, length), lambda b, *_: (b, 0, 0))],
        scratch=[pltpu.VMEM((length, length), F32), pltpu.VMEM((c, length), BF)], us=9, limit=24, name="attend",
    )
    cx = hop(cfar, 2)
    c1r = hop(c1, 1)
    outer_a = hop(after(outer_weight, c1r)[:half], 2)
    inner_x, pack_2 = after(inner_x, c0), after(pack_2, c0)
    inner_y, inner_3x = hop(inner_x, 1, "dp"), hop(inner_x, 1)
    packs = (pack, pack_1, pack_2, hop(pack_2, 1))
    pieces = (c0, c1r, cx, hop(cx, 1))

    def first(soft, pieces):
        scratch = [pltpu.VMEM((t, d), BF), pltpu.SemaphoreType.DMA((blocks,))]
        more = [((t, 128), F32), ((t, d), F32), ((4, t, c), BF)]
        return call(
            partial(first_kernel, soft),
            [((t, d), BF), ((t, d), F32)] + (more if soft else []),
            (ids, *pieces, *packs, tokens, consts),
            prefetch=1, specs=[VM] * 8 + [ANY, VM],
            scratch=scratch if soft else scratch + [pltpu.VMEM((t, d), F32), pltpu.VMEM((4, t, c), BF)], us=4, limit=12, name="first" if soft else "hard_first",
        )

    def inner(soft, low):
        return call(
            partial(inner_kernel, soft), [((4, t, w), BF)] * (2 if soft else 1), (ids, low, *inners, *packs),
            prefetch=1, us=8, limit=16, name="inner" if soft else "hard_inner",
        )

    first_low, normed, inv1, attn, gated = first(True, pieces)
    first_2 = hop(first_low, 2)
    first_1 = hop(first_low, 1)
    inner_y = after(inner_y, first_low)
    inners = (inner_weight, inner_1, inner_x, inner_y, inner_3x, hop(inner_y, 1))
    hard_low, hard_normed = first(False, (after(c0, first_low), *pieces[1:]))
    outer_a = after(outer_a, hard_low)
    outer_3a = hop(outer_a, 1)
    outer_b = hop(after(outer_weight, outer_a)[half:], 2)
    hidden, udact = inner(True, after(first_low, hard_low))
    (hard_hidden,) = inner(False, after(hard_low, hidden))
    outer_b = after(outer_b, hard_hidden)
    outers = (outer_weight, outer_1, outer_a, outer_b, outer_3a, hop(outer_b, 1))

    student_rows, grad_two, gffn, v2 = call(
        second_kernel,
        [((t, d), BF), ((t, d), F32), ((t, d), BF), ((8, d), F32)],
        (ids, hidden, normed, *outers, teacher, present, consts),
        prefetch=1, specs=[VM] * 8 + [ANY] + [VM] * 2,
        scratch=[pltpu.VMEM((t, d), BF), pltpu.VMEM((t, d), F32), pltpu.VMEM((5, 8, d), F32), pltpu.SemaphoreType.DMA((blocks,))], us=6, limit=16, name="second",
    )
    gffn_2 = hop(gffn, 2)
    gffn_1 = hop(gffn, 1)

    g0, g1, gfar, dkeep, dsend, grad_one = call(
        back_kernel,
        [((blocks, c, quarter), BF), ((blocks, c, quarter), BF), ((2, blocks, c, quarter), BF), ((2, c + 16, d), BF), ((2, c + 16, d), BF), ((t, d), F32)],
        (ids, gffn, udact, *inners, *outers, *packs, grad_two, normed, inv1, attn, gated, v2, present, consts),
        prefetch=1,
        scratch=[pltpu.VMEM((4, t, w), BF), pltpu.VMEM((t, d), F32), pltpu.VMEM((t, d), BF), pltpu.VMEM((4, 8, d), F32)], us=13, limit=24, name="back",
    )
    gx = hop(gfar, 2)
    g1r = hop(g1, 1)
    d_got = hop(dsend, 1)
    gffn_2, first_2 = after(gffn_2, g0), after(first_2, g0)
    firsts = (first_low, first_1, first_2, hop(first_2, 1))
    gffns = (gffn, gffn_1, gffn_2, hop(gffn_2, 1))

    hidden_own, udact_own = call(
        units_kernel, [((rows, w), BF), ((rows, w), BF)], (after(firsts[0], g0), *firsts[1:], consts, inner_weight), us=6, limit=16, name="units"
    )
    gx, d_got = after(gx, hidden_own), after(d_got, hidden_own)
    gpieces = (g0, g1r, gx, hop(gx, 1))
    d_mine, d_give = add(dkeep[0], d_got[0]), add(dkeep[1], d_got[1])
    d_recv = hop(d_give, 2)

    akeep, asend = call(
        outer_grad_kernel, [((2, w // 4, d), BF)] * 2, (ids, *gffns, hidden_own), prefetch=1, scratch=[pltpu.VMEM((w, d), F32)], us=3, limit=16, name="outer_grad"
    )
    a_got = hop(asend, 1, "dp")
    bkeep, bsend, vg = call(
        inner_grad_kernel,
        [((2, d // 4, w), BF)] * 2 + [((8, w), F32)],
        (ids, *firsts, after(gffns[0], akeep), *gffns[1:], outer_weight, hidden_own, udact_own),
        prefetch=1, scratch=[pltpu.VMEM((rows, w), BF), pltpu.VMEM((w, d), F32), pltpu.VMEM((2, 8, w), F32)], us=6, limit=24, name="inner_grad",
    )
    gpieces = (after(g0, bkeep, d_recv), *gpieces[1:])
    b_got = hop(bsend, 2, "dp")
    student_rows = after(student_rows, akeep)
    student_2 = hop(student_rows, 2)
    student_1 = hop(student_rows, 1)

    pick = lambda *s: pl.BlockSpec((1,) + s, lambda b, *_: (b,) + (0,) * len(s))
    n_c = 4 * ((3 * c + c + 32 + 63) // 64) * 16
    keep, send, wacc, cacc = call(
        attend_back_kernel,
        [((2, t, d), BF), ((2, t, d), BF), ((3 * c, d), F32), ((16, d), F32)],
        (ids, *gpieces, *(in_hbm(a) for a in (e, inv_l, k, v, q, kt, tokens)), *(in_hbm(a.T) for a in (query_weight, key_weight, value_weight))),
        prefetch=1, grid=(blocks,),
        specs=[pick(c, quarter), pick(c, quarter), pl.BlockSpec((2, 1, c, quarter), lambda b, *_: (0, b, 0, 0)),
               pl.BlockSpec((2, 1, c, quarter), lambda b, *_: (0, b, 0, 0)), pick(heads, length, length), pick(8, length),
               pl.BlockSpec((length, c), lambda b, *_: (b, 0)), pl.BlockSpec((length, c), lambda b, *_: (b, 0)), pl.BlockSpec((length, c), lambda b, *_: (b, 0)), pick(c, length),
               pl.BlockSpec((length, d), lambda b, *_: (b, 0)), full(c, d), full(c, d), full(c, d)],
        out_specs=[full(2, t, d), full(2, t, d), full(3 * c, d), full(16, d)],
        scratch=[pltpu.VMEM((c, length), BF), pltpu.VMEM((length, 3 * c), BF), pltpu.VMEM((length, d), BF)],
        us=15, limit=32, name="attend_back",
    )
    a_got, b_got, student_2 = after(a_got, keep), after(b_got, keep), after(student_2, keep)
    part = (w // 4, d)
    a_mine, a_give, b_mine, b_give, ckeep, csend = call(
        turn_kernel,
        [(part, BF)] * 4 + [((2, n_c // 4, d), BF)] * 2,
        (ids, wacc, cacc, d_mine, d_recv, vg, akeep, after(a_got, student_2), bkeep, b_got),
        prefetch=1, specs=[VM] * 9, scratch=[pltpu.VMEM((n_c, d), F32)], us=0.1, limit=16, name="turn",
    )
    got = hop(after(send, a_mine), 1)
    c_got = hop(csend, 1, "dp")
    a_got, b_got = hop(a_give, 2, "dp"), hop(b_give, 1, "dp")
    give = add(keep[1], got[1])
    mine = add(keep[0], got[0])
    recv = hop(give, 2)
    students = (student_rows, student_1, student_2, hop(after(student_2, give), 1))
    a_mine, b_mine = add(a_mine, after(a_got, give)), add(b_mine, after(b_got, give))

    def across(x):
        mask = 4
        while mask < n_dp:
            got = hop(x, mask, "dp")
            x = (x, got) if mask * 2 == n_dp else add(x, got)
            mask *= 2
        return x

    a_mine, b_mine = across(a_mine), across(b_mine)
    pruned_rows, error = call(
        hard_kernel,
        [((t, d), BF), ((8, 128), F32)],
        (ids, after(hard_hidden, a_mine[0], b_mine[0], give), hard_normed, *outers, teacher, present, consts),
        prefetch=1, specs=[VM] * 8 + [ANY] + [VM] * 2,
        scratch=[pltpu.VMEM((t, d), BF), pltpu.VMEM((t, d), F32), pltpu.VMEM((8, d), F32), pltpu.SemaphoreType.DMA((blocks,))], us=6, limit=16, name="hard",
    )
    error = error + hop(error, 2)
    error_1 = hop(error, 1)
    recv, c_got = after(recv, pruned_rows), after(c_got, pruned_rows)
    c_mine, c_give = add(ckeep[0], c_got[0]), add(ckeep[1], c_got[1])
    c_got = hop(c_give, 2, "dp")
    grad_rows = (grad_one + (mine.astype(F32) + recv.astype(F32))).astype(BF)
    grad_2 = hop(grad_rows, 2)
    grad_1 = hop(grad_rows, 1)
    pruned_2 = hop(after(pruned_rows, grad_rows), 2)
    pruned_1 = hop(pruned_rows, 1)
    a_mine, b_mine = (add(x, after(got, c_give, grad_rows)) for x, got in (a_mine, b_mine))
    a_other, b_other = hop(a_mine, 2, "dp"), hop(b_mine, 1, "dp")
    (c_mine,) = call(
        third_kernel, [((n_c // 4 + 16, d), BF)], (ids, c_mine, after(c_got, a_mine, b_mine), error, error_1), prefetch=1, us=0.1, limit=8, name="third"
    )
    c_mine = across(c_mine)
    a_pair, b_pair = call(pair_kernel, [((2,) + part, BF)] * 2, (a_mine, after(a_other, c_mine[0]), b_mine, b_other), us=0.1, limit=8, name="pair")
    a_parts = (a_mine, a_other, hop(a_pair, 1, "dp"))
    b_parts = (b_mine, b_other, hop(b_pair, 2, "dp"))
    grad_2 = after(grad_2, a_pair)
    grads = (grad_rows, grad_1, grad_2, hop(grad_2, 1))
    c_mine = add(c_mine[0], after(c_mine[1], a_pair))
    c_other = hop(c_mine, 2, "dp")
    pruned_2 = after(pruned_2, c_mine)
    pruneds = (pruned_rows, pruned_1, pruned_2, hop(pruned_2, 1))

    uw, iw = call(weights_kernel, [((w, d), F32), ((d, w), F32)], (ids, after(a_parts[0], grad_2, pruned_2), *a_parts[1:], *b_parts), prefetch=1, us=1, limit=16, name="weights")
    (c_pair,) = call(last_kernel, [((n_c // 2 + 16, d), BF)], (c_mine, after(c_other, uw)), us=0.1, limit=8, name="last")
    c_last = hop(c_pair, 1, "dp")
    outs = call(
        spread_kernel,
        [((blocks, length, d), BF)] * 3,
        (ids, after(students[0], c_pair), *students[1:], *pruneds, *grads),
        prefetch=1, specs=[VM] * 12, out_specs=[ANY] * 3, scratch=[pltpu.SemaphoreType.DMA((12 * blocks,))], us=1, limit=16, name="spread",
    )
    student, pruned, tokens_grad = (o.reshape(rows, d) for o in outs)
    qw, kw, vw, ow, qb, vb, ob, fg, fs, ib, ub, sg, ss, ha, ua, da, me, pe = call(
        final_kernel,
        [((c, d), F32), ((c, d), F32), ((c, d), F32), ((c, d), F32), ((c,), F32), ((c,), F32), ((d,), F32), ((d,), F32), ((d,), F32),
         ((w,), F32), ((d,), F32), ((d,), F32), ((d,), F32), ((heads,), F32), ((w,), F32), ((d,), F32), ((1,), F32), ((1,), F32)],
        (ids, consts, c_pair, after(c_last, outs[0])),
        prefetch=1, specs=[VM] * 3, out_specs=[VM] * 13 + [SM] + [VM] * 2 + [SM] * 2,
        scratch=[pltpu.VMEM((n_c, d), F32)], us=0.1, limit=16, name="final",
    )
    return (
        student, pruned, tokens_grad, qw.T, qb, kw.T, vw.T, vb, ow, ob, fg, fs, iw, ib, uw, ub, sg, ss, ha, ua, da, me.reshape(()), pe.reshape(()),
    )


def solution(mesh):
    row, col, lead, unit, none = P("dp", None), P(None, "head"), P("head", None), P("head"), P()
    return jax.shard_map(
        partial(shards, n_dp=mesh.shape["dp"]),
        mesh=mesh,
        in_specs=(row, row, row, row, col, unit, col, col, unit, lead, none, none, none, col, unit, lead, none, none, none) + (unit,) * 4 + (none,) * 2 + (unit,) * 2 + (none,),
        out_specs=(row, row, row, col, unit, col, col, unit, lead, none, none, none, col, unit, lead, none, none, none, unit, unit, none, none, none),
        check_vma=False,
    )
```

```python
from functools import partial

import jax
import jax.numpy as jnp
from jax import lax
from jax.experimental import pallas as pl
from jax.experimental.pallas import tpu as pltpu
from jax.sharding import PartitionSpec as P

F32 = jnp.float32
BF = jnp.bfloat16
HD = 64
EPS = 1e-05
VEC = 32
CH = 128
MB = 1024 * 1024
COST = 5e8

HGATE, HKEEP, OUTB, FG, FS, OUTERB, SG, SS, UGATE, INB, HEADG, QB, VB = range(13)


def dot(a, b):
    return jnp.dot(a, b, preferred_element_type=F32)


def dot_nt(a, b):
    return lax.dot_general(a, b, (((1,), (1,)), ((), ())), preferred_element_type=F32)


def dot_tn(a, b):
    return lax.dot_general(a, b, (((0,), (0,)), ((), ())), preferred_element_type=F32)


def gelu_parts(v):
    z = jnp.abs(v) * 0.7071067811865476
    e = jnp.exp(-(z * z))
    t = 1.0 / (1.0 + 0.3275911 * z)
    p = 0.5 * 1.061405429
    p = p * t - 0.5 * 1.453152027
    p = p * t + 0.5 * 1.421413741
    p = p * t - 0.5 * 0.284496736
    p = p * t + 0.5 * 0.254829592
    q = p * t * e
    return jnp.where(v >= 0.0, 1.0 - q, q), e


def fold(x):
    return jnp.sum(x.reshape(x.shape[0] // 8, 8, x.shape[1]), axis=0)


def mean(x):
    return jnp.mean(x, axis=1, keepdims=True)


def call(kernel, outs, args, specs=None, scratch=(), grid=(), prefetch=0, out_specs=None, us=1.0, limit=40, name=None):
    vmem = pl.BlockSpec(memory_space=pltpu.VMEM)
    specs = specs or [vmem] * (len(args) - prefetch)
    out_specs = out_specs or [vmem] * len(outs)
    return pl.pallas_call(
        kernel,
        out_shape=[pltpu.HBM(*o[:2]) if len(o) > 2 else jax.ShapeDtypeStruct(*o) for o in outs],
        grid_spec=pltpu.PrefetchScalarGridSpec(
            num_scalar_prefetch=prefetch, grid=grid, in_specs=specs, out_specs=out_specs, scratch_shapes=list(scratch)
        ),
        compiler_params=pltpu.CompilerParams(vmem_limit_bytes=limit * MB),
        cost_estimate=pl.CostEstimate(flops=int(us * COST), bytes_accessed=0, transcendentals=0),
        name=name,
    )(*args)


VM = pl.BlockSpec(memory_space=pltpu.VMEM)
SM = pl.BlockSpec(memory_space=pltpu.SMEM)
ANY = pl.BlockSpec(memory_space=pl.ANY)
HBM = pl.BlockSpec(memory_space=pltpu.HBM)


def prep_kernel(*refs):
    count = (len(refs) - 3) // 2
    srcs, wo, consts, pack, held, sem = refs[:count], refs[count], refs[count + 1], refs[count + 2], refs[count + 3 : -1], refs[-1]
    w = consts.shape[1]
    c = wo.shape[0]
    copies = [pltpu.make_async_copy(a, b, sem.at[i]) for i, (a, b) in enumerate(zip(srcs, held))]
    copies.append(pltpu.make_async_copy(wo, pack.at[pl.ds(0, c)], sem.at[count]))
    for copy in copies:
        copy.start()
    for copy in copies:
        copy.wait()
    ua, un, uk, ib, da, dn, dk, ob, fg, fs, ub, sg, ss, qb, vb, ha, hn, hk = held

    def line(ref):
        return ref[...].astype(F32).reshape(1, ref.shape[0])

    def gate(a, n):
        return jax.nn.sigmoid((a + n) * 1.5)

    consts[...] = jnp.zeros_like(consts)
    consts[HGATE : HGATE + 1, :] = gate(line(da), line(dn))
    for row, ref in ((HKEEP, dk), (OUTB, ob), (FG, fg), (FS, fs), (OUTERB, ub), (SG, sg), (SS, ss), (INB, ib)):
        consts[row : row + 1, :] = line(ref)
    ugate = gate(line(ua), line(un))
    consts[UGATE : UGATE + 1, :] = ugate
    consts[QB : QB + 1, :c] = line(qb)
    consts[VB : VB + 1, :c] = line(vb)
    lane = lax.broadcasted_iota(jnp.int32, (1, w), 1)
    logit = jnp.zeros((1, w), F32)
    keep = jnp.zeros((1, w), F32)
    for i in range(c // HD):
        here = (lane >= i * HD) & (lane < (i + 1) * HD)
        logit = jnp.where(here, ha[i] + hn[i], logit)
        keep = jnp.where(here, hk[i].astype(F32), keep)
    hgate = jax.nn.sigmoid(logit * 1.5)
    consts[HEADG : HEADG + 1, :] = hgate

    def halves(x):
        high = x.astype(BF).astype(F32)
        return high, x - high

    uh, ul = halves(ugate)
    hh, hl = halves(hgate)
    rows = [uh, ul, line(uk), line(ib), hh, hl, keep] + [jnp.zeros((1, w), F32)] * (VEC - 7)
    pack[c:, :] = jnp.concatenate(rows, axis=0).astype(BF)


def attend_kernel(ids, tok, wq, wk, wv, consts, seg, live, c0, c1, cfar, e_ref, inv_ref, k_ref, v_ref, q_ref, qst_ref, kt_ref, bias, ct):
    c = wq.shape[0]
    length = tok.shape[0]
    quarter = length // 4
    x = tok[...]
    q = ((dot_nt(x, wq[...]) + consts[QB : QB + 1, :c]).astype(BF).astype(F32) * HD ** (-0.5)).astype(BF)
    k = dot_nt(x, wk[...]).astype(BF)
    v = (dot_nt(x, wv[...]) + consts[VB : VB + 1, :c]).astype(BF)
    k_ref[...] = k
    v_ref[...] = v
    q_ref[...] = q
    qst = q.astype(F32).T.astype(BF)
    qst_ref[0] = qst
    kt_ref[0] = k.astype(F32).T.astype(BF)
    vt = v.astype(F32).T.astype(BF)
    seg_row = seg[0].astype(F32)
    code = jnp.where(live[0] == 1, seg_row, -1.0)
    code_col = jnp.broadcast_to(code, (128, length)).T[:, :1]
    row = lax.broadcasted_iota(jnp.int32, (length, length), 0)
    col = lax.broadcasted_iota(jnp.int32, (length, length), 1)
    bias[...] = jnp.where((code_col == seg_row) | (row == col), 0.0, -1e30)
    h = ids[0]
    inv_ref[...] = jnp.zeros_like(inv_ref)
    for i in range(c // HD):
        part = slice(i * HD, (i + 1) * HD)
        s = dot(k[:, part], qst[part, :]) + bias[...]
        top = jnp.max(s, axis=0, keepdims=True)
        e = jnp.exp(s - top)
        inv = 1.0 / jnp.sum(e, axis=0, keepdims=True)
        low = e.astype(BF)
        e_ref[0, i] = low
        inv_ref[0, i : i + 1, :] = inv
        ct[part, :] = (dot(vt[part, :], low) * inv).astype(BF)
    for r in range(4):
        piece = ct[:, pl.ds(pl.multiple_of((h ^ r) * quarter, 128), quarter)]
        if r < 2:
            (c0, c1)[r][0] = piece
        else:
            cfar[r - 2, 0] = piece


def mark(marks, value, first, second):
    lane = lax.broadcasted_iota(jnp.int32, marks.shape, 1)
    full = jnp.broadcast_to(value, marks.shape)
    high = full.astype(BF).astype(F32)
    return jnp.where(lane == first, high, jnp.where(lane == second, full - high, marks))


def unit_chunks(weights, p):
    half = weights[2].shape[1]
    chunks = []
    for r in range(2):
        chunks += [(r, weights[r], s, 256, s) for s in range(0, weights[r].shape[1], 256)]
    for r, (mine, other) in ((2, weights[2:4]), (3, weights[4:6])):
        for ref, base in ((mine, p * half), (other, (1 - p) * half)):
            for s in range(0, half, 256):
                chunks.append((r, ref, s, min(256, half - s), pl.multiple_of(base + s, 128)))
    return chunks


def start(copies):
    for copy in copies:
        copy.start()


def wait(copies):
    for copy in copies:
        copy.wait()


def load_rows(src, dst, h, sem, blocks, quarter):
    return [
        pltpu.make_async_copy(src.at[pl.ds(b * 4 * quarter + pl.multiple_of(h * quarter, quarter), quarter)], dst.at[pl.ds(b * quarter, quarter)], sem.at[b])
        for b in range(blocks)
    ]


def head_rows(vec, soft, c):
    if soft:
        return (vec[4:5, :] + vec[5:6, :])[:, :c]
    return vec[6:7, :][:, :c]


def project(pieces, packs, gated, attn, consts, soft):
    blocks, c, quarter = pieces[0].shape
    for r in range(4):
        g = head_rows(packs[r][c:, :].astype(F32), soft, c)
        for b in range(blocks):
            gated[r, b * quarter : (b + 1) * quarter, :] = (pieces[r][b].astype(F32).T * g).astype(BF)
    total = dot(gated[0], packs[0][:c, :])
    for r in range(1, 4):
        total = total + dot(gated[r], packs[r][:c, :])
    attn[...] = total + consts[OUTB : OUTB + 1, :]


def first_kernel(soft, ids, c0, c1, xr, cr, s0, s1, s2, s3, tok_any, consts, first_low, normed, *refs):
    if soft:
        inv, attn, gated, tok, tsem = refs
    else:
        tok, tsem, attn, gated = refs
    blocks, c, quarter = c0.shape
    loads = load_rows(tok_any, tok, ids[0], tsem, blocks, quarter)
    start(loads)
    project([c0, c1, xr.at[0], cr.at[1]], [s0, s1, s2, s3], gated, attn, consts, soft)
    wait(loads)
    gate = HGATE if soft else HKEEP

    @pl.loop(0, tok.shape[0] // CH)
    def _(i):
        rows = pl.ds(pl.multiple_of(i * CH, CH), CH)
        x = tok[rows, :].astype(F32) + consts[gate : gate + 1, :] * attn[rows, :]
        x = x - mean(x)
        iv = lax.rsqrt(mean(x * x) + EPS)
        n = x * iv
        normed[rows, :] = n
        if soft:
            inv[rows, :] = jnp.broadcast_to(iv, (CH, 128))
        first_low[rows, :] = (n * consts[FG : FG + 1, :] + consts[FS : FS + 1, :]).astype(BF)


def ffn_inner(first, wins, packs, p, hidden, soft, udact=None):
    c = packs[0].shape[0] - VEC
    for r, ref, s, n, unit in unit_chunks(wins, p):
        at = pl.ds(unit, n)
        vec = packs[r][c : c + 16, at].astype(F32)
        z = dot(first[...], ref[:, s : s + n]) + vec[3:4, :]
        phi, e = gelu_parts(z)
        if soft:
            g = vec[0:1, :] + vec[1:2, :]
            udact[r, :, at] = (g * (phi + z * e * 0.3989422804014327)).astype(BF)
        else:
            g = vec[2:3, :]
        hidden[r, :, at] = (g * (z * phi)).astype(BF)


def ffn_outer(hidden, outers, ffn, consts):
    half = outers[2].shape[0]
    total = dot(hidden[0], outers[0][...]) + dot(hidden[1], outers[1][...])
    for r, (a, b) in ((2, outers[2:4]), (3, outers[4:6])):
        total = total + dot(hidden[r, :, :half], a[...]) + dot(hidden[r, :, half:], b[...])
    ffn[...] = total + consts[OUTERB : OUTERB + 1, :]


def row_mask(live, h, b, quarter, at):
    count = jnp.sum(live[b : b + 1, :].astype(F32))
    place = (h * quarter + at).astype(F32) + lax.broadcasted_iota(jnp.int32, (CH, 1), 0).astype(F32)
    return jnp.where(place < count, 1.0, 0.0)


def inner_kernel(soft, ids, first_low, *refs):
    ffn_inner(first_low, refs[:6], refs[6:10], ids[1], refs[10], soft, refs[11] if soft else None)


def second_kernel(ids, hidden, normed, *refs):
    wsrc, teach_any, live, consts, student, grad_two, gffn, vecs_out, teach, ffn, acc, tsem = refs[:6], *refs[6:]
    blocks, length = live.shape
    quarter = length // 4
    h = ids[0]
    rowload = load_rows(teach_any, teach, h, tsem, blocks, quarter)
    start(rowload)
    ffn_outer(hidden, wsrc, ffn, consts)
    wait(rowload)
    acc[...] = jnp.zeros_like(acc)
    for b in range(blocks):

        @pl.loop(0, quarter // CH)
        def _(i):
            rows = pl.ds(pl.multiple_of(b * quarter + i * CH, CH), CH)
            f = ffn[rows, :]
            hg = consts[HGATE : HGATE + 1, :]
            x = normed[rows, :] * consts[FG : FG + 1, :] + consts[FS : FS + 1, :] + hg * f
            x = x - mean(x)
            iv = lax.rsqrt(mean(x * x) + EPS)
            n = x * iv
            out = n * consts[SG : SG + 1, :] + consts[SS : SS + 1, :]
            student[rows, :] = out.astype(BF)
            err = (out - teach[rows, :].astype(F32)) * row_mask(live, h, b, quarter, i * CH)
            acc[0] += fold(err * n)
            acc[1] += fold(err)
            acc[4] += fold(err * err)
            e = err * consts[SG : SG + 1, :]
            g = iv * (e - mean(e) - n * mean(e * n))
            grad_two[rows, :] = g
            gf = hg * g
            acc[2] += fold(gf)
            acc[3] += fold(g * f)
            gffn[rows, :] = gf.astype(BF)

    vecs_out[...] = jnp.zeros_like(vecs_out)
    for j in range(5):
        vecs_out[j : j + 1, :] = jnp.sum(acc[j], axis=0, keepdims=True)


def hard_kernel(ids, hidden, normed, *refs):
    wsrc, teach_any, live, consts, pruned, error, teach, ffn, acc, tsem = refs[:6], *refs[6:]
    blocks, length = live.shape
    quarter = length // 4
    h = ids[0]
    rowload = load_rows(teach_any, teach, h, tsem, blocks, quarter)
    start(rowload)
    ffn_outer(hidden, wsrc, ffn, consts)
    wait(rowload)
    acc[...] = jnp.zeros_like(acc)
    for b in range(blocks):

        @pl.loop(0, quarter // CH)
        def _(i):
            rows = pl.ds(pl.multiple_of(b * quarter + i * CH, CH), CH)
            x = normed[rows, :] * consts[FG : FG + 1, :] + consts[FS : FS + 1, :] + consts[HKEEP : HKEEP + 1, :] * ffn[rows, :]
            x = x - mean(x)
            n = x * lax.rsqrt(mean(x * x) + EPS)
            out = n * consts[SG : SG + 1, :] + consts[SS : SS + 1, :]
            pruned[rows, :] = out.astype(BF)
            err = (out - teach[rows, :].astype(F32)) * row_mask(live, h, b, quarter, i * CH)
            acc[...] += fold(err * err)

    error[...] = jnp.broadcast_to(jnp.sum(acc[...]), error.shape)


def back_kernel(ids, gffn, udact, *refs):
    isrc, osrc, packs = refs[:6], refs[6:12], refs[12:16]
    grad_two, normed, inv, attn, gated, v2, live, consts, g0, g1, gfar, dkeep, dsend, grad_one, gi, back, ga, acc = refs[16:]
    c = packs[0].shape[0] - VEC
    w = gi.shape[2]
    half = w // 2
    blocks, _, quarter = g0.shape
    for r, (a, b) in ((0, osrc[:1] * 2), (1, osrc[1:2] * 2), (2, osrc[2:4]), (3, osrc[4:6])):
        for s in (0, 256, 512) if r < 2 else (0, 256, half, half + 256):
            n = 256 if r < 2 or s % half == 0 else half - 256
            ref, row = (a, s) if r < 2 or s < half else (b, s - half)
            at = slice(s, s + n)
            gi[r, :, at] = (dot_nt(gffn[...], ref[row : row + n, :]) * udact[r, :, at].astype(F32)).astype(BF)
    total = dot_nt(gi[0], isrc[0][...]) + dot_nt(gi[1], isrc[1][...])
    for r, (x, y) in ((2, isrc[2:4]), (3, isrc[4:6])):
        for ref, q in ((x, ids[1]), (y, 1 - ids[1])):
            total = total + dot_nt(gi[r, :, pl.ds(pl.multiple_of(q * half, 128), half)], ref[...])
    back[...] = total
    acc[...] = jnp.zeros_like(acc)

    @pl.loop(0, back.shape[0] // CH)
    def _(i):
        rows = pl.ds(pl.multiple_of(i * CH, CH), CH)
        n = normed[rows, :]
        gf = grad_two[rows, :] + back[rows, :]
        acc[0] += fold(gf * n)
        acc[1] += fold(gf)
        e = gf * consts[FG : FG + 1, :]
        g = inv[rows, :1] * (e - mean(e) - n * mean(e * n))
        grad_one[rows, :] = g
        gat = consts[HGATE : HGATE + 1, :] * g
        acc[2] += fold(gat)
        acc[3] += fold(g * attn[rows, :])
        ga[rows, :] = gat.astype(BF)

    d = back.shape[1]
    v3 = [jnp.sum(acc[j], axis=0, keepdims=True) for j in range(4)]
    count = jnp.zeros((), F32)
    for j in range(blocks):
        real = jnp.sum(live[j : j + 1, :].astype(F32))
        count += jnp.clip(real - (ids[0] * quarter).astype(F32), 0.0, float(quarter))
    marks = mark(jnp.zeros((1, d), F32), jnp.sum(v2[4:5, :]), ids[3], ids[3] + ids[4])
    marks = mark(marks, count, ids[3] + 2 * ids[4], ids[3] + 3 * ids[4])
    lines = jnp.concatenate([v2[0:3, :], *v3[:3], v2[3:4, :] + v3[3], marks, jnp.zeros((8, d), F32)], axis=0).astype(BF)
    for r in range(4):
        gg = dot_nt(ga[...], packs[r][:c, :]) * head_rows(packs[r][c:, :].astype(F32), True, c)
        for b in range(blocks):
            piece = gg[b * quarter : (b + 1) * quarter, :].T.astype(BF)
            if r == 0:
                g0[b] = piece
            elif r == 1:
                g1[b] = piece
            else:
                gfar[r - 2, b] = piece
        part = dsend if r % 2 else dkeep
        part[r // 2, :c, :] = dot_tn(gated[r], ga[...]).astype(BF)
        part[r // 2, c:, :] = lines


def units_kernel(f0, f1, fx, fd, consts, win, hidden, udact):
    for r, f in enumerate((f0, f1, fx, fd)):
        rows = slice(r * f0.shape[0], (r + 1) * f0.shape[0])
        for s in range(0, win.shape[1], 256):
            at = slice(s, s + 256)
            z = dot(f[...], win[:, at]) + consts[INB : INB + 1, at]
            phi, e = gelu_parts(z)
            g = consts[UGATE : UGATE + 1, at]
            udact[rows, at] = (g * (phi + z * e * 0.3989422804014327)).astype(BF)
            hidden[rows, at] = (g * (z * phi)).astype(BF)


def slots(src, keep, send, first_bit, second_bit):
    n = keep.shape[1]
    for a in range(2):
        for b in range(2):
            j = (first_bit ^ a) * 2 + (second_bit ^ b)
            rows = src[pl.ds(pl.multiple_of(j * n, 16), n), :].astype(BF)
            if a == 0:
                keep[b] = rows
            else:
                send[b] = rows


def rows_dot(lefts, rights):
    total = dot_tn(lefts[0], rights[0])
    for left, right in zip(lefts[1:], rights[1:]):
        total = total + dot_tn(left, right)
    return total


def unit_grads(first, gffns, outer, hidden, udact, gi, acc):
    n = gffns[0].shape[0]
    for r, gffn in enumerate(gffns):
        rows, own = slice((first + r) * n, (first + r + 1) * n), slice(r * n, (r + 1) * n)
        for s in range(0, outer.shape[0], 256):
            at = slice(s, s + 256)
            gh = dot_nt(gffn[...], outer[at, :])
            g = (gh * udact[rows, at].astype(F32)).astype(BF)
            gi[own, at] = g
            acc[0, :, at] += fold(gh * hidden[rows, at].astype(F32))
            acc[1, :, at] += fold(g.astype(F32))


def near_grad_kernel(g0, g1, outer, hidden, udact, part, gi, acc):
    n = g0.shape[0]
    part[...] = rows_dot([hidden[:n, :], hidden[n : 2 * n, :]], [g0[...], g1[...]])
    acc[...] = jnp.zeros_like(acc)
    unit_grads(0, (g0, g1), outer, hidden, udact, gi, acc)


def outer_grad_kernel(ids, gx, gd, hidden, part, akeep, asend, big):
    n = gx.shape[0]
    big[...] = part[...] + rows_dot([hidden[2 * n : 3 * n, :], hidden[3 * n :, :]], [gx[...], gd[...]])
    slots(big, akeep, asend, ids[2], ids[1])


def inner_grad_kernel(ids, f0, f1, fx, fd, gx, gd, outer, hidden, udact, near, sums, bkeep, bsend, gi, big, acc):
    n = f0.shape[0]
    d = f0.shape[1]
    acc[...] = sums[...]
    unit_grads(2, (gx, gd), outer, hidden, udact, gi, acc)
    big[:d, :] = rows_dot([f0[...], f1[...], fx[...], fd[...]], [near[:n, :], near[n:, :], gi[:n, :], gi[n:, :]])
    big[d:, :] = jnp.zeros((big.shape[0] - d, big.shape[1]), F32)
    for j in range(2):
        big[d + j : d + j + 1, :] = jnp.sum(acc[j], axis=0, keepdims=True)
    slots(big, bkeep, bsend, ids[1], ids[2])


def attend_back_kernel(ids, g0, g1, gxr, gcr, e_ref, inv_ref, k_ref, v_ref, q_ref, kt, tok, wq, wk, wv, keep, send, wacc, cacc, dct, nat, low):
    b = pl.program_id(0)
    h = ids[0]
    c, d = wq.shape
    length = tok.shape[0]
    quarter = length // 4
    heads = c // HD

    @pl.when(b == 0)
    def _():
        wacc[...] = jnp.zeros_like(wacc)
        cacc[...] = jnp.zeros_like(cacc)

    for r, piece in enumerate((g0[0], g1[0], gxr[0, 0], gcr[1, 0])):
        dct[:, pl.ds(pl.multiple_of((h ^ r) * quarter, 128), quarter)] = piece
    dq, dk, dv = [], [], []
    for i in range(heads):
        part = slice(i * HD, (i + 1) * HD)
        inv = inv_ref[0, i : i + 1, :]
        dcp = dct[part, :].astype(F32) * inv
        dp = dot(v_ref[:, part], dcp.astype(BF))
        e = e_ref[0, i].astype(F32)
        w = e * dp
        delta = jnp.sum(w, axis=0, keepdims=True)
        ds = (w - e * (inv * delta)).astype(BF)
        dq.append(dot(kt[0, part, :], ds) * HD ** (-0.5))
        dk.append(dot(ds, q_ref[:, part]).astype(BF))
        dv.append(dot(e_ref[0, i], dcp.T.astype(BF)).astype(BF))
        cacc[8:9, i * 128 : (i + 1) * 128] += jnp.broadcast_to(jnp.sum(delta, axis=1, keepdims=True), (1, 128))
    dq = jnp.concatenate(dq, axis=0).T.astype(BF)
    nat[...] = jnp.concatenate([dq, *dk, *dv], axis=1)
    wacc[...] += dot_tn(nat[...], tok[...])
    cacc[0:8, : 3 * c] += fold(nat[...].astype(F32))
    part = dot(nat[:, :c], wq[...]) + dot(nat[:, c : 2 * c], wk[...]) + dot(nat[:, 2 * c :], wv[...])
    low[...] = part.astype(BF)
    for r in range(4):
        rows = low[pl.ds(pl.multiple_of((h ^ r) * quarter, quarter), quarter), :]
        at = pl.ds(pl.multiple_of(b * quarter, quarter), quarter)
        if r % 2 == 0:
            keep[r // 2, at, :] = rows
        else:
            send[r // 2, at, :] = rows


def turn_kernel(ids, wacc, cacc, dmine, drecv, ckeep, csend, big):
    n = wacc.shape[0]
    c = n // 3
    big[n + c + 32 :, :] = jnp.zeros((big.shape[0] - n - c - 32, big.shape[1]), F32)
    big[:n, :] = wacc[...]
    big[n : n + c + 16, :] = dmine[...].astype(F32) + drecv[...].astype(F32)
    n = n + c + 16
    big[n : n + 16, :] = jnp.zeros((16, big.shape[1]), F32)
    col = jnp.sum(cacc[0:8, :], axis=0, keepdims=True)
    big[n : n + 1, :c] = col[:, :c]
    big[n + 1 : n + 2, :c] = col[:, 2 * c : 3 * c]
    big[n + 2 : n + 3, : c * 2] = cacc[8:9, : c * 2]
    slots(big, ckeep, csend, ids[1], ids[2])


def third_kernel(ids, mine, got, error, error_1, out):
    n, d = mine.shape
    out[:n, :] = (mine[...].astype(F32) + got[...].astype(F32)).astype(BF)
    total = error[0:1, :1] + error_1[0:1, :1]
    place = ids[3] // 4
    zero = jnp.zeros((1, d), F32)
    rows = [mark(zero, total, place, -1), mark(zero, total, -1, place), jnp.zeros((14, d), F32)]
    out[n:, :] = jnp.concatenate(rows, axis=0).astype(BF)


def pair_kernel(mine, other, out):
    out[0], out[1] = mine[...], other[...]


def last_kernel(mine, other, out):
    n = mine.shape[0] - 16
    out[:n, :] = mine[:n, :]
    out[n : 2 * n, :] = other[:n, :]
    out[2 * n :, :] = (mine[n:, :].astype(F32) + other[n:, :].astype(F32)).astype(BF)


def place(ids, swap, k, o, q, dst):
    n = k.shape[0]
    one, two = (ids[2], ids[1]) if swap else (ids[1], ids[2])
    for a in range(2):
        for b in range(2):
            src = (k if b == 0 else o)[...] if a == 0 else q[b]
            dst[pl.ds(pl.multiple_of(((one ^ a) * 2 + (two ^ b)) * n, 16), n), :] = src.astype(F32)


def outer_out_kernel(ids, k, o, q, uw):
    place(ids, True, k, o, q, uw)


def inner_out_kernel(ids, consts, pair, q, live, iw, ib, ua, pe, big):
    n = big.shape[0] // 4
    for a, src in enumerate((pair, q)):
        for b in range(2):
            j = (ids[1] ^ a) * 2 + (ids[2] ^ b)
            big[pl.ds(pl.multiple_of(j * n, 16), n), :] = src[b * n : (b + 1) * n, :].astype(F32)
    d = iw.shape[0]
    iw[...] = big[:d, :]
    ua[...] = (1.5 * big[d : d + 1, :] * (1.0 - consts[UGATE : UGATE + 1, :])).reshape(d)
    ib[...] = big[d + 1 : d + 2, :].reshape(d)
    hard = jnp.sum(pair[2 * n :, :].astype(F32) + q[2 * n :, :].astype(F32))
    pe[0] = 0.5 * hard / live[0]


def final_kernel(ids, consts, ck, co, cq, qw, kw, vw, ow, qb, vb, ob, fg, fs, ub, sg, ss, ha, da, me, live_out, big):
    d = consts.shape[1]
    c = qw.shape[0]

    place(ids, False, ck, co, cq, big)
    qw[...] = big[:c, :]
    kw[...] = big[c : 2 * c, :]
    vw[...] = big[2 * c : 3 * c, :]
    n = 3 * c
    ow[...] = big[n : n + c, :]
    n = n + c
    vec = big[n : n + 16, :]
    own = big[n + 16 : n + 32, :]
    for ref, row in ((sg, 0), (ss, 1), (ub, 2), (fg, 3), (fs, 4), (ob, 5)):
        ref[...] = vec[row : row + 1, :].reshape(d)
    hg = consts[HGATE : HGATE + 1, :]
    da[...] = (1.5 * vec[6:7, :] * hg * (1.0 - hg)).reshape(d)
    qb[...] = own[0:1, :c].reshape(c)
    vb[...] = own[1:2, :c].reshape(c)
    gate = consts[HEADG : HEADG + 1, :]
    for i in range(c // HD):
        g = gate[0, i * HD]
        ha[i] = 1.5 * own[2, i * 128] * (1.0 - g)
    lane = lax.broadcasted_iota(jnp.int32, (1, d), 1)
    nd = ids[4]
    marks = vec[7:8, :]

    def between(lo, hi):
        return jnp.sum(jnp.where((lane >= lo * nd) & (lane < hi * nd), marks, 0.0))

    live = jnp.maximum(between(2, 4), 1.0)
    me[0] = 0.5 * between(0, 2) / live
    live_out[0] = live


def spread_kernel(h_ref, *refs):
    count = (len(refs) - 1) // 5
    sem = refs[-1]
    copies = []
    for a in range(count):
        out = refs[4 * count + a]
        for r in range(4):
            src = refs[4 * a + r]
            blocks = out.shape[0]
            quarter = out.shape[1] // 4
            for b in range(blocks):
                at = pl.ds(pl.multiple_of((h_ref[0] ^ r) * quarter, quarter), quarter)
                copies.append(pltpu.make_async_copy(src.at[pl.ds(b * quarter, quarter)], out.at[b, at], sem.at[len(copies)]))
    for copy in copies:
        copy.start()
    for copy in copies:
        copy.wait()


def shards(
    tokens, teacher, segments, present, query_weight, query_bias, key_weight, value_weight, value_bias, output_weight, output_bias,
    first_gain, first_shift, inner_weight, inner_bias, outer_weight, outer_bias, second_gain, second_shift, head_alpha, head_noise,
    unit_alpha, unit_noise, hidden_alpha, hidden_noise, head_keep, unit_keep, hidden_keep, n_dp,
):
    rows, d = tokens.shape
    blocks, length = segments.shape
    heads = head_alpha.shape[0]
    c = heads * HD
    w = unit_alpha.shape[0]
    quarter = length // 4
    t = blocks * quarter
    n_head = 4
    h = lax.axis_index("head").astype(jnp.int32)
    i_dp = lax.axis_index("dp").astype(jnp.int32)
    bit0, bit1 = i_dp & 1, (i_dp >> 1) & 1
    ids = jnp.stack([h, bit0, bit1, i_dp * n_head + h, jnp.int32(n_dp * n_head)])

    def hop(x, mask, axis="head"):
        size = n_head if axis == "head" else n_dp
        return lax.ppermute(x, axis, [(i, i ^ mask) for i in range(size)])

    def in_hbm(x):
        return pltpu.with_memory_space_constraint(x, pltpu.HBM)

    def after(x, *done):
        return lax.optimization_barrier((x, *done))[0]

    def add(x, y):
        return (x.astype(F32) + y.astype(F32)).astype(BF)

    half = d // 2
    inner_half = lax.dynamic_slice_in_dim(inner_weight, bit0 * half, half, axis=1)
    inner_x = hop(inner_half, 2)

    small = (unit_alpha, unit_noise, unit_keep, inner_bias, hidden_alpha, hidden_noise, hidden_keep, output_bias, first_gain, first_shift,
             outer_bias, second_gain, second_shift, query_bias, value_bias, head_alpha, head_noise, head_keep)
    consts, pack = call(
        prep_kernel,
        [((16, d), F32), ((c + VEC, w), BF)],
        tuple(in_hbm(a) for a in (*small, after(output_weight, inner_half))),
        specs=[ANY] * 19, scratch=[(pltpu.VMEM if a.shape[0] > heads else pltpu.SMEM)(a.shape, a.dtype) for a in small] + [pltpu.SemaphoreType.DMA((19,))], us=2, limit=4, name="prep",
    )
    pack_2 = hop(pack, 2)
    pack_1 = hop(pack, 1)
    inner_1, outer_1 = hop(inner_weight, 1), hop(outer_weight, 1)

    seg3 = segments.reshape(blocks, 1, length)
    live3 = present.reshape(blocks, 1, length)
    full = lambda *s: pl.BlockSpec(s, lambda b, *_: (0,) * len(s))
    c0, c1, cfar, e, inv_l, k, v, q, qst, kt = call(
        attend_kernel,
        [((blocks, c, quarter), BF), ((blocks, c, quarter), BF), ((2, blocks, c, quarter), BF), ((blocks, heads, length, length), BF, HBM),
         ((blocks, 8, length), F32), ((rows, c), BF, HBM), ((rows, c), BF, HBM), ((rows, c), BF, HBM), ((blocks, c, length), BF, HBM), ((blocks, c, length), BF, HBM)],
        (ids, in_hbm(tokens), *(in_hbm(a.T) for a in (query_weight, key_weight, value_weight)), consts, seg3, live3),
        prefetch=1, grid=(blocks,),
        specs=[pl.BlockSpec((length, d), lambda b, *_: (b, 0)), full(c, d), full(c, d), full(c, d), full(16, d),
               pl.BlockSpec((1, 1, length), lambda b, *_: (b, 0, 0)), pl.BlockSpec((1, 1, length), lambda b, *_: (b, 0, 0))],
        out_specs=[pl.BlockSpec((1, c, quarter), lambda b, *_: (b, 0, 0)), pl.BlockSpec((1, c, quarter), lambda b, *_: (b, 0, 0)),
                   pl.BlockSpec((2, 1, c, quarter), lambda b, *_: (0, b, 0, 0)), pl.BlockSpec((1, heads, length, length), lambda b, *_: (b, 0, 0, 0)),
                   pl.BlockSpec((1, 8, length), lambda b, *_: (b, 0, 0)), pl.BlockSpec((length, c), lambda b, *_: (b, 0)),
                   pl.BlockSpec((length, c), lambda b, *_: (b, 0)), pl.BlockSpec((length, c), lambda b, *_: (b, 0)),
                   pl.BlockSpec((1, c, length), lambda b, *_: (b, 0, 0)), pl.BlockSpec((1, c, length), lambda b, *_: (b, 0, 0))],
        scratch=[pltpu.VMEM((length, length), F32), pltpu.VMEM((c, length), BF)], us=9, limit=16, name="attend",
    )
    cx = hop(cfar, 2)
    c1r = hop(c1, 1)
    outer_late = after(outer_weight, c1r)
    outer_a = hop(outer_late[:half], 2)
    outer_b = hop(outer_late[half:], 2)
    inner_x, pack_2 = after(inner_x, c0), after(pack_2, c0)
    inner_y, inner_3x = hop(inner_x, 1, "dp"), hop(inner_x, 1)
    packs = (pack, pack_1, pack_2, hop(pack_2, 1))
    pieces = (c0, c1r, cx, hop(cx, 1))

    def first(soft, pieces):
        scratch = [pltpu.VMEM((t, d), BF), pltpu.SemaphoreType.DMA((blocks,))]
        more = [((t, 128), F32), ((t, d), F32), ((4, t, c), BF)]
        return call(
            partial(first_kernel, soft),
            [((t, d), BF), ((t, d), F32)] + (more if soft else []),
            (ids, *pieces, *packs, tokens, consts),
            prefetch=1, specs=[VM] * 8 + [ANY, VM],
            scratch=scratch if soft else scratch + [pltpu.VMEM((t, d), F32), pltpu.VMEM((4, t, c), BF)], us=4, limit=8, name="first" if soft else "hard_first",
        )

    def inner(soft, low):
        return call(
            partial(inner_kernel, soft), [((4, t, w), BF)] * (2 if soft else 1), (ids, low, *inners, *packs),
            prefetch=1, us=8, limit=8, name="inner" if soft else "hard_inner",
        )

    first_low, normed, inv1, attn, gated = first(True, pieces)
    first_2 = hop(first_low, 2)
    first_1 = hop(first_low, 1)
    inner_y = after(inner_y, first_low)
    inners = (inner_weight, inner_1, inner_x, inner_y, inner_3x, hop(inner_y, 1))
    hard_low, hard_normed = first(False, (after(c0, first_low), *pieces[1:]))
    outer_a = after(outer_a, hard_low)
    outer_3a = hop(outer_a, 1)
    hidden, udact = inner(True, after(first_low, hard_low))
    (hard_hidden,) = inner(False, after(hard_low, hidden))
    outer_b = after(outer_b, hard_hidden)
    outers = (outer_weight, outer_1, outer_a, outer_b, outer_3a, hop(outer_b, 1))

    student_rows, grad_two, gffn, v2 = call(
        second_kernel,
        [((t, d), BF), ((t, d), F32), ((t, d), BF), ((8, d), F32)],
        (ids, hidden, normed, *outers, teacher, present, consts),
        prefetch=1, specs=[VM] * 8 + [ANY] + [VM] * 2,
        scratch=[pltpu.VMEM((t, d), BF), pltpu.VMEM((t, d), F32), pltpu.VMEM((5, 8, d), F32), pltpu.SemaphoreType.DMA((blocks,))], us=6, limit=8, name="second",
    )
    gffn_1 = hop(gffn, 1)

    g0, g1, gfar, dkeep, dsend, grad_one = call(
        back_kernel,
        [((blocks, c, quarter), BF), ((blocks, c, quarter), BF), ((2, blocks, c, quarter), BF), ((2, c + 16, d), BF), ((2, c + 16, d), BF), ((t, d), F32)],
        (ids, gffn, udact, *inners, *outers, *packs, grad_two, normed, inv1, attn, gated, v2, present, consts),
        prefetch=1,
        scratch=[pltpu.VMEM((4, t, w), BF), pltpu.VMEM((t, d), F32), pltpu.VMEM((t, d), BF), pltpu.VMEM((4, 8, d), F32)], us=13, limit=12, name="back",
    )
    gx = hop(gfar, 2)
    g1r = hop(g1, 1)
    d_got = hop(dsend, 1)
    first_2 = after(first_2, g0)
    firsts = (first_low, first_1, first_2, hop(first_2, 1))
    hidden_own, udact_own = call(
        units_kernel, [((rows, w), BF), ((rows, w), BF)], (after(firsts[0], g0), *firsts[1:], consts, inner_weight), us=6, limit=8, name="units"
    )
    gx, d_got = after(gx, hidden_own), after(d_got, hidden_own)
    gpieces = (g0, g1r, gx, hop(gx, 1))
    d_mine, d_give = add(dkeep[0], d_got[0]), add(dkeep[1], d_got[1])
    d_recv = hop(d_give, 2)
    gffn_2 = hop(after(gffn, d_give, gx), 2)
    pick = lambda *s: pl.BlockSpec((1,) + s, lambda b, *_: (b,) + (0,) * len(s))
    keep, send, wacc, cacc = call(
        attend_back_kernel,
        [((2, t, d), BF), ((2, t, d), BF), ((3 * c, d), F32), ((16, d), F32)],
        (ids, *gpieces, *(in_hbm(a) for a in (e, inv_l, k, v, q, kt, tokens)), *(in_hbm(a.T) for a in (query_weight, key_weight, value_weight))),
        prefetch=1, grid=(blocks,),
        specs=[pick(c, quarter), pick(c, quarter), pl.BlockSpec((2, 1, c, quarter), lambda b, *_: (0, b, 0, 0)),
               pl.BlockSpec((2, 1, c, quarter), lambda b, *_: (0, b, 0, 0)), pick(heads, length, length), pick(8, length),
               pl.BlockSpec((length, c), lambda b, *_: (b, 0)), pl.BlockSpec((length, c), lambda b, *_: (b, 0)), pl.BlockSpec((length, c), lambda b, *_: (b, 0)), pick(c, length),
               pl.BlockSpec((length, d), lambda b, *_: (b, 0)), full(c, d), full(c, d), full(c, d)],
        out_specs=[full(2, t, d), full(2, t, d), full(3 * c, d), full(16, d)],
        scratch=[pltpu.VMEM((c, length), BF), pltpu.VMEM((length, 3 * c), BF), pltpu.VMEM((length, d), BF)],
        us=15, limit=20, name="attend_back",
    )
    gffn_2 = after(gffn_2, keep)
    n_c = 4 * ((3 * c + c + 32 + 63) // 64) * 16
    ckeep, csend = call(
        turn_kernel, [((2, n_c // 4, d), BF)] * 2, (ids, wacc, cacc, d_mine, after(d_recv, keep, gffn_2)), prefetch=1, specs=[VM] * 4,
        scratch=[pltpu.VMEM((n_c, d), F32)], us=1, limit=8, name="turn",
    )
    got = hop(after(send, ckeep), 1)
    c_got = hop(csend, 1, "dp")
    gffn_2 = after(gffn_2, ckeep)
    gffn_3 = hop(gffn_2, 1)
    part, near, sums = call(
        near_grad_kernel, [((w, d), F32), ((2 * t, w), BF), ((2, 8, w), F32)], (after(gffn, gffn_2), gffn_1, outer_weight, hidden_own, udact_own),
        us=5, limit=8, name="near_grad",
    )
    got = after(got, near)
    mine, give = add(keep[0], got[0]), add(keep[1], got[1])
    recv = hop(give, 2)
    akeep, asend = call(
        outer_grad_kernel, [((2, w // 4, d), BF)] * 2, (ids, after(gffn_2, give), gffn_3, hidden_own, part), prefetch=1, scratch=[pltpu.VMEM((w, d), F32)],
        us=2, limit=8, name="outer_grad",
    )
    a_got = hop(asend, 2, "dp")
    n_b = d + 64
    bkeep, bsend = call(
        inner_grad_kernel, [((2, n_b // 4, w), BF)] * 2,
        (ids, *firsts, after(gffn_2, akeep), gffn_3, outer_weight, hidden_own, udact_own, near, sums), prefetch=1,
        scratch=[pltpu.VMEM((2 * t, w), BF), pltpu.VMEM((n_b, w), F32), pltpu.VMEM((2, 8, w), F32)], us=4, limit=12, name="inner_grad",
    )
    b_got = hop(bsend, 1, "dp")

    def across(x):
        mask = 4
        while mask < n_dp:
            got = hop(x, mask, "dp")
            x = (x, got) if mask * 2 == n_dp else add(x, got)
            mask *= 2
        return x

    def split(keep, got):
        return add(keep[0], got[0]), add(keep[1], got[1])

    c_mine, c_give = split(ckeep, after(c_got, bkeep))
    c_got = hop(c_give, 2, "dp")
    pruned_rows, error = call(
        hard_kernel,
        [((t, d), BF), ((8, 128), F32)],
        (ids, after(hard_hidden, c_give), hard_normed, *outers, teacher, present, consts),
        prefetch=1, specs=[VM] * 8 + [ANY] + [VM] * 2,
        scratch=[pltpu.VMEM((t, d), BF), pltpu.VMEM((t, d), F32), pltpu.VMEM((8, d), F32), pltpu.SemaphoreType.DMA((blocks,))], us=0.1, limit=8, name="hard",
    )

    recv = after(recv, pruned_rows)
    grad_rows = (grad_one + (mine.astype(F32) + recv.astype(F32))).astype(BF)
    grad_2 = hop(grad_rows, 2)
    grad_1 = hop(grad_rows, 1)
    a_mine, a_give = split(akeep, after(a_got, grad_rows))
    a_got = hop(a_give, 1, "dp")
    b_mine, b_give = split(bkeep, after(b_got, a_give))
    b_got = hop(b_give, 2, "dp")
    pruned_rows = after(pruned_rows, b_give)
    pruned_2 = hop(pruned_rows, 2)
    pruned_1 = hop(pruned_rows, 1)
    c_mine = across(add(c_mine, after(c_got, b_give)))
    error = after(error, b_give)
    error = error + hop(error, 2)
    error_1 = hop(error, 1)
    a_mine = across(add(a_mine, after(a_got, c_mine[0])))
    (b_mine,) = call(
        third_kernel, [((n_b // 4 + 16, d), BF)], (ids, b_mine, after(b_got, a_mine[0]), error, error_1), prefetch=1, us=0.1, limit=4, name="third"
    )
    c_mine = add(c_mine[0], after(c_mine[1], b_mine))
    b_mine = across(b_mine)
    c_other = hop(c_mine, 2, "dp")
    grad_2 = after(grad_2, c_mine)
    grads = (grad_rows, grad_1, grad_2, hop(grad_2, 1))
    student_rows = after(student_rows, grad_2)
    student_2 = hop(student_rows, 2)
    student_1 = hop(student_rows, 1)
    a_mine = add(a_mine[0], after(a_mine[1], grad_2))
    a_other = hop(a_mine, 1, "dp")
    (c_pair,) = call(pair_kernel, [((2,) + c_mine.shape, BF)], (c_mine, after(c_other, a_mine)), us=0.1, limit=4, name="pair3")
    c_last = hop(c_pair, 1, "dp")
    b_mine = add(b_mine[0], after(b_mine[1], c_pair))
    b_other = hop(b_mine, 2, "dp")
    (a_pair,) = call(pair_kernel, [((2,) + a_mine.shape, BF)], (a_mine, after(a_other, b_mine)), us=0.1, limit=4, name="pair")
    a_last = hop(a_pair, 2, "dp")
    pruned_2, student_2 = after(pruned_2, a_pair), after(student_2, a_pair)
    pruneds = (pruned_rows, pruned_1, pruned_2, hop(pruned_2, 1))
    students = (student_rows, student_1, student_2, hop(student_2, 1))
    (b_pair,) = call(last_kernel, [((n_b // 2 + 16, d), BF)], (b_mine, after(b_other, student_2, pruned_2, c_last)), us=0.1, limit=4, name="last")
    b_last = hop(b_pair, 1, "dp")
    outs = call(
        spread_kernel,
        [((blocks, length, d), BF)] * 3,
        (ids, after(students[0], b_pair), *students[1:], *pruneds, *grads),
        prefetch=1, specs=[VM] * 12, out_specs=[ANY] * 3, scratch=[pltpu.SemaphoreType.DMA((12 * blocks,))], us=0.1, limit=4, name="spread",
    )
    student, pruned, tokens_grad = (o.reshape(rows, d) for o in outs)
    qw, kw, vw, ow, qb, vb, ob, fg, fs, ub, sg, ss, ha, da, me, live = call(
        final_kernel,
        [((c, d), F32), ((c, d), F32), ((c, d), F32), ((c, d), F32), ((c,), F32), ((c,), F32), ((d,), F32), ((d,), F32), ((d,), F32),
         ((d,), F32), ((d,), F32), ((d,), F32), ((heads,), F32), ((d,), F32), ((1,), F32), ((1,), F32)],
        (ids, consts, c_mine, c_other, after(c_last, outs[0])),
        prefetch=1, specs=[VM] * 4, out_specs=[VM] * 12 + [SM] + [VM] + [SM] * 2,
        scratch=[pltpu.VMEM((n_c, d), F32)], us=0.1, limit=8, name="final",
    )
    (uw,) = call(outer_out_kernel, [((w, d), F32)], (ids, a_mine, a_other, after(a_last, qw)), prefetch=1, us=0.1, limit=8, name="outer_out")
    iw, ib, ua, pe = call(
        inner_out_kernel, [((d, w), F32), ((w,), F32), ((w,), F32), ((1,), F32)], (ids, consts, b_pair, after(b_last, uw), live), prefetch=1,
        specs=[VM] * 3 + [SM], out_specs=[VM] * 3 + [SM], scratch=[pltpu.VMEM((n_b, w), F32)], us=0.1, limit=12, name="inner_out",
    )
    return (
        student, pruned, tokens_grad, qw.T, qb, kw.T, vw.T, vb, ow, ob, fg, fs, iw, ib, uw, ub, sg, ss, ha, ua, da, me.reshape(()), pe.reshape(()),
    )


def solution(mesh):
    row, col, lead, unit, none = P("dp", None), P(None, "head"), P("head", None), P("head"), P()
    return jax.shard_map(
        partial(shards, n_dp=mesh.shape["dp"]),
        mesh=mesh,
        in_specs=(row, row, row, row, col, unit, col, col, unit, lead, none, none, none, col, unit, lead, none, none, none) + (unit,) * 4 + (none,) * 2 + (unit,) * 2 + (none,),
        out_specs=(row, row, row, col, unit, col, col, unit, lead, none, none, none, col, unit, lead, none, none, none, unit, unit, none, none, none),
        check_vma=False,
    )
```

```python
from functools import partial

import jax
import jax.numpy as jnp
from jax import lax
from jax.experimental import pallas as pl
from jax.experimental.pallas import tpu as pltpu
from jax.sharding import PartitionSpec as P

F32 = jnp.float32
BF = jnp.bfloat16
HD = 64
EPS = 1e-05
VEC = 32
CH = 128
MB = 1024 * 1024
COST = 5e8

HGATE, HKEEP, OUTB, FG, FS, OUTERB, SG, SS, UGATE, INB, HEADG, QB, VB = range(13)


def dot(a, b):
    return jnp.dot(a, b, preferred_element_type=F32)


def dot_nt(a, b):
    return lax.dot_general(a, b, (((1,), (1,)), ((), ())), preferred_element_type=F32)


def dot_tn(a, b):
    return lax.dot_general(a, b, (((0,), (0,)), ((), ())), preferred_element_type=F32)


def gelu_parts(v):
    z = jnp.abs(v) * 0.7071067811865476
    e = jnp.exp(-(z * z))
    t = 1.0 / (1.0 + 0.3275911 * z)
    p = 0.5 * 1.061405429
    p = p * t - 0.5 * 1.453152027
    p = p * t + 0.5 * 1.421413741
    p = p * t - 0.5 * 0.284496736
    p = p * t + 0.5 * 0.254829592
    q = p * t * e
    return jnp.where(v >= 0.0, 1.0 - q, q), e


def fold(x):
    return jnp.sum(x.reshape(x.shape[0] // 8, 8, x.shape[1]), axis=0)


def mean(x):
    return jnp.mean(x, axis=1, keepdims=True)


def call(kernel, outs, args, specs=None, scratch=(), grid=(), prefetch=0, out_specs=None, us=1.0, limit=40, name=None):
    vmem = pl.BlockSpec(memory_space=pltpu.VMEM)
    specs = specs or [vmem] * (len(args) - prefetch)
    out_specs = out_specs or [vmem] * len(outs)
    return pl.pallas_call(
        kernel,
        out_shape=[pltpu.HBM(*o[:2]) if len(o) > 2 else jax.ShapeDtypeStruct(*o) for o in outs],
        grid_spec=pltpu.PrefetchScalarGridSpec(
            num_scalar_prefetch=prefetch, grid=grid, in_specs=specs, out_specs=out_specs, scratch_shapes=list(scratch)
        ),
        compiler_params=pltpu.CompilerParams(vmem_limit_bytes=limit * MB),
        cost_estimate=pl.CostEstimate(flops=int(us * COST), bytes_accessed=0, transcendentals=0),
        name=name,
    )(*args)


VM = pl.BlockSpec(memory_space=pltpu.VMEM)
SM = pl.BlockSpec(memory_space=pltpu.SMEM)
ANY = pl.BlockSpec(memory_space=pl.ANY)
HBM = pl.BlockSpec(memory_space=pltpu.HBM)


def prep_kernel(*refs):
    count = (len(refs) - 3) // 2
    srcs, wo, consts, pack, held, sem = refs[:count], refs[count], refs[count + 1], refs[count + 2], refs[count + 3 : -1], refs[-1]
    w = consts.shape[1]
    c = wo.shape[0]
    copies = [pltpu.make_async_copy(a, b, sem.at[i]) for i, (a, b) in enumerate(zip(srcs, held))]
    copies.append(pltpu.make_async_copy(wo, pack.at[pl.ds(0, c)], sem.at[count]))
    for copy in copies:
        copy.start()
    for copy in copies:
        copy.wait()
    ua, un, uk, ib, da, dn, dk, ob, fg, fs, ub, sg, ss, qb, vb, ha, hn, hk = held

    def line(ref):
        return ref[...].astype(F32).reshape(1, ref.shape[0])

    def gate(a, n):
        return jax.nn.sigmoid((a + n) * 1.5)

    consts[...] = jnp.zeros_like(consts)
    consts[HGATE : HGATE + 1, :] = gate(line(da), line(dn))
    for row, ref in ((HKEEP, dk), (OUTB, ob), (FG, fg), (FS, fs), (OUTERB, ub), (SG, sg), (SS, ss), (INB, ib)):
        consts[row : row + 1, :] = line(ref)
    ugate = gate(line(ua), line(un))
    consts[UGATE : UGATE + 1, :] = ugate
    consts[QB : QB + 1, :c] = line(qb)
    consts[VB : VB + 1, :c] = line(vb)
    lane = lax.broadcasted_iota(jnp.int32, (1, w), 1)
    logit = jnp.zeros((1, w), F32)
    keep = jnp.zeros((1, w), F32)
    for i in range(c // HD):
        here = (lane >= i * HD) & (lane < (i + 1) * HD)
        logit = jnp.where(here, ha[i] + hn[i], logit)
        keep = jnp.where(here, hk[i].astype(F32), keep)
    hgate = jax.nn.sigmoid(logit * 1.5)
    consts[HEADG : HEADG + 1, :] = hgate

    def halves(x):
        high = x.astype(BF).astype(F32)
        return high, x - high

    uh, ul = halves(ugate)
    hh, hl = halves(hgate)
    rows = [uh, ul, line(uk), line(ib), hh, hl, keep] + [jnp.zeros((1, w), F32)] * (VEC - 7)
    pack[c:, :] = jnp.concatenate(rows, axis=0).astype(BF)


def attend_kernel(ids, tok, wq, wk, wv, consts, seg, live, c0, c1, cfar, e_ref, inv_ref, k_ref, v_ref, q_ref, qst_ref, kt_ref, bias, ct):
    c = wq.shape[0]
    length = tok.shape[0]
    quarter = length // 4
    x = tok[...]
    q = ((dot_nt(x, wq[...]) + consts[QB : QB + 1, :c]).astype(BF).astype(F32) * HD ** (-0.5)).astype(BF)
    k = dot_nt(x, wk[...]).astype(BF)
    v = (dot_nt(x, wv[...]) + consts[VB : VB + 1, :c]).astype(BF)
    k_ref[...] = k
    v_ref[...] = v
    q_ref[...] = q
    qst = q.astype(F32).T.astype(BF)
    qst_ref[0] = qst
    kt_ref[0] = k.astype(F32).T.astype(BF)
    vt = v.astype(F32).T.astype(BF)
    seg_row = seg[0].astype(F32)
    code = jnp.where(live[0] == 1, seg_row, -1.0)
    code_col = jnp.broadcast_to(code, (128, length)).T[:, :1]
    row = lax.broadcasted_iota(jnp.int32, (length, length), 0)
    col = lax.broadcasted_iota(jnp.int32, (length, length), 1)
    bias[...] = jnp.where((code_col == seg_row) | (row == col), 0.0, -1e30)
    h = ids[0]
    inv_ref[...] = jnp.zeros_like(inv_ref)
    for i in range(c // HD):
        part = slice(i * HD, (i + 1) * HD)
        s = dot(k[:, part], qst[part, :]) + bias[...]
        top = jnp.max(s, axis=0, keepdims=True)
        e = jnp.exp(s - top)
        inv = 1.0 / jnp.sum(e, axis=0, keepdims=True)
        low = e.astype(BF)
        e_ref[0, i] = low
        inv_ref[0, i : i + 1, :] = inv
        ct[part, :] = (dot(vt[part, :], low) * inv).astype(BF)
    for r in range(4):
        piece = ct[:, pl.ds(pl.multiple_of((h ^ r) * quarter, 128), quarter)]
        if r < 2:
            (c0, c1)[r][0] = piece
        else:
            cfar[r - 2, 0] = piece


def mark(marks, value, first, second):
    lane = lax.broadcasted_iota(jnp.int32, marks.shape, 1)
    full = jnp.broadcast_to(value, marks.shape)
    high = full.astype(BF).astype(F32)
    return jnp.where(lane == first, high, jnp.where(lane == second, full - high, marks))


def unit_chunks(weights, p):
    half = weights[2].shape[1]
    chunks = []
    for r in range(2):
        chunks += [(r, weights[r], s, 256, s) for s in range(0, weights[r].shape[1], 256)]
    for r, (mine, other) in ((2, weights[2:4]), (3, weights[4:6])):
        for ref, base in ((mine, p * half), (other, (1 - p) * half)):
            for s in range(0, half, 256):
                chunks.append((r, ref, s, min(256, half - s), pl.multiple_of(base + s, 128)))
    return chunks


def start(copies):
    for copy in copies:
        copy.start()


def wait(copies):
    for copy in copies:
        copy.wait()


def load_rows(src, dst, h, sem, blocks, quarter):
    return [
        pltpu.make_async_copy(src.at[pl.ds(b * 4 * quarter + pl.multiple_of(h * quarter, quarter), quarter)], dst.at[pl.ds(b * quarter, quarter)], sem.at[b])
        for b in range(blocks)
    ]


def head_rows(vec, soft, c):
    if soft:
        return (vec[4:5, :] + vec[5:6, :])[:, :c]
    return vec[6:7, :][:, :c]


def project(pieces, packs, gated, attn, consts, soft):
    blocks, c, quarter = pieces[0].shape
    for r in range(4):
        g = head_rows(packs[r][c:, :].astype(F32), soft, c)
        for b in range(blocks):
            gated[r, b * quarter : (b + 1) * quarter, :] = (pieces[r][b].astype(F32).T * g).astype(BF)
    total = dot(gated[0], packs[0][:c, :])
    for r in range(1, 4):
        total = total + dot(gated[r], packs[r][:c, :])
    attn[...] = total + consts[OUTB : OUTB + 1, :]


def first_kernel(soft, ids, c0, c1, xr, cr, s0, s1, s2, s3, tok_any, consts, first_low, normed, *refs):
    if soft:
        inv, attn, gated, tok, tsem = refs
    else:
        tok, tsem, attn, gated = refs
    blocks, c, quarter = c0.shape
    loads = load_rows(tok_any, tok, ids[0], tsem, blocks, quarter)
    start(loads)
    project([c0, c1, xr.at[0], cr.at[1]], [s0, s1, s2, s3], gated, attn, consts, soft)
    wait(loads)
    gate = HGATE if soft else HKEEP

    @pl.loop(0, tok.shape[0] // CH)
    def _(i):
        rows = pl.ds(pl.multiple_of(i * CH, CH), CH)
        x = tok[rows, :].astype(F32) + consts[gate : gate + 1, :] * attn[rows, :]
        x = x - mean(x)
        iv = lax.rsqrt(mean(x * x) + EPS)
        n = x * iv
        normed[rows, :] = n
        if soft:
            inv[rows, :] = jnp.broadcast_to(iv, (CH, 128))
        first_low[rows, :] = (n * consts[FG : FG + 1, :] + consts[FS : FS + 1, :]).astype(BF)


def ffn_inner(first, wins, packs, p, hidden, soft, udact=None):
    c = packs[0].shape[0] - VEC
    for r, ref, s, n, unit in unit_chunks(wins, p):
        at = pl.ds(unit, n)
        vec = packs[r][c : c + 16, at].astype(F32)
        z = dot(first[...], ref[:, s : s + n]) + vec[3:4, :]
        phi, e = gelu_parts(z)
        if soft:
            g = vec[0:1, :] + vec[1:2, :]
            udact[r, :, at] = (g * (phi + z * e * 0.3989422804014327)).astype(BF)
        else:
            g = vec[2:3, :]
        hidden[r, :, at] = (g * (z * phi)).astype(BF)


def ffn_outer(hidden, outers, ffn, consts):
    half = outers[2].shape[0]
    total = dot(hidden[0], outers[0][...]) + dot(hidden[1], outers[1][...])
    for r, (a, b) in ((2, outers[2:4]), (3, outers[4:6])):
        total = total + dot(hidden[r, :, :half], a[...]) + dot(hidden[r, :, half:], b[...])
    ffn[...] = total + consts[OUTERB : OUTERB + 1, :]


def row_mask(live, h, b, quarter, at):
    count = jnp.sum(live[b : b + 1, :].astype(F32))
    place = (h * quarter + at).astype(F32) + lax.broadcasted_iota(jnp.int32, (CH, 1), 0).astype(F32)
    return jnp.where(place < count, 1.0, 0.0)


def inner_kernel(soft, ids, first_low, *refs):
    ffn_inner(first_low, refs[:6], refs[6:10], ids[1], refs[10], soft, refs[11] if soft else None)


def second_kernel(ids, hidden, normed, *refs):
    wsrc, teach_any, live, consts, student, grad_two, gffn, vecs_out, teach, ffn, acc, tsem = refs[:6], *refs[6:]
    blocks, length = live.shape
    quarter = length // 4
    h = ids[0]
    rowload = load_rows(teach_any, teach, h, tsem, blocks, quarter)
    start(rowload)
    ffn_outer(hidden, wsrc, ffn, consts)
    wait(rowload)
    acc[...] = jnp.zeros_like(acc)
    for b in range(blocks):

        @pl.loop(0, quarter // CH)
        def _(i):
            rows = pl.ds(pl.multiple_of(b * quarter + i * CH, CH), CH)
            f = ffn[rows, :]
            hg = consts[HGATE : HGATE + 1, :]
            x = normed[rows, :] * consts[FG : FG + 1, :] + consts[FS : FS + 1, :] + hg * f
            x = x - mean(x)
            iv = lax.rsqrt(mean(x * x) + EPS)
            n = x * iv
            out = n * consts[SG : SG + 1, :] + consts[SS : SS + 1, :]
            student[rows, :] = out.astype(BF)
            err = (out - teach[rows, :].astype(F32)) * row_mask(live, h, b, quarter, i * CH)
            acc[0] += fold(err * n)
            acc[1] += fold(err)
            acc[4] += fold(err * err)
            e = err * consts[SG : SG + 1, :]
            g = iv * (e - mean(e) - n * mean(e * n))
            grad_two[rows, :] = g
            gf = hg * g
            acc[2] += fold(gf)
            acc[3] += fold(g * f)
            gffn[rows, :] = gf.astype(BF)

    vecs_out[...] = jnp.zeros_like(vecs_out)
    for j in range(5):
        vecs_out[j : j + 1, :] = jnp.sum(acc[j], axis=0, keepdims=True)


def hard_kernel(ids, hidden, normed, *refs):
    wsrc, teach_any, live, consts, pruned, error, teach, ffn, acc, tsem = refs[:6], *refs[6:]
    blocks, length = live.shape
    quarter = length // 4
    h = ids[0]
    rowload = load_rows(teach_any, teach, h, tsem, blocks, quarter)
    start(rowload)
    ffn_outer(hidden, wsrc, ffn, consts)
    wait(rowload)
    acc[...] = jnp.zeros_like(acc)
    for b in range(blocks):

        @pl.loop(0, quarter // CH)
        def _(i):
            rows = pl.ds(pl.multiple_of(b * quarter + i * CH, CH), CH)
            x = normed[rows, :] * consts[FG : FG + 1, :] + consts[FS : FS + 1, :] + consts[HKEEP : HKEEP + 1, :] * ffn[rows, :]
            x = x - mean(x)
            n = x * lax.rsqrt(mean(x * x) + EPS)
            out = n * consts[SG : SG + 1, :] + consts[SS : SS + 1, :]
            pruned[rows, :] = out.astype(BF)
            err = (out - teach[rows, :].astype(F32)) * row_mask(live, h, b, quarter, i * CH)
            acc[...] += fold(err * err)

    error[...] = jnp.broadcast_to(jnp.sum(acc[...]), error.shape)


def back_kernel(ids, gffn, udact, *refs):
    isrc, osrc, packs = refs[:6], refs[6:12], refs[12:16]
    grad_two, normed, inv, attn, gated, v2, live, consts, g0, g1, gfar, dkeep, dsend, grad_one, gi, back, ga, acc = refs[16:]
    c = packs[0].shape[0] - VEC
    w = gi.shape[2]
    half = w // 2
    blocks, _, quarter = g0.shape
    for r, (a, b) in ((0, osrc[:1] * 2), (1, osrc[1:2] * 2), (2, osrc[2:4]), (3, osrc[4:6])):
        for s in (0, 256, 512) if r < 2 else (0, 256, half, half + 256):
            n = 256 if r < 2 or s % half == 0 else half - 256
            ref, row = (a, s) if r < 2 or s < half else (b, s - half)
            at = slice(s, s + n)
            gi[r, :, at] = (dot_nt(gffn[...], ref[row : row + n, :]) * udact[r, :, at].astype(F32)).astype(BF)
    total = dot_nt(gi[0], isrc[0][...]) + dot_nt(gi[1], isrc[1][...])
    for r, (x, y) in ((2, isrc[2:4]), (3, isrc[4:6])):
        for ref, q in ((x, ids[1]), (y, 1 - ids[1])):
            total = total + dot_nt(gi[r, :, pl.ds(pl.multiple_of(q * half, 128), half)], ref[...])
    back[...] = total
    acc[...] = jnp.zeros_like(acc)

    @pl.loop(0, back.shape[0] // CH)
    def _(i):
        rows = pl.ds(pl.multiple_of(i * CH, CH), CH)
        n = normed[rows, :]
        gf = grad_two[rows, :] + back[rows, :]
        acc[0] += fold(gf * n)
        acc[1] += fold(gf)
        e = gf * consts[FG : FG + 1, :]
        g = inv[rows, :1] * (e - mean(e) - n * mean(e * n))
        grad_one[rows, :] = g
        gat = consts[HGATE : HGATE + 1, :] * g
        acc[2] += fold(gat)
        acc[3] += fold(g * attn[rows, :])
        ga[rows, :] = gat.astype(BF)

    d = back.shape[1]
    v3 = [jnp.sum(acc[j], axis=0, keepdims=True) for j in range(4)]
    count = jnp.zeros((), F32)
    for j in range(blocks):
        real = jnp.sum(live[j : j + 1, :].astype(F32))
        count += jnp.clip(real - (ids[0] * quarter).astype(F32), 0.0, float(quarter))
    marks = mark(jnp.zeros((1, d), F32), jnp.sum(v2[4:5, :]), ids[3], ids[3] + ids[4])
    marks = mark(marks, count, ids[3] + 2 * ids[4], ids[3] + 3 * ids[4])
    lines = jnp.concatenate([v2[0:3, :], *v3[:3], v2[3:4, :] + v3[3], marks, jnp.zeros((8, d), F32)], axis=0).astype(BF)
    for r in range(4):
        gg = dot_nt(ga[...], packs[r][:c, :]) * head_rows(packs[r][c:, :].astype(F32), True, c)
        for b in range(blocks):
            piece = gg[b * quarter : (b + 1) * quarter, :].T.astype(BF)
            if r == 0:
                g0[b] = piece
            elif r == 1:
                g1[b] = piece
            else:
                gfar[r - 2, b] = piece
        part = dsend if r % 2 else dkeep
        part[r // 2, :c, :] = dot_tn(gated[r], ga[...]).astype(BF)
        part[r // 2, c:, :] = lines


def units_kernel(f0, f1, fx, fd, consts, win, hidden, udact):
    for r, f in enumerate((f0, f1, fx, fd)):
        rows = slice(r * f0.shape[0], (r + 1) * f0.shape[0])
        for s in range(0, win.shape[1], 256):
            at = slice(s, s + 256)
            z = dot(f[...], win[:, at]) + consts[INB : INB + 1, at]
            phi, e = gelu_parts(z)
            g = consts[UGATE : UGATE + 1, at]
            udact[rows, at] = (g * (phi + z * e * 0.3989422804014327)).astype(BF)
            hidden[rows, at] = (g * (z * phi)).astype(BF)


def slots(src, keep, send, first_bit, second_bit):
    n = keep.shape[1]
    for a in range(2):
        for b in range(2):
            j = (first_bit ^ a) * 2 + (second_bit ^ b)
            rows = src[pl.ds(pl.multiple_of(j * n, 16), n), :].astype(BF)
            if a == 0:
                keep[b] = rows
            else:
                send[b] = rows


def rows_dot(lefts, rights):
    total = dot_tn(lefts[0], rights[0])
    for left, right in zip(lefts[1:], rights[1:]):
        total = total + dot_tn(left, right)
    return total


def unit_grads(first, gffns, outer, hidden, udact, gi, acc):
    n = gffns[0].shape[0]
    for r, gffn in enumerate(gffns):
        rows, own = slice((first + r) * n, (first + r + 1) * n), slice(r * n, (r + 1) * n)
        for s in range(0, outer.shape[0], 256):
            at = slice(s, s + 256)
            gh = dot_nt(gffn[...], outer[at, :])
            g = (gh * udact[rows, at].astype(F32)).astype(BF)
            gi[own, at] = g
            acc[0, :, at] += fold(gh * hidden[rows, at].astype(F32))
            acc[1, :, at] += fold(g.astype(F32))


def near_grad_kernel(g0, g1, outer, hidden, udact, part, gi, acc):
    n = g0.shape[0]
    part[...] = rows_dot([hidden[:n, :], hidden[n : 2 * n, :]], [g0[...], g1[...]])
    acc[...] = jnp.zeros_like(acc)
    unit_grads(0, (g0, g1), outer, hidden, udact, gi, acc)


def outer_grad_kernel(ids, gx, gd, hidden, part, akeep, asend, big):
    n = gx.shape[0]
    big[...] = part[...] + rows_dot([hidden[2 * n : 3 * n, :], hidden[3 * n :, :]], [gx[...], gd[...]])
    slots(big, akeep, asend, ids[2], ids[1])


def inner_grad_kernel(ids, f0, f1, fx, fd, gx, gd, outer, hidden, udact, near, sums, bkeep, bsend, gi, big, acc):
    n = f0.shape[0]
    d = f0.shape[1]
    acc[...] = sums[...]
    unit_grads(2, (gx, gd), outer, hidden, udact, gi, acc)
    big[:d, :] = rows_dot([f0[...], f1[...], fx[...], fd[...]], [near[:n, :], near[n:, :], gi[:n, :], gi[n:, :]])
    big[d:, :] = jnp.zeros((big.shape[0] - d, big.shape[1]), F32)
    for j in range(2):
        big[d + j : d + j + 1, :] = jnp.sum(acc[j], axis=0, keepdims=True)
    slots(big, bkeep, bsend, ids[1], ids[2])


def attend_back_kernel(ids, g0, g1, gxr, gcr, e_ref, inv_ref, k_ref, v_ref, q_ref, kt, tok, wq, wk, wv, keep, send, wacc, cacc, dct, nat, low):
    b = pl.program_id(0)
    h = ids[0]
    c, d = wq.shape
    length = tok.shape[0]
    quarter = length // 4
    heads = c // HD

    @pl.when(b == 0)
    def _():
        wacc[...] = jnp.zeros_like(wacc)
        cacc[...] = jnp.zeros_like(cacc)

    for r, piece in enumerate((g0[0], g1[0], gxr[0, 0], gcr[1, 0])):
        dct[:, pl.ds(pl.multiple_of((h ^ r) * quarter, 128), quarter)] = piece
    dq, dk, dv = [], [], []
    for i in range(heads):
        part = slice(i * HD, (i + 1) * HD)
        inv = inv_ref[0, i : i + 1, :]
        dcp = dct[part, :].astype(F32) * inv
        dp = dot(v_ref[:, part], dcp.astype(BF))
        e = e_ref[0, i].astype(F32)
        w = e * dp
        delta = jnp.sum(w, axis=0, keepdims=True)
        ds = (w - e * (inv * delta)).astype(BF)
        dq.append(dot(kt[0, part, :], ds) * HD ** (-0.5))
        dk.append(dot(ds, q_ref[:, part]).astype(BF))
        dv.append(dot(e_ref[0, i], dcp.T.astype(BF)).astype(BF))
        cacc[8:9, i * 128 : (i + 1) * 128] += jnp.broadcast_to(jnp.sum(delta, axis=1, keepdims=True), (1, 128))
    dq = jnp.concatenate(dq, axis=0).T.astype(BF)
    nat[...] = jnp.concatenate([dq, *dk, *dv], axis=1)
    wacc[...] += dot_tn(nat[...], tok[...])
    cacc[0:8, : 3 * c] += fold(nat[...].astype(F32))
    part = dot(nat[:, :c], wq[...]) + dot(nat[:, c : 2 * c], wk[...]) + dot(nat[:, 2 * c :], wv[...])
    low[...] = part.astype(BF)
    for r in range(4):
        rows = low[pl.ds(pl.multiple_of((h ^ r) * quarter, quarter), quarter), :]
        at = pl.ds(pl.multiple_of(b * quarter, quarter), quarter)
        if r % 2 == 0:
            keep[r // 2, at, :] = rows
        else:
            send[r // 2, at, :] = rows


def turn_kernel(ids, wacc, cacc, dmine, drecv, ckeep, csend, big):
    n = wacc.shape[0]
    c = n // 3
    big[n + c + 32 :, :] = jnp.zeros((big.shape[0] - n - c - 32, big.shape[1]), F32)
    big[:n, :] = wacc[...]
    big[n : n + c + 16, :] = dmine[...].astype(F32) + drecv[...].astype(F32)
    n = n + c + 16
    big[n : n + 16, :] = jnp.zeros((16, big.shape[1]), F32)
    col = jnp.sum(cacc[0:8, :], axis=0, keepdims=True)
    big[n : n + 1, :c] = col[:, :c]
    big[n + 1 : n + 2, :c] = col[:, 2 * c : 3 * c]
    big[n + 2 : n + 3, : c * 2] = cacc[8:9, : c * 2]
    slots(big, ckeep, csend, ids[1], ids[2])


def third_kernel(ids, mine, got, error, error_1, out):
    n, d = mine.shape
    out[:n, :] = (mine[...].astype(F32) + got[...].astype(F32)).astype(BF)
    total = error[0:1, :1] + error_1[0:1, :1]
    place = ids[3] // 4
    zero = jnp.zeros((1, d), F32)
    rows = [mark(zero, total, place, -1), mark(zero, total, -1, place), jnp.zeros((14, d), F32)]
    out[n:, :] = jnp.concatenate(rows, axis=0).astype(BF)


def pair_kernel(mine, other, out):
    out[0], out[1] = mine[...], other[...]


def last_kernel(mine, other, out):
    n = mine.shape[0] - 16
    out[:n, :] = mine[:n, :]
    out[n : 2 * n, :] = other[:n, :]
    out[2 * n :, :] = (mine[n:, :].astype(F32) + other[n:, :].astype(F32)).astype(BF)


def place(ids, swap, k, o, q, dst):
    n = k.shape[0]
    one, two = (ids[2], ids[1]) if swap else (ids[1], ids[2])
    for a in range(2):
        for b in range(2):
            src = (k if b == 0 else o)[...] if a == 0 else q[b]
            dst[pl.ds(pl.multiple_of(((one ^ a) * 2 + (two ^ b)) * n, 16), n), :] = src.astype(F32)


def weights_out_kernel(ids, consts, ak, ao, aq, pair, q, live, uw, iw, ib, ua, pe, sums):
    place(ids, True, ak, ao, aq, uw)
    d = iw.shape[0]
    n = pair.shape[0] // 2 - 8
    head = d - 3 * n
    for a, src in enumerate((pair, q)):
        for b in range(2):
            j = (ids[1] ^ a) * 2 + (ids[2] ^ b)
            iw[pl.ds(pl.multiple_of(j * n, 16), head), :] = src[b * n : b * n + head, :].astype(F32)
            rest = src[b * n + head : (b + 1) * n, :].astype(F32)

            @pl.when(j < 3)
            def _():
                iw[pl.ds(pl.multiple_of(j * n + head, 16), n - head), :] = rest

            @pl.when(j == 3)
            def _():
                sums[...] = rest

    ua[...] = (1.5 * sums[0:1, :] * (1.0 - consts[UGATE : UGATE + 1, :])).reshape(d)
    ib[...] = sums[1:2, :].reshape(d)
    hard = jnp.sum(pair[2 * n :, :].astype(F32) + q[2 * n :, :].astype(F32))
    pe[0] = 0.5 * hard / live[0]


def final_kernel(ids, consts, ck, co, cq, qw, kw, vw, ow, qb, vb, ob, fg, fs, ub, sg, ss, ha, da, me, live_out, big):
    d = consts.shape[1]
    c = qw.shape[0]

    place(ids, False, ck, co, cq, big)
    qw[...] = big[:c, :]
    kw[...] = big[c : 2 * c, :]
    vw[...] = big[2 * c : 3 * c, :]
    n = 3 * c
    ow[...] = big[n : n + c, :]
    n = n + c
    vec = big[n : n + 16, :]
    own = big[n + 16 : n + 32, :]
    for ref, row in ((sg, 0), (ss, 1), (ub, 2), (fg, 3), (fs, 4), (ob, 5)):
        ref[...] = vec[row : row + 1, :].reshape(d)
    hg = consts[HGATE : HGATE + 1, :]
    da[...] = (1.5 * vec[6:7, :] * hg * (1.0 - hg)).reshape(d)
    qb[...] = own[0:1, :c].reshape(c)
    vb[...] = own[1:2, :c].reshape(c)
    gate = consts[HEADG : HEADG + 1, :]
    for i in range(c // HD):
        g = gate[0, i * HD]
        ha[i] = 1.5 * own[2, i * 128] * (1.0 - g)
    lane = lax.broadcasted_iota(jnp.int32, (1, d), 1)
    nd = ids[4]
    marks = vec[7:8, :]

    def between(lo, hi):
        return jnp.sum(jnp.where((lane >= lo * nd) & (lane < hi * nd), marks, 0.0))

    live = jnp.maximum(between(2, 4), 1.0)
    me[0] = 0.5 * between(0, 2) / live
    live_out[0] = live


def spread_kernel(h_ref, *refs):
    count = (len(refs) - 1) // 5
    sem = refs[-1]
    copies = []
    for a in range(count):
        out = refs[4 * count + a]
        for r in range(4):
            src = refs[4 * a + r]
            blocks = out.shape[0]
            quarter = out.shape[1] // 4
            for b in range(blocks):
                at = pl.ds(pl.multiple_of((h_ref[0] ^ r) * quarter, quarter), quarter)
                copies.append(pltpu.make_async_copy(src.at[pl.ds(b * quarter, quarter)], out.at[b, at], sem.at[len(copies)]))
    for copy in copies:
        copy.start()
    for copy in copies:
        copy.wait()


def shards(
    tokens, teacher, segments, present, query_weight, query_bias, key_weight, value_weight, value_bias, output_weight, output_bias,
    first_gain, first_shift, inner_weight, inner_bias, outer_weight, outer_bias, second_gain, second_shift, head_alpha, head_noise,
    unit_alpha, unit_noise, hidden_alpha, hidden_noise, head_keep, unit_keep, hidden_keep, n_dp,
):
    rows, d = tokens.shape
    blocks, length = segments.shape
    heads = head_alpha.shape[0]
    c = heads * HD
    w = unit_alpha.shape[0]
    quarter = length // 4
    t = blocks * quarter
    n_head = 4
    h = lax.axis_index("head").astype(jnp.int32)
    i_dp = lax.axis_index("dp").astype(jnp.int32)
    bit0, bit1 = i_dp & 1, (i_dp >> 1) & 1
    ids = jnp.stack([h, bit0, bit1, i_dp * n_head + h, jnp.int32(n_dp * n_head)])

    def hop(x, mask, axis="head"):
        size = n_head if axis == "head" else n_dp
        return lax.ppermute(x, axis, [(i, i ^ mask) for i in range(size)])

    def in_hbm(x):
        return pltpu.with_memory_space_constraint(x, pltpu.HBM)

    def after(x, *done):
        return lax.optimization_barrier((x, *done))[0]

    def add(x, y):
        return (x.astype(F32) + y.astype(F32)).astype(BF)

    half = d // 2
    inner_half = lax.dynamic_slice_in_dim(inner_weight, bit0 * half, half, axis=1)
    inner_x = hop(inner_half, 2)

    small = (unit_alpha, unit_noise, unit_keep, inner_bias, hidden_alpha, hidden_noise, hidden_keep, output_bias, first_gain, first_shift,
             outer_bias, second_gain, second_shift, query_bias, value_bias, head_alpha, head_noise, head_keep)
    consts, pack = call(
        prep_kernel,
        [((16, d), F32), ((c + VEC, w), BF)],
        tuple(in_hbm(a) for a in (*small, after(output_weight, inner_half))),
        specs=[ANY] * 19, scratch=[(pltpu.VMEM if a.shape[0] > heads else pltpu.SMEM)(a.shape, a.dtype) for a in small] + [pltpu.SemaphoreType.DMA((19,))], us=2, limit=4, name="prep",
    )
    pack_2 = hop(pack, 2)
    pack_1 = hop(pack, 1)
    inner_1, outer_1 = hop(inner_weight, 1), hop(outer_weight, 1)

    seg3 = segments.reshape(blocks, 1, length)
    live3 = present.reshape(blocks, 1, length)
    full = lambda *s: pl.BlockSpec(s, lambda b, *_: (0,) * len(s))
    c0, c1, cfar, e, inv_l, k, v, q, qst, kt = call(
        attend_kernel,
        [((blocks, c, quarter), BF), ((blocks, c, quarter), BF), ((2, blocks, c, quarter), BF), ((blocks, heads, length, length), BF),
         ((blocks, 8, length), F32), ((rows, c), BF, HBM), ((rows, c), BF, HBM), ((rows, c), BF, HBM), ((blocks, c, length), BF, HBM), ((blocks, c, length), BF, HBM)],
        (ids, in_hbm(tokens), *(in_hbm(a.T) for a in (query_weight, key_weight, value_weight)), consts, seg3, live3),
        prefetch=1, grid=(blocks,),
        specs=[pl.BlockSpec((length, d), lambda b, *_: (b, 0)), full(c, d), full(c, d), full(c, d), full(16, d),
               pl.BlockSpec((1, 1, length), lambda b, *_: (b, 0, 0)), pl.BlockSpec((1, 1, length), lambda b, *_: (b, 0, 0))],
        out_specs=[pl.BlockSpec((1, c, quarter), lambda b, *_: (b, 0, 0)), pl.BlockSpec((1, c, quarter), lambda b, *_: (b, 0, 0)),
                   pl.BlockSpec((2, 1, c, quarter), lambda b, *_: (0, b, 0, 0)), pl.BlockSpec((1, heads, length, length), lambda b, *_: (b, 0, 0, 0)),
                   pl.BlockSpec((1, 8, length), lambda b, *_: (b, 0, 0)), pl.BlockSpec((length, c), lambda b, *_: (b, 0)),
                   pl.BlockSpec((length, c), lambda b, *_: (b, 0)), pl.BlockSpec((length, c), lambda b, *_: (b, 0)),
                   pl.BlockSpec((1, c, length), lambda b, *_: (b, 0, 0)), pl.BlockSpec((1, c, length), lambda b, *_: (b, 0, 0))],
        scratch=[pltpu.VMEM((length, length), F32), pltpu.VMEM((c, length), BF)], us=9, limit=16, name="attend",
    )
    cx = hop(cfar, 2)
    c1r = hop(c1, 1)
    outer_late = after(outer_weight, c1r)
    outer_a = hop(outer_late[:half], 2)
    outer_b = hop(outer_late[half:], 2)
    inner_x, pack_2 = after(inner_x, c0), after(pack_2, c0)
    inner_y, inner_3x = hop(inner_x, 1, "dp"), hop(inner_x, 1)
    packs = (pack, pack_1, pack_2, hop(pack_2, 1))
    pieces = (c0, c1r, cx, hop(cx, 1))

    def first(soft, pieces):
        scratch = [pltpu.VMEM((t, d), BF), pltpu.SemaphoreType.DMA((blocks,))]
        more = [((t, 128), F32), ((t, d), F32), ((4, t, c), BF)]
        return call(
            partial(first_kernel, soft),
            [((t, d), BF), ((t, d), F32)] + (more if soft else []),
            (ids, *pieces, *packs, tokens, consts),
            prefetch=1, specs=[VM] * 8 + [ANY, VM],
            scratch=scratch if soft else scratch + [pltpu.VMEM((t, d), F32), pltpu.VMEM((4, t, c), BF)], us=4, limit=8, name="first" if soft else "hard_first",
        )

    def inner(soft, low):
        return call(
            partial(inner_kernel, soft), [((4, t, w), BF)] * (2 if soft else 1), (ids, low, *inners, *packs),
            prefetch=1, us=8, limit=8, name="inner" if soft else "hard_inner",
        )

    first_low, normed, inv1, attn, gated = first(True, pieces)
    first_2 = hop(first_low, 2)
    first_1 = hop(first_low, 1)
    inner_y = after(inner_y, first_low)
    inners = (inner_weight, inner_1, inner_x, inner_y, inner_3x, hop(inner_y, 1))
    hard_low, hard_normed = first(False, (after(c0, first_low), *pieces[1:]))
    outer_a = after(outer_a, hard_low)
    outer_3a = hop(outer_a, 1)
    hidden, udact = inner(True, after(first_low, hard_low))
    (hard_hidden,) = inner(False, after(hard_low, hidden))
    outer_b = after(outer_b, hard_hidden)
    outers = (outer_weight, outer_1, outer_a, outer_b, outer_3a, hop(outer_b, 1))

    student_rows, grad_two, gffn, v2 = call(
        second_kernel,
        [((t, d), BF), ((t, d), F32), ((t, d), BF), ((8, d), F32)],
        (ids, hidden, normed, *outers, teacher, present, consts),
        prefetch=1, specs=[VM] * 8 + [ANY] + [VM] * 2,
        scratch=[pltpu.VMEM((t, d), BF), pltpu.VMEM((t, d), F32), pltpu.VMEM((5, 8, d), F32), pltpu.SemaphoreType.DMA((blocks,))], us=6, limit=8, name="second",
    )
    gffn_1 = hop(gffn, 1)

    g0, g1, gfar, dkeep, dsend, grad_one = call(
        back_kernel,
        [((blocks, c, quarter), BF), ((blocks, c, quarter), BF), ((2, blocks, c, quarter), BF), ((2, c + 16, d), BF), ((2, c + 16, d), BF), ((t, d), F32)],
        (ids, gffn, udact, *inners, *outers, *packs, grad_two, normed, inv1, attn, gated, v2, present, consts),
        prefetch=1,
        scratch=[pltpu.VMEM((4, t, w), BF), pltpu.VMEM((t, d), F32), pltpu.VMEM((t, d), BF), pltpu.VMEM((4, 8, d), F32)], us=13, limit=12, name="back",
    )
    gx = hop(gfar, 2)
    g1r = hop(g1, 1)
    d_got = hop(dsend, 1)
    first_2 = after(first_2, g0)
    firsts = (first_low, first_1, first_2, hop(first_2, 1))
    hidden_own, udact_own = call(
        units_kernel, [((rows, w), BF), ((rows, w), BF)], (after(firsts[0], g0), *firsts[1:], consts, inner_weight), us=6, limit=8, name="units"
    )
    gx, d_got = after(gx, hidden_own), after(d_got, hidden_own)
    gpieces = (g0, g1r, gx, hop(gx, 1))
    d_mine, d_give = add(dkeep[0], d_got[0]), add(dkeep[1], d_got[1])
    d_recv = hop(d_give, 2)
    gffn_2 = hop(after(gffn, d_give, gx), 2)
    pick = lambda *s: pl.BlockSpec((1,) + s, lambda b, *_: (b,) + (0,) * len(s))
    keep, send, wacc, cacc = call(
        attend_back_kernel,
        [((2, t, d), BF), ((2, t, d), BF), ((3 * c, d), F32), ((16, d), F32)],
        (ids, *gpieces, e, *(in_hbm(a) for a in (inv_l, k, v, q, kt, tokens)), *(in_hbm(a.T) for a in (query_weight, key_weight, value_weight))),
        prefetch=1, grid=(blocks,),
        specs=[pick(c, quarter), pick(c, quarter), pl.BlockSpec((2, 1, c, quarter), lambda b, *_: (0, b, 0, 0)),
               pl.BlockSpec((2, 1, c, quarter), lambda b, *_: (0, b, 0, 0)), pick(heads, length, length), pick(8, length),
               pl.BlockSpec((length, c), lambda b, *_: (b, 0)), pl.BlockSpec((length, c), lambda b, *_: (b, 0)), pl.BlockSpec((length, c), lambda b, *_: (b, 0)), pick(c, length),
               pl.BlockSpec((length, d), lambda b, *_: (b, 0)), full(c, d), full(c, d), full(c, d)],
        out_specs=[full(2, t, d), full(2, t, d), full(3 * c, d), full(16, d)],
        scratch=[pltpu.VMEM((c, length), BF), pltpu.VMEM((length, 3 * c), BF), pltpu.VMEM((length, d), BF)],
        us=15, limit=20, name="attend_back",
    )
    gffn_2 = after(gffn_2, keep)
    n_c = 4 * ((3 * c + c + 32 + 63) // 64) * 16
    ckeep, csend = call(
        turn_kernel, [((2, n_c // 4, d), BF)] * 2, (ids, wacc, cacc, d_mine, after(d_recv, keep, gffn_2)), prefetch=1, specs=[VM] * 4,
        scratch=[pltpu.VMEM((n_c, d), F32)], us=1, limit=8, name="turn",
    )
    got = hop(after(send, ckeep), 1)
    c_got = hop(csend, 1, "dp")
    gffn_2 = after(gffn_2, ckeep)
    gffn_3 = hop(gffn_2, 1)
    part, near, sums = call(
        near_grad_kernel, [((w, d), F32), ((2 * t, w), BF), ((2, 8, w), F32)], (after(gffn, gffn_2), gffn_1, outer_weight, hidden_own, udact_own),
        us=5, limit=8, name="near_grad",
    )
    got = after(got, near)
    mine, give = add(keep[0], got[0]), add(keep[1], got[1])
    recv = hop(give, 2)
    akeep, asend = call(
        outer_grad_kernel, [((2, w // 4, d), BF)] * 2, (ids, after(gffn_2, give), gffn_3, hidden_own, part), prefetch=1, scratch=[pltpu.VMEM((w, d), F32)],
        us=2, limit=8, name="outer_grad",
    )
    a_got = hop(asend, 2, "dp")
    n_b = d + 64
    bkeep, bsend = call(
        inner_grad_kernel, [((2, n_b // 4, w), BF)] * 2,
        (ids, *firsts, after(gffn_2, akeep), gffn_3, outer_weight, hidden_own, udact_own, near, sums), prefetch=1,
        scratch=[pltpu.VMEM((2 * t, w), BF), pltpu.VMEM((n_b, w), F32), pltpu.VMEM((2, 8, w), F32)], us=4, limit=12, name="inner_grad",
    )
    b_got = hop(bsend, 1, "dp")

    def across(x):
        mask = 4
        while mask < n_dp:
            got = hop(x, mask, "dp")
            x = (x, got) if mask * 2 == n_dp else add(x, got)
            mask *= 2
        return x

    def split(keep, got):
        return add(keep[0], got[0]), add(keep[1], got[1])

    c_mine, c_give = split(ckeep, after(c_got, bkeep))
    c_got = hop(c_give, 2, "dp")
    pruned_rows, error = call(
        hard_kernel,
        [((t, d), BF), ((8, 128), F32)],
        (ids, after(hard_hidden, c_give), hard_normed, *outers, teacher, present, consts),
        prefetch=1, specs=[VM] * 8 + [ANY] + [VM] * 2,
        scratch=[pltpu.VMEM((t, d), BF), pltpu.VMEM((t, d), F32), pltpu.VMEM((8, d), F32), pltpu.SemaphoreType.DMA((blocks,))], us=0.1, limit=8, name="hard",
    )

    recv = after(recv, pruned_rows)
    grad_rows = (grad_one + (mine.astype(F32) + recv.astype(F32))).astype(BF)
    grad_2 = hop(grad_rows, 2)
    grad_1 = hop(grad_rows, 1)
    a_mine, a_give = split(akeep, after(a_got, grad_rows))
    a_got = hop(a_give, 1, "dp")
    b_mine, b_give = split(bkeep, after(b_got, a_give))
    b_got = hop(b_give, 2, "dp")
    pruned_rows = after(pruned_rows, b_give)
    pruned_2 = hop(pruned_rows, 2)
    pruned_1 = hop(pruned_rows, 1)
    c_mine = across(add(c_mine, after(c_got, b_give)))
    error = after(error, b_give)
    error = error + hop(error, 2)
    error_1 = hop(error, 1)
    a_mine = across(add(a_mine, after(a_got, c_mine[0])))
    (b_mine,) = call(
        third_kernel, [((n_b // 4 + 16, d), BF)], (ids, b_mine, after(b_got, a_mine[0]), error, error_1), prefetch=1, us=0.1, limit=4, name="third"
    )
    c_mine = add(c_mine[0], after(c_mine[1], b_mine))
    b_mine = across(b_mine)
    c_other = hop(c_mine, 2, "dp")
    grad_2 = after(grad_2, c_mine)
    grads = (grad_rows, grad_1, grad_2, hop(grad_2, 1))
    student_rows = after(student_rows, grad_2)
    student_2 = hop(student_rows, 2)
    student_1 = hop(student_rows, 1)
    a_mine = add(a_mine[0], after(a_mine[1], grad_2))
    a_other = hop(a_mine, 1, "dp")
    (c_pair,) = call(pair_kernel, [((2,) + c_mine.shape, BF)], (c_mine, after(c_other, a_mine)), us=0.1, limit=4, name="pair3")
    c_last = hop(c_pair, 1, "dp")
    b_mine = add(b_mine[0], after(b_mine[1], c_pair))
    b_other = hop(b_mine, 2, "dp")
    (a_pair,) = call(pair_kernel, [((2,) + a_mine.shape, BF)], (a_mine, after(a_other, b_mine)), us=0.1, limit=4, name="pair")
    a_last = hop(a_pair, 2, "dp")
    pruned_2, student_2 = after(pruned_2, a_pair), after(student_2, a_pair)
    pruneds = (pruned_rows, pruned_1, pruned_2, hop(pruned_2, 1))
    students = (student_rows, student_1, student_2, hop(student_2, 1))
    (b_pair,) = call(last_kernel, [((n_b // 2 + 16, d), BF)], (b_mine, after(b_other, student_2, pruned_2, c_last)), us=0.1, limit=4, name="last")
    b_last = hop(b_pair, 1, "dp")
    outs = call(
        spread_kernel,
        [((blocks, length, d), BF)] * 3,
        (ids, after(students[0], b_pair), *students[1:], *pruneds, *grads),
        prefetch=1, specs=[VM] * 12, out_specs=[ANY] * 3, scratch=[pltpu.SemaphoreType.DMA((12 * blocks,))], us=0.1, limit=4, name="spread",
    )
    student, pruned, tokens_grad = (o.reshape(rows, d) for o in outs)
    qw, kw, vw, ow, qb, vb, ob, fg, fs, ub, sg, ss, ha, da, me, live = call(
        final_kernel,
        [((c, d), F32), ((c, d), F32), ((c, d), F32), ((c, d), F32), ((c,), F32), ((c,), F32), ((d,), F32), ((d,), F32), ((d,), F32),
         ((d,), F32), ((d,), F32), ((d,), F32), ((heads,), F32), ((d,), F32), ((1,), F32), ((1,), F32)],
        (ids, consts, c_mine, c_other, after(c_last, outs[0])),
        prefetch=1, specs=[VM] * 4, out_specs=[VM] * 12 + [SM] + [VM] + [SM] * 2,
        scratch=[pltpu.VMEM((n_c, d), F32)], us=0.1, limit=8, name="final",
    )
    uw, iw, ib, ua, pe = call(
        weights_out_kernel,
        [((w, d), F32), ((d, w), F32), ((w,), F32), ((w,), F32), ((1,), F32)],
        (ids, consts, a_mine, a_other, after(a_last, qw), b_pair, b_last, live), prefetch=1,
        specs=[VM] * 6 + [SM], out_specs=[VM] * 4 + [SM], scratch=[pltpu.VMEM((n_b - d, w), F32)], us=0.1, limit=8, name="weights_out",
    )
    return (
        student, pruned, tokens_grad, qw.T, qb, kw.T, vw.T, vb, ow, ob, fg, fs, iw, ib, uw, ub, sg, ss, ha, ua, da, me.reshape(()), pe.reshape(()),
    )


def solution(mesh):
    row, col, lead, unit, none = P("dp", None), P(None, "head"), P("head", None), P("head"), P()
    return jax.shard_map(
        partial(shards, n_dp=mesh.shape["dp"]),
        mesh=mesh,
        in_specs=(row, row, row, row, col, unit, col, col, unit, lead, none, none, none, col, unit, lead, none, none, none) + (unit,) * 4 + (none,) * 2 + (unit,) * 2 + (none,),
        out_specs=(row, row, row, col, unit, col, col, unit, lead, none, none, none, col, unit, lead, none, none, none, unit, unit, none, none, none),
        check_vma=False,
    )
```

```python
from functools import partial

import jax
import jax.numpy as jnp
from jax import lax
from jax.experimental import pallas as pl
from jax.experimental.pallas import tpu as pltpu
from jax.sharding import PartitionSpec as P

F32 = jnp.float32
BF = jnp.bfloat16
HD = 64
EPS = 1e-05
VEC = 32
CH = 128
MB = 1024 * 1024
COST = 5e8

HGATE, HKEEP, OUTB, FG, FS, OUTERB, SG, SS, UGATE, INB, HEADG, QB, VB = range(13)


def dot(a, b):
    return jnp.dot(a, b, preferred_element_type=F32)


def dot_nt(a, b):
    return lax.dot_general(a, b, (((1,), (1,)), ((), ())), preferred_element_type=F32)


def dot_tn(a, b):
    return lax.dot_general(a, b, (((0,), (0,)), ((), ())), preferred_element_type=F32)


def gelu_parts(v):
    z = jnp.abs(v) * 0.7071067811865476
    e = jnp.exp(-(z * z))
    t = 1.0 / (1.0 + 0.3275911 * z)
    p = 0.5 * 1.061405429
    p = p * t - 0.5 * 1.453152027
    p = p * t + 0.5 * 1.421413741
    p = p * t - 0.5 * 0.284496736
    p = p * t + 0.5 * 0.254829592
    q = p * t * e
    return jnp.where(v >= 0.0, 1.0 - q, q), e


def fold(x):
    return jnp.sum(x.reshape(x.shape[0] // 8, 8, x.shape[1]), axis=0)


def mean(x):
    return jnp.mean(x, axis=1, keepdims=True)


def call(kernel, outs, args, specs=None, scratch=(), grid=(), prefetch=0, out_specs=None, us=1.0, limit=40, name=None):
    vmem = pl.BlockSpec(memory_space=pltpu.VMEM)
    specs = specs or [vmem] * (len(args) - prefetch)
    out_specs = out_specs or [vmem] * len(outs)
    return pl.pallas_call(
        kernel,
        out_shape=[pltpu.HBM(*o[:2]) if len(o) > 2 else jax.ShapeDtypeStruct(*o) for o in outs],
        grid_spec=pltpu.PrefetchScalarGridSpec(
            num_scalar_prefetch=prefetch, grid=grid, in_specs=specs, out_specs=out_specs, scratch_shapes=list(scratch)
        ),
        compiler_params=pltpu.CompilerParams(vmem_limit_bytes=limit * MB),
        cost_estimate=pl.CostEstimate(flops=int(us * COST), bytes_accessed=0, transcendentals=0),
        name=name,
    )(*args)


VM = pl.BlockSpec(memory_space=pltpu.VMEM)
SM = pl.BlockSpec(memory_space=pltpu.SMEM)
ANY = pl.BlockSpec(memory_space=pl.ANY)
HBM = pl.BlockSpec(memory_space=pltpu.HBM)


def prep_kernel(*refs):
    count = (len(refs) - 3) // 2
    srcs, wo, consts, pack, held, sem = refs[:count], refs[count], refs[count + 1], refs[count + 2], refs[count + 3 : -1], refs[-1]
    w = consts.shape[1]
    c = wo.shape[0]
    copies = [pltpu.make_async_copy(a, b, sem.at[i]) for i, (a, b) in enumerate(zip(srcs, held))]
    copies.append(pltpu.make_async_copy(wo, pack.at[pl.ds(0, c)], sem.at[count]))
    for copy in copies:
        copy.start()
    for copy in copies:
        copy.wait()
    ua, un, uk, ib, da, dn, dk, ob, fg, fs, ub, sg, ss, qb, vb, ha, hn, hk = held

    def line(ref):
        return ref[...].astype(F32).reshape(1, ref.shape[0])

    def gate(a, n):
        return jax.nn.sigmoid((a + n) * 1.5)

    consts[...] = jnp.zeros_like(consts)
    consts[HGATE : HGATE + 1, :] = gate(line(da), line(dn))
    for row, ref in ((HKEEP, dk), (OUTB, ob), (FG, fg), (FS, fs), (OUTERB, ub), (SG, sg), (SS, ss), (INB, ib)):
        consts[row : row + 1, :] = line(ref)
    ugate = gate(line(ua), line(un))
    consts[UGATE : UGATE + 1, :] = ugate
    consts[QB : QB + 1, :c] = line(qb)
    consts[VB : VB + 1, :c] = line(vb)
    lane = lax.broadcasted_iota(jnp.int32, (1, w), 1)
    logit = jnp.zeros((1, w), F32)
    keep = jnp.zeros((1, w), F32)
    for i in range(c // HD):
        here = (lane >= i * HD) & (lane < (i + 1) * HD)
        logit = jnp.where(here, ha[i] + hn[i], logit)
        keep = jnp.where(here, hk[i].astype(F32), keep)
    hgate = jax.nn.sigmoid(logit * 1.5)
    consts[HEADG : HEADG + 1, :] = hgate

    def halves(x):
        high = x.astype(BF).astype(F32)
        return high, x - high

    uh, ul = halves(ugate)
    hh, hl = halves(hgate)
    rows = [uh, ul, line(uk), line(ib), hh, hl, keep] + [jnp.zeros((1, w), F32)] * (VEC - 7)
    pack[c:, :] = jnp.concatenate(rows, axis=0).astype(BF)


def attend_kernel(ids, tok, wq, wk, wv, consts, seg, live, c0, c1, cfar, e_ref, inv_ref, k_ref, v_ref, q_ref, qst_ref, kt_ref, bias, ct):
    c = wq.shape[0]
    length = tok.shape[0]
    quarter = length // 4
    x = tok[...]
    q = ((dot_nt(x, wq[...]) + consts[QB : QB + 1, :c]).astype(BF).astype(F32) * HD ** (-0.5)).astype(BF)
    k = dot_nt(x, wk[...]).astype(BF)
    v = (dot_nt(x, wv[...]) + consts[VB : VB + 1, :c]).astype(BF)
    k_ref[...] = k
    v_ref[...] = v
    q_ref[...] = q
    qst = q.astype(F32).T.astype(BF)
    qst_ref[0] = qst
    kt_ref[0] = k.astype(F32).T.astype(BF)
    vt = v.astype(F32).T.astype(BF)
    seg_row = seg[0].astype(F32)
    code = jnp.where(live[0] == 1, seg_row, -1.0)
    code_col = jnp.broadcast_to(code, (128, length)).T[:, :1]
    row = lax.broadcasted_iota(jnp.int32, (length, length), 0)
    col = lax.broadcasted_iota(jnp.int32, (length, length), 1)
    bias[...] = jnp.where((code_col == seg_row) | (row == col), 0.0, -1e30)
    h = ids[0]
    inv_ref[...] = jnp.zeros_like(inv_ref)
    for i in range(c // HD):
        part = slice(i * HD, (i + 1) * HD)
        s = dot(k[:, part], qst[part, :]) + bias[...]
        top = jnp.max(s, axis=0, keepdims=True)
        e = jnp.exp(s - top)
        inv = 1.0 / jnp.sum(e, axis=0, keepdims=True)
        low = e.astype(BF)
        e_ref[0, i] = low
        inv_ref[0, i : i + 1, :] = inv
        ct[part, :] = (dot(vt[part, :], low) * inv).astype(BF)
    for r in range(4):
        piece = ct[:, pl.ds(pl.multiple_of((h ^ r) * quarter, 128), quarter)]
        if r < 2:
            (c0, c1)[r][0] = piece
        else:
            cfar[r - 2, 0] = piece


def mark(marks, value, first, second):
    lane = lax.broadcasted_iota(jnp.int32, marks.shape, 1)
    full = jnp.broadcast_to(value, marks.shape)
    high = full.astype(BF).astype(F32)
    return jnp.where(lane == first, high, jnp.where(lane == second, full - high, marks))


def unit_chunks(weights, p):
    half = weights[2].shape[1]
    chunks = []
    for r in range(2):
        chunks += [(r, weights[r], s, 256, s) for s in range(0, weights[r].shape[1], 256)]
    for r, (mine, other) in ((2, weights[2:4]), (3, weights[4:6])):
        for ref, base in ((mine, p * half), (other, (1 - p) * half)):
            for s in range(0, half, 256):
                chunks.append((r, ref, s, min(256, half - s), pl.multiple_of(base + s, 128)))
    return chunks


def start(copies):
    for copy in copies:
        copy.start()


def wait(copies):
    for copy in copies:
        copy.wait()


def load_rows(src, dst, h, sem, blocks, quarter):
    return [
        pltpu.make_async_copy(src.at[pl.ds(b * 4 * quarter + pl.multiple_of(h * quarter, quarter), quarter)], dst.at[pl.ds(b * quarter, quarter)], sem.at[b])
        for b in range(blocks)
    ]


def head_rows(vec, soft, c):
    if soft:
        return (vec[4:5, :] + vec[5:6, :])[:, :c]
    return vec[6:7, :][:, :c]


def project(pieces, packs, gated, attn, consts, soft):
    blocks, c, quarter = pieces[0].shape
    for r in range(4):
        g = head_rows(packs[r][c:, :].astype(F32), soft, c)
        for b in range(blocks):
            gated[r, b * quarter : (b + 1) * quarter, :] = (pieces[r][b].astype(F32).T * g).astype(BF)
    total = dot(gated[0], packs[0][:c, :])
    for r in range(1, 4):
        total = total + dot(gated[r], packs[r][:c, :])
    attn[...] = total + consts[OUTB : OUTB + 1, :]


def first_kernel(soft, ids, c0, c1, xr, cr, s0, s1, s2, s3, tok_any, consts, first_low, normed, *refs):
    if soft:
        inv, attn, gated, tok, tsem = refs
    else:
        tok, tsem, attn, gated = refs
    blocks, c, quarter = c0.shape
    loads = load_rows(tok_any, tok, ids[0], tsem, blocks, quarter)
    start(loads)
    project([c0, c1, xr.at[0], cr.at[1]], [s0, s1, s2, s3], gated, attn, consts, soft)
    wait(loads)
    gate = HGATE if soft else HKEEP

    @pl.loop(0, tok.shape[0] // CH)
    def _(i):
        rows = pl.ds(pl.multiple_of(i * CH, CH), CH)
        x = tok[rows, :].astype(F32) + consts[gate : gate + 1, :] * attn[rows, :]
        x = x - mean(x)
        iv = lax.rsqrt(mean(x * x) + EPS)
        n = x * iv
        normed[rows, :] = n
        if soft:
            inv[rows, :] = jnp.broadcast_to(iv, (CH, 128))
        first_low[rows, :] = (n * consts[FG : FG + 1, :] + consts[FS : FS + 1, :]).astype(BF)


def ffn_inner(first, wins, packs, p, hidden, soft, udact=None):
    c = packs[0].shape[0] - VEC
    for r, ref, s, n, unit in unit_chunks(wins, p):
        at = pl.ds(unit, n)
        vec = packs[r][c : c + 16, at].astype(F32)
        z = dot(first[...], ref[:, s : s + n]) + vec[3:4, :]
        phi, e = gelu_parts(z)
        if soft:
            g = vec[0:1, :] + vec[1:2, :]
            udact[r, :, at] = (g * (phi + z * e * 0.3989422804014327)).astype(BF)
        else:
            g = vec[2:3, :]
        hidden[r, :, at] = (g * (z * phi)).astype(BF)


def ffn_outer(hidden, outers, ffn, consts):
    half = outers[2].shape[0]
    total = dot(hidden[0], outers[0][...]) + dot(hidden[1], outers[1][...])
    for r, (a, b) in ((2, outers[2:4]), (3, outers[4:6])):
        total = total + dot(hidden[r, :, :half], a[...]) + dot(hidden[r, :, half:], b[...])
    ffn[...] = total + consts[OUTERB : OUTERB + 1, :]


def row_mask(live, h, b, quarter, at):
    count = jnp.sum(live[b : b + 1, :].astype(F32))
    place = (h * quarter + at).astype(F32) + lax.broadcasted_iota(jnp.int32, (CH, 1), 0).astype(F32)
    return jnp.where(place < count, 1.0, 0.0)


def inner_kernel(soft, ids, first_low, *refs):
    ffn_inner(first_low, refs[:6], refs[6:10], ids[1], refs[10], soft, refs[11] if soft else None)


def second_kernel(ids, hidden, normed, *refs):
    wsrc, teach_any, live, consts, student, grad_two, gffn, vecs_out, teach, ffn, acc, tsem = refs[:6], *refs[6:]
    blocks, length = live.shape
    quarter = length // 4
    h = ids[0]
    rowload = load_rows(teach_any, teach, h, tsem, blocks, quarter)
    start(rowload)
    ffn_outer(hidden, wsrc, ffn, consts)
    wait(rowload)
    acc[...] = jnp.zeros_like(acc)
    for b in range(blocks):

        @pl.loop(0, quarter // CH)
        def _(i):
            rows = pl.ds(pl.multiple_of(b * quarter + i * CH, CH), CH)
            f = ffn[rows, :]
            hg = consts[HGATE : HGATE + 1, :]
            x = normed[rows, :] * consts[FG : FG + 1, :] + consts[FS : FS + 1, :] + hg * f
            x = x - mean(x)
            iv = lax.rsqrt(mean(x * x) + EPS)
            n = x * iv
            out = n * consts[SG : SG + 1, :] + consts[SS : SS + 1, :]
            student[rows, :] = out.astype(BF)
            err = (out - teach[rows, :].astype(F32)) * row_mask(live, h, b, quarter, i * CH)
            acc[0] += fold(err * n)
            acc[1] += fold(err)
            acc[4] += fold(err * err)
            e = err * consts[SG : SG + 1, :]
            g = iv * (e - mean(e) - n * mean(e * n))
            grad_two[rows, :] = g
            gf = hg * g
            acc[2] += fold(gf)
            acc[3] += fold(g * f)
            gffn[rows, :] = gf.astype(BF)

    vecs_out[...] = jnp.zeros_like(vecs_out)
    for j in range(5):
        vecs_out[j : j + 1, :] = jnp.sum(acc[j], axis=0, keepdims=True)


def hard_kernel(ids, hidden, normed, *refs):
    wsrc, teach_any, live, consts, pruned, error, teach, ffn, acc, tsem = refs[:6], *refs[6:]
    blocks, length = live.shape
    quarter = length // 4
    h = ids[0]
    rowload = load_rows(teach_any, teach, h, tsem, blocks, quarter)
    start(rowload)
    ffn_outer(hidden, wsrc, ffn, consts)
    wait(rowload)
    acc[...] = jnp.zeros_like(acc)
    for b in range(blocks):

        @pl.loop(0, quarter // CH)
        def _(i):
            rows = pl.ds(pl.multiple_of(b * quarter + i * CH, CH), CH)
            x = normed[rows, :] * consts[FG : FG + 1, :] + consts[FS : FS + 1, :] + consts[HKEEP : HKEEP + 1, :] * ffn[rows, :]
            x = x - mean(x)
            n = x * lax.rsqrt(mean(x * x) + EPS)
            out = n * consts[SG : SG + 1, :] + consts[SS : SS + 1, :]
            pruned[rows, :] = out.astype(BF)
            err = (out - teach[rows, :].astype(F32)) * row_mask(live, h, b, quarter, i * CH)
            acc[...] += fold(err * err)

    error[...] = jnp.broadcast_to(jnp.sum(acc[...]), error.shape)


def back_kernel(ids, gffn, udact, *refs):
    isrc, osrc, packs = refs[:6], refs[6:12], refs[12:16]
    grad_two, normed, inv, attn, gated, v2, live, consts, g0, g1, gfar, dkeep, dsend, grad_one, gi, back, ga, acc = refs[16:]
    c = packs[0].shape[0] - VEC
    w = gi.shape[2]
    half = w // 2
    blocks, _, quarter = g0.shape
    for r, (a, b) in ((0, osrc[:1] * 2), (1, osrc[1:2] * 2), (2, osrc[2:4]), (3, osrc[4:6])):
        for s in (0, 256, 512) if r < 2 else (0, 256, half, half + 256):
            n = 256 if r < 2 or s % half == 0 else half - 256
            ref, row = (a, s) if r < 2 or s < half else (b, s - half)
            at = slice(s, s + n)
            gi[r, :, at] = (dot_nt(gffn[...], ref[row : row + n, :]) * udact[r, :, at].astype(F32)).astype(BF)
    total = dot_nt(gi[0], isrc[0][...]) + dot_nt(gi[1], isrc[1][...])
    for r, (x, y) in ((2, isrc[2:4]), (3, isrc[4:6])):
        for ref, q in ((x, ids[1]), (y, 1 - ids[1])):
            total = total + dot_nt(gi[r, :, pl.ds(pl.multiple_of(q * half, 128), half)], ref[...])
    back[...] = total
    acc[...] = jnp.zeros_like(acc)

    @pl.loop(0, back.shape[0] // CH)
    def _(i):
        rows = pl.ds(pl.multiple_of(i * CH, CH), CH)
        n = normed[rows, :]
        gf = grad_two[rows, :] + back[rows, :]
        acc[0] += fold(gf * n)
        acc[1] += fold(gf)
        e = gf * consts[FG : FG + 1, :]
        g = inv[rows, :1] * (e - mean(e) - n * mean(e * n))
        grad_one[rows, :] = g
        gat = consts[HGATE : HGATE + 1, :] * g
        acc[2] += fold(gat)
        acc[3] += fold(g * attn[rows, :])
        ga[rows, :] = gat.astype(BF)

    d = back.shape[1]
    v3 = [jnp.sum(acc[j], axis=0, keepdims=True) for j in range(4)]
    count = jnp.zeros((), F32)
    for j in range(blocks):
        real = jnp.sum(live[j : j + 1, :].astype(F32))
        count += jnp.clip(real - (ids[0] * quarter).astype(F32), 0.0, float(quarter))
    marks = mark(jnp.zeros((1, d), F32), jnp.sum(v2[4:5, :]), ids[3], ids[3] + ids[4])
    marks = mark(marks, count, ids[3] + 2 * ids[4], ids[3] + 3 * ids[4])
    lines = jnp.concatenate([v2[0:3, :], *v3[:3], v2[3:4, :] + v3[3], marks, jnp.zeros((8, d), F32)], axis=0).astype(BF)
    for r in range(4):
        gg = dot_nt(ga[...], packs[r][:c, :]) * head_rows(packs[r][c:, :].astype(F32), True, c)
        for b in range(blocks):
            piece = gg[b * quarter : (b + 1) * quarter, :].T.astype(BF)
            if r == 0:
                g0[b] = piece
            elif r == 1:
                g1[b] = piece
            else:
                gfar[r - 2, b] = piece
        part = dsend if r % 2 else dkeep
        part[r // 2, :c, :] = dot_tn(gated[r], ga[...]).astype(BF)
        part[r // 2, c:, :] = lines


def units_kernel(f0, f1, fx, fd, consts, win, hidden, udact):
    for r, f in enumerate((f0, f1, fx, fd)):
        rows = slice(r * f0.shape[0], (r + 1) * f0.shape[0])
        for s in range(0, win.shape[1], 256):
            at = slice(s, s + 256)
            z = dot(f[...], win[:, at]) + consts[INB : INB + 1, at]
            phi, e = gelu_parts(z)
            g = consts[UGATE : UGATE + 1, at]
            udact[rows, at] = (g * (phi + z * e * 0.3989422804014327)).astype(BF)
            hidden[rows, at] = (g * (z * phi)).astype(BF)


def slots(src, keep, send, first_bit, second_bit):
    n = keep.shape[1]
    for a in range(2):
        for b in range(2):
            j = (first_bit ^ a) * 2 + (second_bit ^ b)
            rows = src[pl.ds(pl.multiple_of(j * n, 16), n), :].astype(BF)
            if a == 0:
                keep[b] = rows
            else:
                send[b] = rows


def rows_dot(lefts, rights):
    total = dot_tn(lefts[0], rights[0])
    for left, right in zip(lefts[1:], rights[1:]):
        total = total + dot_tn(left, right)
    return total


def unit_grads(first, gffns, outer, hidden, udact, gi, acc):
    n = gffns[0].shape[0]
    for r, gffn in enumerate(gffns):
        rows, own = slice((first + r) * n, (first + r + 1) * n), slice(r * n, (r + 1) * n)
        for s in range(0, outer.shape[0], 256):
            at = slice(s, s + 256)
            gh = dot_nt(gffn[...], outer[at, :])
            g = (gh * udact[rows, at].astype(F32)).astype(BF)
            gi[own, at] = g
            acc[0, :, at] += fold(gh * hidden[rows, at].astype(F32))
            acc[1, :, at] += fold(g.astype(F32))


def near_grad_kernel(g0, g1, outer, hidden, udact, part, gi, acc):
    n = g0.shape[0]
    part[...] = rows_dot([hidden[:n, :], hidden[n : 2 * n, :]], [g0[...], g1[...]])
    acc[...] = jnp.zeros_like(acc)
    unit_grads(0, (g0, g1), outer, hidden, udact, gi, acc)


def outer_grad_kernel(ids, gx, gd, hidden, part, akeep, asend, big):
    n = gx.shape[0]
    big[...] = part[...] + rows_dot([hidden[2 * n : 3 * n, :], hidden[3 * n :, :]], [gx[...], gd[...]])
    slots(big, akeep, asend, ids[2], ids[1])


def inner_grad_kernel(ids, f0, f1, fx, fd, gx, gd, outer, hidden, udact, near, sums, bkeep, bsend, gi, big, acc):
    n = f0.shape[0]
    d = f0.shape[1]
    acc[...] = sums[...]
    unit_grads(2, (gx, gd), outer, hidden, udact, gi, acc)
    big[:d, :] = rows_dot([f0[...], f1[...], fx[...], fd[...]], [near[:n, :], near[n:, :], gi[:n, :], gi[n:, :]])
    big[d:, :] = jnp.zeros((big.shape[0] - d, big.shape[1]), F32)
    for j in range(2):
        big[d + j : d + j + 1, :] = jnp.sum(acc[j], axis=0, keepdims=True)
    slots(big, bkeep, bsend, ids[1], ids[2])


def attend_back_kernel(ids, g0, g1, gxr, gcr, e_ref, inv_ref, k_ref, v_ref, q_ref, kt, tok, wq, wk, wv, keep, send, wacc, cacc, dct, nat, low):
    b = pl.program_id(0)
    h = ids[0]
    c, d = wq.shape
    length = tok.shape[0]
    quarter = length // 4
    heads = c // HD

    @pl.when(b == 0)
    def _():
        wacc[...] = jnp.zeros_like(wacc)
        cacc[...] = jnp.zeros_like(cacc)

    for r, piece in enumerate((g0[0], g1[0], gxr[0, 0], gcr[1, 0])):
        dct[:, pl.ds(pl.multiple_of((h ^ r) * quarter, 128), quarter)] = piece
    dq, dk, dv = [], [], []
    for i in range(heads):
        part = slice(i * HD, (i + 1) * HD)
        inv = inv_ref[0, i : i + 1, :]
        dcp = dct[part, :].astype(F32) * inv
        dp = dot(v_ref[:, part], dcp.astype(BF))
        e = e_ref[0, i].astype(F32)
        w = e * dp
        delta = jnp.sum(w, axis=0, keepdims=True)
        ds = (w - e * (inv * delta)).astype(BF)
        dq.append(dot(kt[0, part, :], ds) * HD ** (-0.5))
        dk.append(dot(ds, q_ref[:, part]).astype(BF))
        dv.append(dot(e_ref[0, i], dcp.T.astype(BF)).astype(BF))
        cacc[8:9, i * 128 : (i + 1) * 128] += jnp.broadcast_to(jnp.sum(delta, axis=1, keepdims=True), (1, 128))
    dq = jnp.concatenate(dq, axis=0).T.astype(BF)
    nat[...] = jnp.concatenate([dq, *dk, *dv], axis=1)
    wacc[...] += dot_tn(nat[...], tok[...])
    cacc[0:8, : 3 * c] += fold(nat[...].astype(F32))
    part = dot(nat[:, :c], wq[...]) + dot(nat[:, c : 2 * c], wk[...]) + dot(nat[:, 2 * c :], wv[...])
    low[...] = part.astype(BF)
    for r in range(4):
        rows = low[pl.ds(pl.multiple_of((h ^ r) * quarter, quarter), quarter), :]
        at = pl.ds(pl.multiple_of(b * quarter, quarter), quarter)
        if r % 2 == 0:
            keep[r // 2, at, :] = rows
        else:
            send[r // 2, at, :] = rows


def turn_kernel(ids, wacc, cacc, dmine, drecv, ckeep, csend, big):
    n = wacc.shape[0]
    c = n // 3
    big[n + c + 32 :, :] = jnp.zeros((big.shape[0] - n - c - 32, big.shape[1]), F32)
    big[:n, :] = wacc[...]
    big[n : n + c + 16, :] = dmine[...].astype(F32) + drecv[...].astype(F32)
    n = n + c + 16
    big[n : n + 16, :] = jnp.zeros((16, big.shape[1]), F32)
    col = jnp.sum(cacc[0:8, :], axis=0, keepdims=True)
    big[n : n + 1, :c] = col[:, :c]
    big[n + 1 : n + 2, :c] = col[:, 2 * c : 3 * c]
    big[n + 2 : n + 3, : c * 2] = cacc[8:9, : c * 2]
    slots(big, ckeep, csend, ids[1], ids[2])


def third_kernel(ids, mine, got, error, error_1, out):
    n, d = mine.shape
    out[:n, :] = (mine[...].astype(F32) + got[...].astype(F32)).astype(BF)
    total = error[0:1, :1] + error_1[0:1, :1]
    place = ids[3] // 4
    zero = jnp.zeros((1, d), F32)
    rows = [mark(zero, total, place, -1), mark(zero, total, -1, place), jnp.zeros((14, d), F32)]
    out[n:, :] = jnp.concatenate(rows, axis=0).astype(BF)


def pair_kernel(mine, other, out):
    out[0], out[1] = mine[...], other[...]


def last_kernel(mine, other, out):
    n = mine.shape[0] - 16
    out[:n, :] = mine[:n, :]
    out[n : 2 * n, :] = other[:n, :]
    out[2 * n :, :] = (mine[n:, :].astype(F32) + other[n:, :].astype(F32)).astype(BF)


def place(ids, swap, k, o, q, dst):
    n = k.shape[0]
    one, two = (ids[2], ids[1]) if swap else (ids[1], ids[2])
    for a in range(2):
        for b in range(2):
            src = (k if b == 0 else o)[...] if a == 0 else q[b]
            dst[pl.ds(pl.multiple_of(((one ^ a) * 2 + (two ^ b)) * n, 16), n), :] = src.astype(F32)


def weights_out_kernel(ids, consts, ak, ao, aq, pair, q, live, uw, iw, ib, ua, pe, sums):
    place(ids, True, ak, ao, aq, uw)
    d = iw.shape[0]
    n = pair.shape[0] // 2 - 8
    head = d - 3 * n
    for a, src in enumerate((pair, q)):
        for b in range(2):
            j = (ids[1] ^ a) * 2 + (ids[2] ^ b)
            iw[pl.ds(pl.multiple_of(j * n, 16), head), :] = src[b * n : b * n + head, :].astype(F32)
            rest = src[b * n + head : (b + 1) * n, :].astype(F32)

            @pl.when(j < 3)
            def _():
                iw[pl.ds(pl.multiple_of(j * n + head, 16), n - head), :] = rest

            @pl.when(j == 3)
            def _():
                sums[...] = rest

    ua[...] = (1.5 * sums[0:1, :] * (1.0 - consts[UGATE : UGATE + 1, :])).reshape(d)
    ib[...] = sums[1:2, :].reshape(d)
    hard = jnp.sum(pair[2 * n :, :].astype(F32) + q[2 * n :, :].astype(F32))
    pe[0] = 0.5 * hard / live[0]


def final_kernel(ids, consts, ck, co, cq, qw, kw, vw, ow, qb, vb, ob, fg, fs, ub, sg, ss, ha, da, me, live_out, big):
    d = consts.shape[1]
    c = qw.shape[0]

    place(ids, False, ck, co, cq, big)
    qw[...] = big[:c, :]
    kw[...] = big[c : 2 * c, :]
    vw[...] = big[2 * c : 3 * c, :]
    n = 3 * c
    ow[...] = big[n : n + c, :]
    n = n + c
    vec = big[n : n + 16, :]
    own = big[n + 16 : n + 32, :]
    for ref, row in ((sg, 0), (ss, 1), (ub, 2), (fg, 3), (fs, 4), (ob, 5)):
        ref[...] = vec[row : row + 1, :].reshape(d)
    hg = consts[HGATE : HGATE + 1, :]
    da[...] = (1.5 * vec[6:7, :] * hg * (1.0 - hg)).reshape(d)
    qb[...] = own[0:1, :c].reshape(c)
    vb[...] = own[1:2, :c].reshape(c)
    gate = consts[HEADG : HEADG + 1, :]
    for i in range(c // HD):
        g = gate[0, i * HD]
        ha[i] = 1.5 * own[2, i * 128] * (1.0 - g)
    lane = lax.broadcasted_iota(jnp.int32, (1, d), 1)
    nd = ids[4]
    marks = vec[7:8, :]

    def between(lo, hi):
        return jnp.sum(jnp.where((lane >= lo * nd) & (lane < hi * nd), marks, 0.0))

    live = jnp.maximum(between(2, 4), 1.0)
    me[0] = 0.5 * between(0, 2) / live
    live_out[0] = live


def spread_kernel(h_ref, *refs):
    count = (len(refs) - 1) // 5
    sem = refs[-1]
    copies = []
    for a in range(count):
        out = refs[4 * count + a]
        for r in range(4):
            src = refs[4 * a + r]
            blocks = out.shape[0]
            quarter = out.shape[1] // 4
            for b in range(blocks):
                at = pl.ds(pl.multiple_of((h_ref[0] ^ r) * quarter, quarter), quarter)
                copies.append(pltpu.make_async_copy(src.at[pl.ds(b * quarter, quarter)], out.at[b, at], sem.at[len(copies)]))
    for copy in copies:
        copy.start()
    for copy in copies:
        copy.wait()


def shards(
    tokens, teacher, segments, present, query_weight, query_bias, key_weight, value_weight, value_bias, output_weight, output_bias,
    first_gain, first_shift, inner_weight, inner_bias, outer_weight, outer_bias, second_gain, second_shift, head_alpha, head_noise,
    unit_alpha, unit_noise, hidden_alpha, hidden_noise, head_keep, unit_keep, hidden_keep, n_dp,
):
    rows, d = tokens.shape
    blocks, length = segments.shape
    heads = head_alpha.shape[0]
    c = heads * HD
    w = unit_alpha.shape[0]
    quarter = length // 4
    t = blocks * quarter
    n_head = 4
    h = lax.axis_index("head").astype(jnp.int32)
    i_dp = lax.axis_index("dp").astype(jnp.int32)
    bit0, bit1 = i_dp & 1, (i_dp >> 1) & 1
    ids = jnp.stack([h, bit0, bit1, i_dp * n_head + h, jnp.int32(n_dp * n_head)])

    def hop(x, mask, axis="head"):
        size = n_head if axis == "head" else n_dp
        return lax.ppermute(x, axis, [(i, i ^ mask) for i in range(size)])

    def in_hbm(x):
        return pltpu.with_memory_space_constraint(x, pltpu.HBM)

    def after(x, *done):
        return lax.optimization_barrier((x, *done))[0]

    def add(x, y):
        return (x.astype(F32) + y.astype(F32)).astype(BF)

    half = d // 2
    inner_half = lax.dynamic_slice_in_dim(inner_weight, bit0 * half, half, axis=1)
    inner_x = hop(inner_half, 2)

    small = (unit_alpha, unit_noise, unit_keep, inner_bias, hidden_alpha, hidden_noise, hidden_keep, output_bias, first_gain, first_shift,
             outer_bias, second_gain, second_shift, query_bias, value_bias, head_alpha, head_noise, head_keep)
    consts, pack = call(
        prep_kernel,
        [((16, d), F32), ((c + VEC, w), BF)],
        tuple(in_hbm(a) for a in (*small, after(output_weight, inner_half))),
        specs=[ANY] * 19, scratch=[(pltpu.VMEM if a.shape[0] > heads else pltpu.SMEM)(a.shape, a.dtype) for a in small] + [pltpu.SemaphoreType.DMA((19,))], us=2, limit=4, name="prep",
    )
    pack_2 = hop(pack, 2)
    pack_1 = hop(pack, 1)
    inner_1, outer_1 = hop(inner_weight, 1), hop(outer_weight, 1)

    seg3 = segments.reshape(blocks, 1, length)
    live3 = present.reshape(blocks, 1, length)
    full = lambda *s: pl.BlockSpec(s, lambda b, *_: (0,) * len(s))
    c0, c1, cfar, e, inv_l, k, v, q, qst, kt = call(
        attend_kernel,
        [((blocks, c, quarter), BF), ((blocks, c, quarter), BF), ((2, blocks, c, quarter), BF), ((blocks, heads, length, length), BF),
         ((blocks, 8, length), F32), ((rows, c), BF, HBM), ((rows, c), BF, HBM), ((rows, c), BF, HBM), ((blocks, c, length), BF, HBM), ((blocks, c, length), BF, HBM)],
        (ids, in_hbm(tokens), *(in_hbm(a.T) for a in (query_weight, key_weight, value_weight)), consts, seg3, live3),
        prefetch=1, grid=(blocks,),
        specs=[pl.BlockSpec((length, d), lambda b, *_: (b, 0)), full(c, d), full(c, d), full(c, d), full(16, d),
               pl.BlockSpec((1, 1, length), lambda b, *_: (b, 0, 0)), pl.BlockSpec((1, 1, length), lambda b, *_: (b, 0, 0))],
        out_specs=[pl.BlockSpec((1, c, quarter), lambda b, *_: (b, 0, 0)), pl.BlockSpec((1, c, quarter), lambda b, *_: (b, 0, 0)),
                   pl.BlockSpec((2, 1, c, quarter), lambda b, *_: (0, b, 0, 0)), pl.BlockSpec((1, heads, length, length), lambda b, *_: (b, 0, 0, 0)),
                   pl.BlockSpec((1, 8, length), lambda b, *_: (b, 0, 0)), pl.BlockSpec((length, c), lambda b, *_: (b, 0)),
                   pl.BlockSpec((length, c), lambda b, *_: (b, 0)), pl.BlockSpec((length, c), lambda b, *_: (b, 0)),
                   pl.BlockSpec((1, c, length), lambda b, *_: (b, 0, 0)), pl.BlockSpec((1, c, length), lambda b, *_: (b, 0, 0))],
        scratch=[pltpu.VMEM((length, length), F32), pltpu.VMEM((c, length), BF)], us=9, limit=16, name="attend",
    )
    cx = hop(cfar, 2)
    c1r = hop(c1, 1)
    outer_late = after(outer_weight, c1r)
    outer_a = hop(outer_late[:half], 2)
    outer_b = hop(outer_late[half:], 2)
    inner_x, pack_2 = after(inner_x, c0), after(pack_2, c0)
    inner_y, inner_3x = hop(inner_x, 1, "dp"), hop(inner_x, 1)
    packs = (pack, pack_1, pack_2, hop(pack_2, 1))
    pieces = (c0, c1r, cx, hop(cx, 1))

    def first(soft, pieces):
        scratch = [pltpu.VMEM((t, d), BF), pltpu.SemaphoreType.DMA((blocks,))]
        more = [((t, 128), F32), ((t, d), F32), ((4, t, c), BF)]
        return call(
            partial(first_kernel, soft),
            [((t, d), BF), ((t, d), F32)] + (more if soft else []),
            (ids, *pieces, *packs, tokens, consts),
            prefetch=1, specs=[VM] * 8 + [ANY, VM],
            scratch=scratch if soft else scratch + [pltpu.VMEM((t, d), F32), pltpu.VMEM((4, t, c), BF)], us=4, limit=8, name="first" if soft else "hard_first",
        )

    def inner(soft, low):
        return call(
            partial(inner_kernel, soft), [((4, t, w), BF)] * (2 if soft else 1), (ids, low, *inners, *packs),
            prefetch=1, us=8, limit=8, name="inner" if soft else "hard_inner",
        )

    first_low, normed, inv1, attn, gated = first(True, pieces)
    first_2 = hop(first_low, 2)
    first_1 = hop(first_low, 1)
    inner_y = after(inner_y, first_low)
    inners = (inner_weight, inner_1, inner_x, inner_y, inner_3x, hop(inner_y, 1))
    hard_low, hard_normed = first(False, (after(c0, first_low), *pieces[1:]))
    outer_a = after(outer_a, hard_low)
    outer_3a = hop(outer_a, 1)
    hidden, udact = inner(True, after(first_low, hard_low))
    (hard_hidden,) = inner(False, after(hard_low, hidden))
    outer_b = after(outer_b, hard_hidden)
    outers = (outer_weight, outer_1, outer_a, outer_b, outer_3a, hop(outer_b, 1))

    student_rows, grad_two, gffn, v2 = call(
        second_kernel,
        [((t, d), BF), ((t, d), F32), ((t, d), BF), ((8, d), F32)],
        (ids, hidden, normed, *outers, teacher, present, consts),
        prefetch=1, specs=[VM] * 8 + [ANY] + [VM] * 2,
        scratch=[pltpu.VMEM((t, d), BF), pltpu.VMEM((t, d), F32), pltpu.VMEM((5, 8, d), F32), pltpu.SemaphoreType.DMA((blocks,))], us=6, limit=8, name="second",
    )
    gffn_1 = hop(gffn, 1)

    g0, g1, gfar, dkeep, dsend, grad_one = call(
        back_kernel,
        [((blocks, c, quarter), BF), ((blocks, c, quarter), BF), ((2, blocks, c, quarter), BF), ((2, c + 16, d), BF), ((2, c + 16, d), BF), ((t, d), F32)],
        (ids, gffn, udact, *inners, *outers, *packs, grad_two, normed, inv1, attn, gated, v2, present, consts),
        prefetch=1,
        scratch=[pltpu.VMEM((4, t, w), BF), pltpu.VMEM((t, d), F32), pltpu.VMEM((t, d), BF), pltpu.VMEM((4, 8, d), F32)], us=13, limit=12, name="back",
    )
    gx = hop(gfar, 2)
    g1r = hop(g1, 1)
    d_got = hop(dsend, 1)
    first_2 = after(first_2, g0)
    firsts = (first_low, first_1, first_2, hop(first_2, 1))
    hidden_own, udact_own = call(
        units_kernel, [((rows, w), BF), ((rows, w), BF)], (after(firsts[0], g0), *firsts[1:], consts, inner_weight), us=6, limit=8, name="units"
    )
    gx, d_got = after(gx, hidden_own), after(d_got, hidden_own)
    gpieces = (g0, g1r, gx, hop(gx, 1))
    d_mine, d_give = add(dkeep[0], d_got[0]), add(dkeep[1], d_got[1])
    d_recv = hop(d_give, 2)
    gffn_2 = hop(after(gffn, gx), 2)
    pick = lambda *s: pl.BlockSpec((1,) + s, lambda b, *_: (b,) + (0,) * len(s))
    keep, send, wacc, cacc = call(
        attend_back_kernel,
        [((2, t, d), BF), ((2, t, d), BF), ((3 * c, d), F32), ((16, d), F32)],
        (ids, *gpieces, e, *(in_hbm(a) for a in (inv_l, k, v, q, kt, tokens)), *(in_hbm(a.T) for a in (query_weight, key_weight, value_weight))),
        prefetch=1, grid=(blocks,),
        specs=[pick(c, quarter), pick(c, quarter), pl.BlockSpec((2, 1, c, quarter), lambda b, *_: (0, b, 0, 0)),
               pl.BlockSpec((2, 1, c, quarter), lambda b, *_: (0, b, 0, 0)), pick(heads, length, length), pick(8, length),
               pl.BlockSpec((length, c), lambda b, *_: (b, 0)), pl.BlockSpec((length, c), lambda b, *_: (b, 0)), pl.BlockSpec((length, c), lambda b, *_: (b, 0)), pick(c, length),
               pl.BlockSpec((length, d), lambda b, *_: (b, 0)), full(c, d), full(c, d), full(c, d)],
        out_specs=[full(2, t, d), full(2, t, d), full(3 * c, d), full(16, d)],
        scratch=[pltpu.VMEM((c, length), BF), pltpu.VMEM((length, 3 * c), BF), pltpu.VMEM((length, d), BF)],
        us=15, limit=20, name="attend_back",
    )
    gffn_2 = after(gffn_2, keep)
    n_c = 4 * ((3 * c + c + 32 + 63) // 64) * 16
    ckeep, csend = call(
        turn_kernel, [((2, n_c // 4, d), BF)] * 2, (ids, wacc, cacc, d_mine, after(d_recv, keep, gffn_2)), prefetch=1, specs=[VM] * 4,
        scratch=[pltpu.VMEM((n_c, d), F32)], us=1, limit=8, name="turn",
    )
    got = hop(after(send, ckeep), 1)
    c_got = hop(csend, 1, "dp")
    gffn_2 = after(gffn_2, ckeep)
    gffn_3 = hop(gffn_2, 1)
    part, near, sums = call(
        near_grad_kernel, [((w, d), F32), ((2 * t, w), BF), ((2, 8, w), F32)], (after(gffn, gffn_2), gffn_1, outer_weight, hidden_own, udact_own),
        us=5, limit=8, name="near_grad",
    )
    got = after(got, near)
    mine, give = add(keep[0], got[0]), add(keep[1], got[1])
    recv = hop(give, 2)
    akeep, asend = call(
        outer_grad_kernel, [((2, w // 4, d), BF)] * 2, (ids, after(gffn_2, give), gffn_3, hidden_own, part), prefetch=1, scratch=[pltpu.VMEM((w, d), F32)],
        us=2, limit=8, name="outer_grad",
    )
    a_got = hop(asend, 2, "dp")
    n_b = d + 64
    bkeep, bsend = call(
        inner_grad_kernel, [((2, n_b // 4, w), BF)] * 2,
        (ids, *firsts, after(gffn_2, akeep), gffn_3, outer_weight, hidden_own, udact_own, near, sums), prefetch=1,
        scratch=[pltpu.VMEM((2 * t, w), BF), pltpu.VMEM((n_b, w), F32), pltpu.VMEM((2, 8, w), F32)], us=4, limit=12, name="inner_grad",
    )
    b_got = hop(bsend, 1, "dp")

    def across(x):
        mask = 4
        while mask < n_dp:
            got = hop(x, mask, "dp")
            x = (x, got) if mask * 2 == n_dp else add(x, got)
            mask *= 2
        return x

    def split(keep, got):
        return add(keep[0], got[0]), add(keep[1], got[1])

    c_mine, c_give = split(ckeep, after(c_got, bkeep))
    c_got = hop(c_give, 2, "dp")
    pruned_rows, error = call(
        hard_kernel,
        [((t, d), BF), ((8, 128), F32)],
        (ids, after(hard_hidden, c_give), hard_normed, *outers, teacher, present, consts),
        prefetch=1, specs=[VM] * 8 + [ANY] + [VM] * 2,
        scratch=[pltpu.VMEM((t, d), BF), pltpu.VMEM((t, d), F32), pltpu.VMEM((8, d), F32), pltpu.SemaphoreType.DMA((blocks,))], us=0.1, limit=8, name="hard",
    )

    recv = after(recv, pruned_rows)
    grad_rows = (grad_one + (mine.astype(F32) + recv.astype(F32))).astype(BF)
    grad_2 = hop(grad_rows, 2)
    grad_1 = hop(grad_rows, 1)
    a_mine, a_give = split(akeep, after(a_got, grad_rows))
    a_got = hop(a_give, 1, "dp")
    b_mine, b_give = split(bkeep, after(b_got, a_give))
    b_got = hop(b_give, 2, "dp")
    pruned_rows = after(pruned_rows, b_give)
    pruned_2 = hop(pruned_rows, 2)
    pruned_1 = hop(pruned_rows, 1)
    c_mine = across(add(c_mine, after(c_got, b_give)))
    error = after(error, b_give)
    error = error + hop(error, 2)
    error_1 = hop(error, 1)
    a_mine = across(add(a_mine, after(a_got, c_mine[0])))
    (b_mine,) = call(
        third_kernel, [((n_b // 4 + 16, d), BF)], (ids, b_mine, after(b_got, a_mine[0]), error, error_1), prefetch=1, us=0.1, limit=4, name="third"
    )
    c_mine = add(c_mine[0], after(c_mine[1], b_mine))
    b_mine = across(b_mine)
    c_other = hop(c_mine, 2, "dp")
    grad_2 = after(grad_2, c_mine)
    grads = (grad_rows, grad_1, grad_2, hop(grad_2, 1))
    student_rows = after(student_rows, grad_2)
    student_2 = hop(student_rows, 2)
    student_1 = hop(student_rows, 1)
    a_mine = add(a_mine[0], after(a_mine[1], grad_2))
    a_other = hop(a_mine, 1, "dp")
    (c_pair,) = call(pair_kernel, [((2,) + c_mine.shape, BF)], (c_mine, after(c_other, a_mine)), us=0.1, limit=4, name="pair3")
    c_last = hop(c_pair, 1, "dp")
    b_mine = add(b_mine[0], after(b_mine[1], c_pair))
    b_other = hop(b_mine, 2, "dp")
    (a_pair,) = call(pair_kernel, [((2,) + a_mine.shape, BF)], (a_mine, after(a_other, b_mine)), us=0.1, limit=4, name="pair")
    a_last = hop(a_pair, 2, "dp")
    pruned_2, student_2 = after(pruned_2, a_pair), after(student_2, a_pair)
    pruneds = (pruned_rows, pruned_1, pruned_2, hop(pruned_2, 1))
    students = (student_rows, student_1, student_2, hop(student_2, 1))
    (b_pair,) = call(last_kernel, [((n_b // 2 + 16, d), BF)], (b_mine, after(b_other, student_2, pruned_2, c_last)), us=0.1, limit=4, name="last")
    b_last = hop(b_pair, 1, "dp")
    outs = call(
        spread_kernel,
        [((blocks, length, d), BF)] * 3,
        (ids, after(students[0], b_pair), *students[1:], *pruneds, *grads),
        prefetch=1, specs=[VM] * 12, out_specs=[ANY] * 3, scratch=[pltpu.SemaphoreType.DMA((12 * blocks,))], us=0.1, limit=4, name="spread",
    )
    student, pruned, tokens_grad = (o.reshape(rows, d) for o in outs)
    qw, kw, vw, ow, qb, vb, ob, fg, fs, ub, sg, ss, ha, da, me, live = call(
        final_kernel,
        [((c, d), F32), ((c, d), F32), ((c, d), F32), ((c, d), F32), ((c,), F32), ((c,), F32), ((d,), F32), ((d,), F32), ((d,), F32),
         ((d,), F32), ((d,), F32), ((d,), F32), ((heads,), F32), ((d,), F32), ((1,), F32), ((1,), F32)],
        (ids, consts, c_mine, c_other, after(c_last, outs[0])),
        prefetch=1, specs=[VM] * 4, out_specs=[VM] * 12 + [SM] + [VM] + [SM] * 2,
        scratch=[pltpu.VMEM((n_c, d), F32)], us=0.1, limit=8, name="final",
    )
    uw, iw, ib, ua, pe = call(
        weights_out_kernel,
        [((w, d), F32), ((d, w), F32), ((w,), F32), ((w,), F32), ((1,), F32)],
        (ids, consts, a_mine, a_other, after(a_last, qw), b_pair, b_last, live), prefetch=1,
        specs=[VM] * 6 + [SM], out_specs=[VM] * 4 + [SM], scratch=[pltpu.VMEM((n_b - d, w), F32)], us=0.1, limit=8, name="weights_out",
    )
    return (
        student, pruned, tokens_grad, qw.T, qb, kw.T, vw.T, vb, ow, ob, fg, fs, iw, ib, uw, ub, sg, ss, ha, ua, da, me.reshape(()), pe.reshape(()),
    )


def solution(mesh):
    row, col, lead, unit, none = P("dp", None), P(None, "head"), P("head", None), P("head"), P()
    return jax.shard_map(
        partial(shards, n_dp=mesh.shape["dp"]),
        mesh=mesh,
        in_specs=(row, row, row, row, col, unit, col, col, unit, lead, none, none, none, col, unit, lead, none, none, none) + (unit,) * 4 + (none,) * 2 + (unit,) * 2 + (none,),
        out_specs=(row, row, row, col, unit, col, col, unit, lead, none, none, none, col, unit, lead, none, none, none, unit, unit, none, none, none),
        check_vma=False,
    )
```
